32 devices in a mesh: lon: 2 (over x), lat: 4 (over z), lev: 4 (over y, core).
Axes of the slice: x: 2, y: 2, z: 4, core: 2. Of those that a mesh axis runs over, the one named last changes fastest.
Arguments:
- tokens_in: bfloat16 [4, 64, 32, 512], P('lev', 'lat', 'lon'), may hold values from -6 to 6
- cotangent: bfloat16 [4, 64, 32, 512], P('lev', 'lat', 'lon'), may hold values from -6 to 6
- qkv_weight: bfloat16 [512, 1536], replicated, may hold values from -5 to 5
- out_weight: bfloat16 [512, 512], replicated, may hold values from -0.25 to 0.25
- norm_gain: float32 [512], replicated, may hold values from 0.5 to 1.5
- ocean_mask: int32 [4, 64, 32], P('lev', 'lat', 'lon'), may hold values from 0 to 1, as said below
Outputs:
- layer_out: bfloat16 [4, 64, 32, 512], P('lev', 'lat', 'lon')
- input_grad: bfloat16 [4, 64, 32, 512], P('lev', 'lat', 'lon')
- qkv_grad: float32 [512, 1536], P('lev')
- out_grad: float32 [512, 512], P('lev')
- gain_grad: float32 [512], P('lev')
The draws below stay inside these ranges and needn't reach their ends.
Inputs may be any that keep to these rules, and one draw needn't show every extreme that they name: `ocean_mask`: at each level group, at most 3 of the windows of one device hold an ocean patch, and some device holds exactly 3 such windows.
All inputs are finite; a program needn't handle non-finite values.
Results may differ from the reference program's by a relative error of at most 0.017.
The reference program's roundings to bfloat16 on the way (of `hidden`, `projected`, `probabilities_low`, `mixed_out`, `grad_branch`, `grad_mixed`, `grad_scores` and `grad_qkv`) count: a program that leaves them out, or rounds other values in their place, can miss the bound.
Values may be sent and summed in bfloat16 or wider, within the bound.
No kernel may reach another device: no remote copies, remote signals or barrier semaphores. Data moves between devices by JAX's collectives and lax.ppermute only.
A program may use at most 128 MiB of HBM per device.

```python
import jax
import jax.numpy as jnp
from jax import lax

D = 512
HEADS = 8
WIN = 8
WLAT = 2
WLON = 2
LEVG = 4
NLAT_P = 64
NLON_P = 32
OCEAN_MAX = 3


def draw_qkv_weight(key, part):
    values_out = jnp.clip(jax.random.normal(key, (D, 3 * D), jnp.float32), -5.0, 5.0) * D ** (-0.5)
    return values_out.astype(jnp.bfloat16)


def draw_ocean_mask(key, part):
    lat_tiles = NLAT_P // (WLAT * WIN)
    lon_tiles = NLON_P // (WLON * WIN)
    tile_count = LEVG * lat_tiles * lon_tiles
    window_count = WLAT * WLON
    keys_all = jax.random.split(key, 5)
    order_bits = jax.random.randint(keys_all[0], (tile_count, window_count), 0, 2 ** 30)
    ranking = jnp.argsort(jnp.argsort(order_bits, axis=1, stable=True), axis=1, stable=True)
    counts = jax.random.randint(keys_all[1], (tile_count,), max(1, OCEAN_MAX // 2), OCEAN_MAX + 1)
    fullest = jax.random.randint(keys_all[2], (), 0, tile_count)
    counts = jnp.where(jnp.arange(tile_count) == fullest, OCEAN_MAX, counts)
    alive_flag = ranking < counts[:, None]
    patches = jax.random.randint(keys_all[3], (tile_count, window_count, WIN * WIN), 0, 5) < 3
    forced = jax.random.randint(keys_all[4], (tile_count, window_count), 0, WIN * WIN)
    patches = patches | (jnp.arange(WIN * WIN)[None, None, :] == forced[..., None])
    ocean = (patches & alive_flag[..., None]).astype(jnp.int32)
    ocean = ocean.reshape(LEVG, lat_tiles, lon_tiles, WLAT, WLON, WIN, WIN)
    ocean = jnp.transpose(ocean, (0, 1, 3, 5, 2, 4, 6))
    return ocean.reshape(LEVG, NLAT_P, NLON_P)


def shard_levels(own_key, dims, cuts, low, high):
    def one(axis_at, parts):
        steps = jax.random.uniform(jax.random.fold_in(jax.random.fold_in(own_key, 6), axis_at), (parts,), jnp.float32, low / len(cuts), high / len(cuts))
        return jnp.repeat(jnp.exp(steps), dims[axis_at] // parts).reshape((-1,) + (1,) * (len(dims) - axis_at - 1))

    loudness = one(*cuts[0])
    for cut in cuts[1:]:
        loudness = loudness * one(*cut)
    return loudness


def bell_draw(rng, extent, scale, most, cuts=(), kind=jnp.bfloat16):
    factor_of = shard_levels(rng, extent, cuts, -0.22, 0.18) if cuts else 1.0
    array = jax.random.normal(rng, extent, jnp.float32) * scale * factor_of
    return jnp.minimum(jnp.maximum(array, -most), most).astype(kind)


def setup_inputs(seed: int = 0) -> dict:
    keys = jax.random.split(jax.random.key(seed), 7)
    return {
        "tokens_in": bell_draw(keys[0], (LEVG, NLAT_P, NLON_P, D), 1.0, 6.0, ((0, 4), (1, 4), (2, 2))),
        "cotangent": bell_draw(keys[1], (LEVG, NLAT_P, NLON_P, D), 1.0, 6.0, ((0, 4), (1, 4), (2, 2))),
        "qkv_weight": draw_qkv_weight(jax.random.fold_in(keys[6], 71), 0),
        "out_weight": bell_draw(keys[3], (D, D), D ** -0.5, 0.25),
        "norm_gain": jnp.clip(1.0 + 0.1 * jax.random.normal(keys[4], (D,), jnp.float32), 0.5, 1.5),
        "ocean_mask": draw_ocean_mask(jax.random.fold_in(keys[6], 71), 0),
    }


def norm_rows(values_in):
    center = values_in - lax.optimization_barrier(jnp.mean(values_in, axis=-1, keepdims=True))
    spread = lax.optimization_barrier(jnp.mean(center * center, axis=-1, keepdims=True))
    scaling = lax.rsqrt(spread + 1e-05)
    return (center * scaling, scaling)

def to_windows(grid_in, lat_windows, lon_windows, window_side):
    channels = grid_in.shape[-1]
    blocks = grid_in.reshape(lat_windows, window_side, lon_windows, window_side, channels)
    return jnp.transpose(blocks, (0, 2, 1, 3, 4)).reshape(lat_windows * lon_windows, window_side * window_side, channels)

def from_windows(blocks, lat_windows, lon_windows, window_side):
    channels = blocks.shape[-1]
    grid_out = blocks.reshape(lat_windows, lon_windows, window_side, window_side, channels)
    return jnp.transpose(grid_out, (0, 2, 1, 3, 4)).reshape(lat_windows * window_side, lon_windows * window_side, channels)

def neighbours(padded, lat_windows, lon_windows, window_side):
    pieces = []
    for lat_step in range(3):
        for lon_step in range(3):
            section = padded[lat_step * window_side:(lat_step + lat_windows) * window_side, lon_step * window_side:(lon_step + lon_windows) * window_side]
            pieces.append(to_windows(section, lat_windows, lon_windows, window_side))
    return jnp.concatenate(pieces, axis=1)

def spread_back(gathered, lat_windows, lon_windows, window_side):
    channels = gathered.shape[-1]
    window_area = window_side * window_side
    totals = jnp.zeros(((lat_windows + 2) * window_side, (lon_windows + 2) * window_side, channels), jnp.float32)
    for lat_step in range(3):
        for lon_step in range(3):
            slot_index = lat_step * 3 + lon_step
            section = from_windows(gathered[:, slot_index * window_area:(slot_index + 1) * window_area], lat_windows, lon_windows, window_side)
            totals = totals.at[lat_step * window_side:(lat_step + lat_windows) * window_side, lon_step * window_side:(lon_step + lon_windows) * window_side].add(section)
    return totals

def split_heads(array_in, head_count):
    return array_in.reshape(array_in.shape[0], array_in.shape[1], head_count, array_in.shape[2] // head_count).astype(jnp.float32)

def attend_forward(queries, key_rows, value_rows, key_mask, alive_flag, head_count):
    features = queries.shape[-1]
    inv_root = (features // head_count) ** (-0.5)
    scores = jnp.einsum('wqhd,wkhd->whqk', split_heads(queries, head_count), split_heads(key_rows, head_count)) * inv_root
    scores = scores + (key_mask[:, None, None, :] - 1.0) * 1000000000.0
    row_top = lax.optimization_barrier(jnp.max(scores, axis=-1, keepdims=True))
    weights = jnp.exp(scores - row_top)
    probabilities = weights / lax.optimization_barrier(jnp.sum(weights, axis=-1, keepdims=True))
    probabilities_low = probabilities.astype(jnp.bfloat16)
    mixed_out = jnp.einsum('whqk,wkhd->wqhd', probabilities_low.astype(jnp.float32), split_heads(value_rows, head_count))
    mixed_out = mixed_out.reshape(queries.shape) * alive_flag[:, None, None]
    return (mixed_out.astype(jnp.bfloat16), probabilities)

def attend_backward(queries, key_rows, value_rows, probabilities, mixed_out, grad_mixed, head_count):
    features = queries.shape[-1]
    inv_root = (features // head_count) ** (-0.5)
    grad_heads = split_heads(grad_mixed, head_count)
    query_heads = split_heads(queries, head_count)
    grad_probs = jnp.einsum('wqhd,wkhd->whqk', grad_heads, split_heads(value_rows, head_count))
    delta_rows = jnp.einsum('wqhd,wqhd->whq', grad_heads, split_heads(mixed_out, head_count))
    grad_scores = (probabilities * (grad_probs - delta_rows[..., None]) * inv_root).astype(jnp.bfloat16).astype(jnp.float32)
    grad_query = jnp.einsum('whqk,wkhd->wqhd', grad_scores, split_heads(key_rows, head_count)).reshape(queries.shape)
    key_shape = (key_rows.shape[0], key_rows.shape[1], features)
    grad_key = jnp.einsum('whqk,wqhd->wkhd', grad_scores, query_heads).reshape(key_shape)
    grad_value = jnp.einsum('whqk,wqhd->wkhd', probabilities.astype(jnp.bfloat16).astype(jnp.float32), grad_heads).reshape(key_shape)
    return (grad_query, jnp.concatenate([grad_key, grad_value], axis=-1))

def pad_grid(grid_in):
    wrapped = jnp.concatenate([grid_in[:, NLON_P - WIN:], grid_in, grid_in[:, :WIN]], axis=1)
    border = jnp.zeros((WIN,) + wrapped.shape[1:], wrapped.dtype)
    return jnp.concatenate([border, wrapped, border], axis=0)

def level_pass(level_tokens, level_cotangent, level_mask, qkv_weight, out_weight, norm_gain):
    lat_windows = NLAT_P // WIN
    lon_windows = NLON_P // WIN
    flat_in = level_tokens.reshape(-1, D).astype(jnp.float32)
    normed, scaling = norm_rows(flat_in)
    hidden = (normed * norm_gain).astype(jnp.bfloat16)
    projected = jnp.dot(hidden, qkv_weight, preferred_element_type=jnp.float32).astype(jnp.bfloat16)
    queries = projected[:, :D].reshape(NLAT_P, NLON_P, D)
    key_vals = projected[:, D:].reshape(NLAT_P, NLON_P, 2 * D)
    ocean = level_mask.astype(jnp.float32)
    padded = pad_grid(key_vals)
    padded_mask = pad_grid(ocean[..., None])
    grad_branch = level_cotangent * ocean[..., None].astype(jnp.bfloat16)
    grad_flat = grad_branch.reshape(-1, D)
    grad_mixed = jnp.dot(grad_flat, out_weight.T, preferred_element_type=jnp.float32).astype(jnp.bfloat16).reshape(NLAT_P, NLON_P, D)

    def row_step(grad_pad, row_index):
        start = (row_index * WIN).astype(jnp.int32)
        slab = lax.dynamic_slice_in_dim(padded, start, 3 * WIN, 0)
        slab_mask = lax.dynamic_slice_in_dim(padded_mask, start, 3 * WIN, 0)
        near = neighbours(slab, 1, lon_windows, WIN)
        near_mask = neighbours(slab_mask, 1, lon_windows, WIN)[..., 0]
        query_rows = to_windows(lax.dynamic_slice_in_dim(queries, start, WIN, 0), 1, lon_windows, WIN)
        ocean_rows = to_windows(lax.dynamic_slice_in_dim(ocean[..., None], start, WIN, 0), 1, lon_windows, WIN)[..., 0]
        alive_flag = lax.optimization_barrier(jnp.max(ocean_rows, axis=1))
        grad_rows = to_windows(lax.dynamic_slice_in_dim(grad_mixed, start, WIN, 0), 1, lon_windows, WIN)
        mixed_out, probabilities = attend_forward(query_rows, near[..., :D], near[..., D:], near_mask, alive_flag, HEADS)
        grad_query, grad_near = attend_backward(query_rows, near[..., :D], near[..., D:], probabilities, mixed_out, grad_rows, HEADS)
        spread = spread_back(grad_near, 1, lon_windows, WIN)
        current = lax.dynamic_slice_in_dim(grad_pad, start, 3 * WIN, 0)
        grad_pad = lax.dynamic_update_slice_in_dim(grad_pad, current + spread, start, 0)
        return (grad_pad, (from_windows(mixed_out, 1, lon_windows, WIN), from_windows(grad_query, 1, lon_windows, WIN)))
    start_pad = jnp.zeros((NLAT_P + 2 * WIN, NLON_P + 2 * WIN, 2 * D), jnp.float32)
    grad_pad, (mixed_rows, query_rows) = lax.scan(row_step, start_pad, jnp.arange(lat_windows, dtype=jnp.int32))
    mixed_flat = mixed_rows.reshape(-1, D)
    grad_query = query_rows.reshape(-1, D)
    inner_rows = grad_pad[WIN:WIN + NLAT_P]
    grad_kv = inner_rows[:, WIN:WIN + NLON_P]
    grad_kv = grad_kv.at[:, :WIN].add(inner_rows[:, WIN + NLON_P:])
    grad_kv = grad_kv.at[:, NLON_P - WIN:].add(inner_rows[:, :WIN])
    branch = jnp.dot(mixed_flat, out_weight, preferred_element_type=jnp.float32)
    layer_out = (flat_in + ocean.reshape(-1, 1) * branch).astype(jnp.bfloat16)
    out_grad = jnp.dot(mixed_flat.T, grad_flat, preferred_element_type=jnp.float32)
    grad_qkv = jnp.concatenate([grad_query.astype(jnp.bfloat16), grad_kv.reshape(-1, 2 * D).astype(jnp.bfloat16)], axis=1)
    grad_hidden = jnp.dot(grad_qkv, qkv_weight.T, preferred_element_type=jnp.float32)
    qkv_grad = jnp.dot(hidden.T, grad_qkv, preferred_element_type=jnp.float32)
    gain_grad = lax.optimization_barrier(jnp.sum(grad_hidden * normed, axis=0))
    scaled = grad_hidden * norm_gain
    correction = scaled - lax.optimization_barrier(jnp.mean(scaled, axis=-1, keepdims=True)) - normed * lax.optimization_barrier(jnp.mean(scaled * normed, axis=-1, keepdims=True))
    input_grad = (level_cotangent.reshape(-1, D).astype(jnp.float32) + scaling * correction).astype(jnp.bfloat16)
    return (layer_out.reshape(NLAT_P, NLON_P, D), input_grad.reshape(NLAT_P, NLON_P, D), qkv_grad, out_grad, gain_grad)

def reference(tokens_in, cotangent, qkv_weight, out_weight, norm_gain, ocean_mask):

    def one_level(inputs):
        return level_pass(inputs[0], inputs[1], inputs[2], qkv_weight, out_weight, norm_gain)
    layer_out, input_grad, qkv_grads, out_grads, gain_grads = lax.map(one_level, (tokens_in, cotangent, ocean_mask))
    return (layer_out, input_grad, lax.optimization_barrier(jnp.sum(qkv_grads, axis=0)), lax.optimization_barrier(jnp.sum(out_grads, axis=0)), lax.optimization_barrier(jnp.sum(gain_grads, axis=0)))
```

```python
import functools

import jax
import jax.numpy as jnp
from jax import lax
from jax.experimental import pallas as pl
from jax.experimental.pallas import tpu as pltpu
from jax.sharding import PartitionSpec as P

HEADS = 8
WIN = 8
AREA = WIN * WIN
D = 512
HEAD_DIM = D // HEADS
GROUP = 256
GROUP_HEADS = GROUP // HEAD_DIM
GROUPS = D // GROUP
KEYS = 8 * AREA
LAND = 1000.0
NEVER = -1e9
FAR = 1e30
F32 = jnp.float32
BF16 = jnp.bfloat16
EXACT = lax.Precision.HIGHEST


def dot(a, b, ca, cb, precision=None):
    return lax.dot_general(
        a, b, (((ca,), (cb,)), ((), ())), preferred_element_type=F32, precision=precision
    )


def iota(shape, dim):
    return lax.broadcasted_iota(jnp.int32, shape, dim)


def window_of(grid, w):
    r, c = divmod(w, 2)
    part = grid[r * WIN : (r + 1) * WIN, c * WIN : (c + 1) * WIN, :]
    return part.reshape(AREA, grid.shape[-1])


def grid_of(windows):
    rows = []
    for r in range(2):
        parts = [windows[2 * r + c].reshape(WIN, WIN, -1) for c in range(2)]
        rows.append(jnp.concatenate(parts, axis=1))
    return jnp.concatenate(rows, axis=0)


def token_mask(mask):
    t = iota((4 * AREA, 2 * WIN), 0)
    lane = iota((4 * AREA, 2 * WIN), 1)
    w, i, j = t // AREA, (t % AREA) // WIN, t % WIN
    pick_row = (lane == WIN * (w // 2) + i).astype(F32)
    pick_col = (lane == WIN * (w % 2) + j).astype(F32)
    rows = dot(pick_row, mask, 1, 0)
    return jnp.sum(rows * pick_col, axis=1, keepdims=True)


def norm_rows(x):
    center = x - jnp.mean(x, axis=-1, keepdims=True)
    spread = jnp.mean(center * center, axis=-1, keepdims=True)
    scaling = lax.rsqrt(spread + 1e-05)
    return center * scaling, scaling


def head_blocks():
    row = iota((GROUP, GROUP), 0) // HEAD_DIM
    col = iota((GROUP, GROUP), 1) // HEAD_DIM
    return (row == col).astype(F32)


def stack_heads(part, blocks):
    return jnp.concatenate([part] * GROUP_HEADS, axis=0) * blocks.astype(part.dtype)


def unstack_heads(full, blocks):
    kept = full * blocks
    return sum(kept[h * AREA : (h + 1) * AREA] for h in range(GROUP_HEADS))


def lanes(g):
    return slice(g * GROUP, (g + 1) * GROUP)


def prep_kernel(x_ref, mask_ref, all_ref, top_ref, bottom_ref):
    ocean = token_mask(mask_ref[0].astype(F32))
    x = x_ref[0].astype(F32)
    for w in range(4):
        part = jnp.where(ocean[w * AREA : (w + 1) * AREA] > 0.5, window_of(x, w), LAND)
        part = part.astype(BF16)
        all_ref[w] = part
        (top_ref if w < 2 else bottom_ref)[w % 2] = part


def own_kernel(
    tok_ref, cot_ref, mask_ref, wqkv_ref, wout_ref, gain_ref,
    q_ref, kv_ref, gm_ref, gm_top_ref, gm_bottom_ref, gb_ref, hid_ref, bias_ref, info_ref,
):
    mask = mask_ref[0].astype(F32)
    ocean = token_mask(mask)
    tokens = tok_ref[...].reshape(4 * AREA, D).astype(F32)
    normed, _ = norm_rows(tokens)
    hidden = (normed * gain_ref[...]).astype(BF16)
    hid_ref[...] = hidden
    projected = dot(hidden, wqkv_ref[...], 1, 0).astype(BF16)
    q_ref[...] = (projected[:, :D] * BF16(HEAD_DIM ** -0.5)).reshape(4, AREA, D)
    kv_ref[...] = projected[:, D:].reshape(4, AREA, 2 * D)
    bias_ref[...] = jnp.where(tokens[:, :128] > 0.5 * LAND, NEVER, 0.0).reshape(4, AREA, 128)
    cot = cot_ref[0].astype(F32)
    for w in range(4):
        branch = window_of(cot, w) * ocean[w * AREA : (w + 1) * AREA]
        gb_ref[w * AREA : (w + 1) * AREA, :] = branch.astype(BF16)
    gm = dot(gb_ref[...], wout_ref[...], 1, 1).astype(BF16).reshape(4, AREA, D)
    gm_ref[...] = gm
    gm_top_ref[...] = gm[:2]
    gm_bottom_ref[...] = gm[2:]
    alive = []
    for w in range(4):
        alive.append((jnp.max(ocean[w * AREA : (w + 1) * AREA]) > 0.5).astype(jnp.int32))
        info_ref[1 + w] = alive[w]
    left_out = jnp.where(
        alive[3] == 0, 3, jnp.where(alive[2] == 0, 2, jnp.where(alive[1] == 0, 1, 0))
    )
    info_ref[0] = left_out


def slot_window(info_ref, slot):
    left_out = info_ref[0]
    return slot + (slot >= left_out).astype(jnp.int32)


def fill_slots(info_ref, own_ref, cat_ref):
    for slot in range(3):
        cat_ref[slot * AREA : (slot + 1) * AREA] = own_ref[slot_window(info_ref, slot)]


def fill_near(w, halo_ref, cat_ref):
    r, c = w // 2, w % 2
    base = 3 * AREA
    lon_at, lat_at, corner_at = 2 * (1 - c), 4 + 2 * r, 8 + 2 * r + 1 - c
    for k, at in enumerate((lon_at, lon_at + 1, lat_at, lat_at + 1, corner_at)):
        cat_ref[base + k * AREA : base + (k + 1) * AREA] = halo_ref[at]


def forward_kernel(
    info_ref, place_ref, q_ref, kv_ref, bias_ref, lon_ref, up_ref, down_ref, upc_ref, downc_ref,
    wqkv_ref, gain_ref,
    mixed_ref, stats_ref, srow_ref, qh_ref, kvh_ref, biash_ref,
    gm_ref, kcat, bcat,
):
    up_ok, down_ok = place_ref[0] > 0, place_ref[0] < place_ref[1] - 1
    groups = (
        ((lon_ref, 0, None), (lon_ref, 2, None), (lon_ref, 1, None), (lon_ref, 3, None)),
        ((up_ref, 0, up_ok), (up_ref, 1, up_ok), (down_ref, 0, down_ok), (down_ref, 1, down_ok)),
        ((upc_ref, 0, up_ok), (upc_ref, 1, up_ok), (downc_ref, 0, down_ok), (downc_ref, 1, down_ok)),
    )
    for n, group in enumerate(groups):
        tokens = jnp.concatenate([ref[at] for ref, at, _ in group], axis=0).astype(F32)
        normed, _ = norm_rows(tokens)
        hidden = (normed * gain_ref[...]).astype(BF16)
        projected = dot(hidden, wqkv_ref[...], 1, 0).astype(BF16)
        span = slice(4 * n, 4 * n + 4)
        qh_ref[span] = (projected[:, :D] * BF16(HEAD_DIM ** -0.5)).reshape(4, AREA, D)
        kvh_ref[span] = projected[:, D:].reshape(4, AREA, 2 * D)
        for k, (_, _, ok) in enumerate(group):
            out = tokens[k * AREA : (k + 1) * AREA, :128] > 0.5 * LAND
            bias = jnp.where(out, NEVER, 0.0)
            if ok is not None:
                bias = jnp.where(ok, bias, NEVER)
            biash_ref[4 * n + k] = bias
    mixed_ref[...] = jnp.zeros_like(mixed_ref)
    stats_ref[:, :HEADS, :] = jnp.full((4, HEADS, AREA), FAR, F32)
    stats_ref[:, HEADS:, :] = jnp.zeros((4, HEADS, AREA), F32)
    srow_ref[...] = jnp.zeros_like(srow_ref)
    blocks = head_blocks()
    head_row = (iota((8, GROUP), 0) == iota((8, GROUP), 1) // HEAD_DIM).astype(F32)
    spot = (iota((GROUP, AREA), 0) % AREA == iota((GROUP, AREA), 1)).astype(F32)
    ones = jnp.ones((8, GROUP), F32)
    fill_slots(info_ref, kv_ref, kcat)
    fill_slots(info_ref, bias_ref, bcat)

    def slot_step(slot, carry):
        w = slot_window(info_ref, slot)

        @pl.when(info_ref[1 + w] > 0)
        def _():
            fill_near(w, kvh_ref, kcat)
            fill_near(w, biash_ref, bcat)
            bias = bcat[...]
            bias = jnp.concatenate([bias, bias], axis=1)
            for g in range(GROUPS):
                q_stack = stack_heads(q_ref[w, :, lanes(g)], blocks)
                scores = dot(kcat[:, lanes(g)], q_stack, 1, 1) + bias
                top = jnp.max(scores, axis=0, keepdims=True)
                weights = jnp.exp(scores - top)
                total = jnp.sum(weights, axis=0, keepdims=True)
                low = (weights * (1.0 / total)).astype(BF16)
                values = kcat[:, D + g * GROUP : D + (g + 1) * GROUP]
                out = unstack_heads(dot(low, values, 0, 0), blocks).astype(BF16)
                mixed_ref[w, :, lanes(g)] = out
                log_sum = top + jnp.log(total)
                product = out.astype(F32) * gm_ref[w, :, lanes(g)].astype(F32)
                product = jnp.concatenate([product] * GROUP_HEADS, axis=0) * blocks
                delta = dot(ones, product, 1, 1, EXACT)[:1]
                srow_ref[w, g : g + 1] = log_sum
                srow_ref[w, 2 + g : 3 + g] = delta
                low_rows = dot(head_row * log_sum, spot, 1, 0, EXACT)
                delta_rows = dot(head_row * delta, spot, 1, 0, EXACT)
                at = g * GROUP_HEADS
                stats_ref[w, at : at + GROUP_HEADS] = low_rows[:GROUP_HEADS]
                stats_ref[w, HEADS + at : HEADS + at + GROUP_HEADS] = delta_rows[:GROUP_HEADS]

        return carry

    lax.fori_loop(0, 3, slot_step, 0)


def query_kernel(
    info_ref, place_ref, q_ref, kv_ref, bias_ref, kvh_ref, biash_ref, gm_ref, mixed_ref, srow_ref,
    hid_ref, gb_ref, x_ref, mask_ref, wout_ref,
    gq_ref, out_ref, keep_ref, send_ref,
    kcat, bcat,
):
    blocks = head_blocks()
    gq_ref[...] = jnp.zeros_like(gq_ref)
    fill_slots(info_ref, kv_ref, kcat)
    fill_slots(info_ref, bias_ref, bcat)

    def slot_step(slot, carry):
        w = slot_window(info_ref, slot)

        @pl.when(info_ref[1 + w] > 0)
        def _():
            fill_near(w, kvh_ref, kcat)
            fill_near(w, biash_ref, bcat)
            bias = bcat[...]
            bias = jnp.concatenate([bias, bias], axis=1)
            for g in range(GROUPS):
                q_stack = stack_heads(q_ref[w, :, lanes(g)], blocks)
                gm_stack = stack_heads(gm_ref[w, :, lanes(g)], blocks)
                keys = kcat[:, lanes(g)]
                values = kcat[:, D + g * GROUP : D + (g + 1) * GROUP]
                scores = dot(keys, q_stack, 1, 1) + bias
                probs = jnp.exp(scores - srow_ref[w, g : g + 1])
                grad_probs = dot(values, gm_stack, 1, 1)
                grad_scores = (probs * (grad_probs - srow_ref[w, 2 + g : 3 + g])).astype(BF16)
                grad = unstack_heads(dot(grad_scores, keys, 0, 0), blocks)
                gq_ref[w, :, lanes(g)] = (grad * HEAD_DIM ** -0.5).astype(BF16)

        return carry

    lax.fori_loop(0, 3, slot_step, 0)
    mixed = mixed_ref[...].reshape(4 * AREA, D)
    branch = dot(mixed, wout_ref[...], 1, 0)
    ocean = token_mask(mask_ref[0].astype(F32))
    added = (branch * ocean).reshape(4, AREA, D)
    out_ref[0] = (x_ref[0].astype(F32) + grid_of([added[w] for w in range(4)])).astype(BF16)
    gq = gq_ref[...].reshape(4 * AREA, D)
    gb = gb_ref[...]
    lev = place_ref[2]
    for rel in range(4):
        at = pl.ds(pl.multiple_of((lev ^ rel) * 128, 128), 128)
        to = keep_ref if rel % 2 == 0 else send_ref
        to[rel // 2, :, :D] = dot(hid_ref[:, at], gq, 0, 0).astype(BF16)
        mixed_cols = mixed_ref[:, :, at].reshape(4 * AREA, 128)
        to[rel // 2, :, D:] = dot(mixed_cols, gb, 0, 0).astype(BF16)


def key_kernel(
    info_ref, place_ref, q_ref, kv_ref, gm_ref, stats_ref, qh_ref,
    gm_lon_ref, gm_up_ref, gm_down_ref, gm_upc_ref, gm_downc_ref,
    st_lon_ref, st_up_ref, st_down_ref, st_upc_ref, st_downc_ref,
    hid_ref, gq_ref, tok_ref, cot_ref, wqkv_ref, gain_ref,
    ing_ref, keep_ref, send_ref,
    qcat, gmcat, gmh, scat, gkv,
):
    blocks = head_blocks()
    gkv[...] = jnp.zeros_like(gkv)
    halo = (
        (gm_lon_ref, 0), (gm_lon_ref, 2), (gm_lon_ref, 1), (gm_lon_ref, 3),
        (gm_up_ref, 0), (gm_up_ref, 1), (gm_down_ref, 0), (gm_down_ref, 1),
        (gm_upc_ref, 0), (gm_upc_ref, 1), (gm_downc_ref, 0), (gm_downc_ref, 1),
    )
    for k, (ref, at) in enumerate(halo):
        gmh[k] = ref[at]
    stats = (
        (st_lon_ref, 0), (st_lon_ref, 2), (st_lon_ref, 1), (st_lon_ref, 3),
        (st_up_ref, 0), (st_up_ref, 1), (st_down_ref, 0), (st_down_ref, 1),
        (st_upc_ref, 0), (st_upc_ref, 1), (st_downc_ref, 0), (st_downc_ref, 1),
    )
    spread = [
        (iota((HEADS, GROUP), 0) == g * GROUP_HEADS + iota((HEADS, GROUP), 1) // HEAD_DIM).astype(F32)
        for g in range(GROUPS)
    ]
    for k, (ref, at) in enumerate(stats):
        scat[3 + k] = ref[at]
    for slot in range(3):
        scat[slot] = stats_ref[slot_window(info_ref, slot)]
    fill_slots(info_ref, q_ref, qcat)
    fill_slots(info_ref, gm_ref, gmcat)

    def slot_step(slot, carry):
        w = slot_window(info_ref, slot)

        @pl.when(info_ref[1 + w] > 0)
        def _():
            fill_near(w, qh_ref, qcat)
            fill_near(w, gmh, gmcat)
            r, c = w // 2, w % 2
            lon_at, lat_at, corner_at = 3 + 2 * (1 - c), 7 + 2 * r, 11 + 2 * r + 1 - c
            picked = [scat[k] for k in (0, 1, 2, lon_at, lon_at + 1, lat_at, lat_at + 1, corner_at)]
            for g in range(GROUPS):
                k_stack = stack_heads(kv_ref[w, :, lanes(g)], blocks)
                v_stack = stack_heads(kv_ref[w, :, D + g * GROUP : D + (g + 1) * GROUP], blocks)
                queries = qcat[:, lanes(g)]
                grads = gmcat[:, lanes(g)]
                scores = dot(queries, k_stack, 1, 1)
                log_sum = jnp.concatenate([dot(p[:HEADS], spread[g], 0, 0, EXACT) for p in picked], axis=0)
                probs = jnp.exp(jnp.minimum(scores - log_sum, 0.0))
                grad_probs = dot(grads, v_stack, 1, 1)
                delta = jnp.concatenate([dot(p[HEADS:], spread[g], 0, 0, EXACT) for p in picked], axis=0)
                grad_scores = (probs * (grad_probs - delta)).astype(BF16)
                gkv[w, :, lanes(g)] = unstack_heads(dot(grad_scores, queries, 0, 0), blocks)
                gkv[w, :, D + g * GROUP : D + (g + 1) * GROUP] = unstack_heads(
                    dot(probs.astype(BF16), grads, 0, 0), blocks
                )

        return carry

    lax.fori_loop(0, 3, slot_step, 0)
    tokens = tok_ref[...].reshape(4 * AREA, D).astype(F32)
    land = tokens[:, :1] > 0.5 * LAND
    grad_kv = jnp.where(land, 0.0, gkv[...].reshape(4 * AREA, 2 * D)).astype(BF16)
    lev = place_ref[2]
    for rel in range(4):
        at = pl.ds(pl.multiple_of((lev ^ rel) * 128, 128), 128)
        to = keep_ref if rel % 2 == 0 else send_ref
        to[rel // 2] = dot(hid_ref[:, at], grad_kv, 0, 0).astype(BF16)
    gq = gq_ref[...].reshape(4 * AREA, D)
    grad_hidden = dot(gq, wqkv_ref[:, :D], 1, 1) + dot(grad_kv, wqkv_ref[:, D:], 1, 1)
    normed, scaling = norm_rows(tokens)
    scaled = grad_hidden * gain_ref[...]
    correction = (
        scaled
        - jnp.mean(scaled, axis=-1, keepdims=True)
        - normed * jnp.mean(scaled * normed, axis=-1, keepdims=True)
    )
    added = (scaling * correction).reshape(4, AREA, D)
    ing_ref[0] = (cot_ref[0].astype(F32) + grid_of([added[w] for w in range(4)])).astype(BF16)


def finish_kernel(whole_rows, place_ref, own_ref, *refs):
    others, (wqkv_ref, gain_ref, qkv_ref, out_ref, gg_ref) = refs[:-5], refs[-5:]
    lat, lat_count, lev = place_ref[0], place_ref[1], place_ref[2]
    for k, ref in enumerate((own_ref,) + tuple(others)):
        z = lax.rem(lat - k + lat_count, lat_count)
        value = ref[...].astype(F32)
        for x in range(value.shape[0]):
            qkv_ref[x, z, :, :D] = value[x, :, :D]
            qkv_ref[x, z, :, D:] = value[x, :, 2 * D :]
            out_ref[x, z] = value[x, :, D : 2 * D]
    if whole_rows:
        at = pl.ds(pl.multiple_of(lev * 128, 128), 128)
        product = wqkv_ref[at, :].astype(F32) * qkv_ref[...].reshape(128, 3 * D)
        sums = dot(jnp.ones((8, 3 * D), F32), product, 1, 1, EXACT)[:1]
        gg_ref[...] = sums / gain_ref[:, at]
    else:
        gg_ref[...] = jnp.zeros_like(gg_ref)


VMEM = pl.BlockSpec(memory_space=pltpu.VMEM)
SMEM = pl.BlockSpec(memory_space=pltpu.SMEM)


def call(kernel, outs, scalars, arrays, scratch=(), flops=0, name=None, smem_out=False):
    moved = sum(a.size * a.dtype.itemsize for a in arrays)
    moved += sum(o.size * o.dtype.itemsize for o in outs)
    out_specs = [VMEM] * len(outs)
    if smem_out:
        out_specs[-1] = SMEM
    return pl.pallas_call(
        kernel,
        out_shape=outs,
        in_specs=[SMEM] * len(scalars) + [VMEM] * len(arrays),
        out_specs=out_specs,
        scratch_shapes=list(scratch),
        compiler_params=pltpu.CompilerParams(vmem_limit_bytes=40 * 1024 * 1024),
        cost_estimate=pl.CostEstimate(flops=flops, bytes_accessed=moved, transcendentals=0),
        name=name,
    )(*scalars, *arrays)


def shape(dims, dtype=BF16):
    return jax.ShapeDtypeStruct(dims, dtype)


def ring(count, step, periodic):
    return [
        (i, (i + step) % count) for i in range(count) if periodic or 0 <= i + step < count
    ]


def lon_halo(own):
    count = lax.axis_size("lon")
    if count == 2:
        return lax.ppermute(own, "lon", [(0, 1), (1, 0)])
    left = lax.ppermute(own[1::2], "lon", ring(count, 1, True))
    right = lax.ppermute(own[0::2], "lon", ring(count, -1, True))
    return jnp.stack([right, left], axis=1).reshape(own.shape)


def lat_halo(top, bottom):
    count = lax.axis_size("lat")
    up = lax.ppermute(bottom, "lat", ring(count, 1, False))
    down = lax.ppermute(top, "lat", ring(count, -1, False))
    return up, down


def lev_sum(keep, send):
    arrived = lax.ppermute(send, "lev", [(i, i ^ 1) for i in range(4)]).astype(F32)
    onward = (keep[1].astype(F32) + arrived[1]).astype(BF16)
    last = lax.ppermute(onward, "lev", [(i, i ^ 2) for i in range(4)])
    return keep[0].astype(F32) + arrived[0] + last.astype(F32)


def plane_parts(total):
    lon, lon_count = lax.axis_index("lon"), lax.axis_size("lon")
    lat, lat_count = lax.axis_index("lat"), lax.axis_size("lat")
    width = total.shape[1]
    parts = total.reshape(lon_count, -1, width)
    own = lax.dynamic_index_in_dim(parts, lon, 0, False)
    low = parts.astype(BF16)
    for k in range(1, lon_count):
        piece = lax.dynamic_index_in_dim(low, (lon + k) % lon_count, 0, False)
        own = own + lax.ppermute(piece, "lon", ring(lon_count, k, True)).astype(F32)
    parts = own.reshape(lat_count, -1, width)
    own = lax.dynamic_index_in_dim(parts, lat, 0, False)
    low = parts.astype(BF16)
    for k in range(1, lat_count):
        piece = lax.dynamic_index_in_dim(low, (lat + k) % lat_count, 0, False)
        own = own + lax.ppermute(piece, "lat", ring(lat_count, k, True)).astype(F32)
    own = own.astype(BF16)
    across = [own] + [
        lax.ppermute(own, "lon", ring(lon_count, k, True)) for k in range(1, lon_count)
    ]
    if lon_count == 2:
        first = lon == 0
        across = [jnp.where(first, across[0], across[1]), jnp.where(first, across[1], across[0])]
        both = jnp.stack(across)
    else:
        both = jnp.roll(jnp.stack(across[:1] + across[:0:-1]), lon, axis=0)
    return [both] + [lax.ppermute(both, "lat", ring(lat_count, k, True)) for k in range(1, lat_count)]


def on_device(tokens_in, cotangent, qkv_weight, out_weight, norm_gain, ocean_mask):
    lat_count, lon_count = lax.axis_size("lat"), lax.axis_size("lon")
    gain = norm_gain.reshape(1, D)
    place = jnp.stack(
        [lax.axis_index("lat"), jnp.int32(lat_count), lax.axis_index("lev")]
    ).astype(jnp.int32)
    half = shape((2, AREA, D))
    four = shape((4, AREA, D))
    flat = shape((4 * AREA, D))
    tok, tok_top, tok_bottom = call(
        prep_kernel, [four, half, half], [], [tokens_in, ocean_mask], name="prep"
    )
    tok_lon = lon_halo(tok)
    tok_up, tok_down = lat_halo(tok_top, tok_bottom)
    q, kv, gm, gm_top, gm_bottom, gb, hid, bias, info = call(
        own_kernel,
        [four, shape((4, AREA, 2 * D)), four, half, half, flat, flat,
         shape((4, AREA, 128), F32), shape((8,), jnp.int32)],
        [],
        [tok, cotangent, ocean_mask, qkv_weight, out_weight, gain],
        flops=2 * 256 * 512 * 2048,
        name="own",
        smem_out=True,
    )
    tok_upc, tok_downc = lat_halo(tok_lon[:2], tok_lon[2:])
    gm_lon = lon_halo(gm)
    gm_up, gm_down = lat_halo(gm_top, gm_bottom)
    cat_scratch = [pltpu.VMEM((KEYS, 2 * D), BF16), pltpu.VMEM((KEYS, 128), F32)]
    mixed, stats, srow, qh, kvh, biash = call(
        lambda *refs: forward_kernel(*refs[:10], *refs[11:13], *refs[13:19], refs[10], *refs[19:]),
        [four, shape((4, 2 * HEADS, AREA), F32), shape((4, 8, GROUP), F32), shape((12, AREA, D)),
         shape((12, AREA, 2 * D)), shape((12, AREA, 128), F32)],
        [info, place],
        [q, kv, bias, tok_lon, tok_up, tok_down, tok_upc, tok_downc, gm, qkv_weight, gain],
        cat_scratch,
        flops=2 * 768 * 512 * 1536 + 3 * 4 * 2 * 512 * 256 * 256,
        name="forward",
    )
    gm_upc, gm_downc = lat_halo(gm_lon[:2], gm_lon[2:])
    st_lon = lon_halo(stats)
    st_up, st_down = lat_halo(stats[:2], stats[2:])
    st_upc, st_downc = lat_halo(st_lon[:2], st_lon[2:])
    share = shape((2, 128, 2 * D))
    gq, layer_out, keep_a, send_a = call(
        query_kernel,
        [four, shape(tokens_in.shape), share, share],
        [info, place],
        [q, kv, bias, kvh, biash, gm, mixed, srow, hid, gb, tokens_in, ocean_mask, out_weight],
        cat_scratch,
        flops=3 * 6 * 2 * 512 * 256 * 256 + 3 * 2 * 256 * 512 * 512,
        name="query",
    )
    total_a = lev_sum(keep_a, send_a)
    input_grad, keep_b, send_b = call(
        key_kernel,
        [shape(tokens_in.shape), share, share],
        [info, place],
        [q, kv, gm, stats, qh, gm_lon, gm_up, gm_down, gm_upc, gm_downc,
         st_lon, st_up, st_down, st_upc, st_downc, hid, gq, tok, cotangent, qkv_weight, gain],
        [pltpu.VMEM((KEYS, D), BF16), pltpu.VMEM((KEYS, D), BF16), pltpu.VMEM((12, AREA, D), BF16),
         pltpu.VMEM((15, 2 * HEADS, AREA), F32), pltpu.VMEM((4, AREA, 2 * D), F32)],
        flops=3 * 8 * 2 * 512 * 256 * 256 + 2 * 2 * 256 * 512 * 1536,
        name="key",
    )
    total_b = lev_sum(keep_b, send_b)
    parts = plane_parts(jnp.concatenate([total_a, total_b], axis=1))
    rows = parts[0].shape[1]
    whole_rows = rows % 8 == 0
    qkv_grad, out_grad, gain_grad = call(
        functools.partial(finish_kernel, whole_rows),
        [shape((lon_count, lat_count, rows, 3 * D), F32), shape((lon_count, lat_count, rows, D), F32),
         shape((1, 128), F32)],
        [place],
        parts + [qkv_weight, gain],
        name="finish",
    )
    qkv_grad = qkv_grad.reshape(128, 3 * D)
    out_grad = out_grad.reshape(128, D)
    if whole_rows:
        gain_grad = gain_grad.reshape(128)
    else:
        at = lax.axis_index("lev") * 128
        rows_in = lax.dynamic_slice_in_dim(qkv_weight, at, 128, 0).astype(F32)
        gain_grad = jnp.sum(rows_in * qkv_grad, axis=1)
        gain_grad = gain_grad / lax.dynamic_slice_in_dim(norm_gain, at, 128, 0)
    return layer_out, input_grad, qkv_grad, out_grad, gain_grad


def solution(mesh):
    placed = (
        P("lev", "lat", "lon", None),
        P("lev", "lat", "lon", None),
        P(),
        P(),
        P(),
        P("lev", "lat", "lon"),
    )
    return jax.shard_map(
        on_device,
        mesh=mesh,
        in_specs=placed,
        out_specs=(
            P("lev", "lat", "lon", None),
            P("lev", "lat", "lon", None),
            P("lev", None),
            P("lev", None),
            P("lev"),
        ),
        check_vma=False,
    )
```

```python
import functools

import jax
import jax.numpy as jnp
from jax import lax
from jax.experimental import pallas as pl
from jax.experimental.pallas import tpu as pltpu
from jax.sharding import PartitionSpec as P

HEADS = 8
WIN = 8
AREA = WIN * WIN
D = 512
HEAD_DIM = D // HEADS
GROUP = 256
GROUP_HEADS = GROUP // HEAD_DIM
GROUPS = D // GROUP
KEYS = 8 * AREA
LAND = 1000.0
NEVER = -1e9
FAR = 1e30
F32 = jnp.float32
BF16 = jnp.bfloat16
EXACT = lax.Precision.HIGHEST


def dot(a, b, ca, cb, precision=None):
    return lax.dot_general(
        a, b, (((ca,), (cb,)), ((), ())), preferred_element_type=F32, precision=precision
    )


def iota(shape, dim):
    return lax.broadcasted_iota(jnp.int32, shape, dim)


def window_of(grid, w):
    r, c = divmod(w, 2)
    part = grid[r * WIN : (r + 1) * WIN, c * WIN : (c + 1) * WIN, :]
    return part.reshape(AREA, grid.shape[-1])


def grid_of(windows):
    rows = []
    for r in range(2):
        parts = [windows[2 * r + c].reshape(WIN, WIN, -1) for c in range(2)]
        rows.append(jnp.concatenate(parts, axis=1))
    return jnp.concatenate(rows, axis=0)


def token_mask(mask):
    t = iota((4 * AREA, 2 * WIN), 0)
    lane = iota((4 * AREA, 2 * WIN), 1)
    w, i, j = t // AREA, (t % AREA) // WIN, t % WIN
    pick_row = (lane == WIN * (w // 2) + i).astype(F32)
    pick_col = (lane == WIN * (w % 2) + j).astype(F32)
    rows = dot(pick_row, mask, 1, 0)
    return jnp.sum(rows * pick_col, axis=1, keepdims=True)


def norm_rows(x):
    center = x - jnp.mean(x, axis=-1, keepdims=True)
    spread = jnp.mean(center * center, axis=-1, keepdims=True)
    scaling = lax.rsqrt(spread + 1e-05)
    return center * scaling, scaling


def head_blocks():
    row = iota((GROUP, GROUP), 0) // HEAD_DIM
    col = iota((GROUP, GROUP), 1) // HEAD_DIM
    return (row == col).astype(F32)


def stack_heads(part, blocks):
    return jnp.concatenate([part] * GROUP_HEADS, axis=0) * blocks.astype(part.dtype)


def unstack_heads(full, blocks):
    kept = full * blocks
    return sum(kept[h * AREA : (h + 1) * AREA] for h in range(GROUP_HEADS))


def lanes(g):
    return slice(g * GROUP, (g + 1) * GROUP)


def prep_kernel(x_ref, mask_ref, all_ref, top_ref, bottom_ref):
    ocean = token_mask(mask_ref[0].astype(F32))
    x = x_ref[0].astype(F32)
    for w in range(4):
        part = jnp.where(ocean[w * AREA : (w + 1) * AREA] > 0.5, window_of(x, w), LAND)
        part = part.astype(BF16)
        all_ref[w] = part
        (top_ref if w < 2 else bottom_ref)[w % 2] = part


def own_kernel(
    tok_ref, cot_ref, mask_ref, wqkv_ref, wout_ref, gain_ref,
    q_ref, kv_ref, gm_ref, gb_ref, hid_ref, info_ref,
):
    ocean = token_mask(mask_ref[0].astype(F32))
    tokens = tok_ref[...].reshape(4 * AREA, D).astype(F32)
    normed, _ = norm_rows(tokens)
    hidden = (normed * gain_ref[...]).astype(BF16)
    hid_ref[...] = hidden
    projected = dot(hidden, wqkv_ref[...], 1, 0).astype(BF16)
    q_ref[...] = (projected[:, :D] * BF16(HEAD_DIM ** -0.5)).reshape(4, AREA, D)
    kv_ref[...] = projected[:, D:].reshape(4, AREA, 2 * D)
    cot = cot_ref[0].astype(F32)
    for w in range(4):
        branch = window_of(cot, w) * ocean[w * AREA : (w + 1) * AREA]
        gb_ref[w * AREA : (w + 1) * AREA, :] = branch.astype(BF16)
    gm = dot(gb_ref[...], wout_ref[...], 1, 1).astype(BF16)
    gm_ref[...] = gm.reshape(4, AREA, D)
    alive = []
    for w in range(4):
        alive.append((jnp.max(ocean[w * AREA : (w + 1) * AREA]) > 0.5).astype(jnp.int32))
        info_ref[1 + w] = alive[w]
    info_ref[0] = jnp.where(
        alive[3] == 0, 3, jnp.where(alive[2] == 0, 2, jnp.where(alive[1] == 0, 1, 0))
    )


def slot_window(info_ref, slot):
    return slot + (slot >= info_ref[0]).astype(jnp.int32)


def near_places(w):
    r, c = w // 2, w % 2
    lon_at, lat_at = 2 * (1 - c), 4 + 2 * r
    return lon_at, lon_at + 1, lat_at, lat_at + 1, 8 + 2 * r + 1 - c


def land_bias(tokens):
    first = (iota((8, D), 1) == 0).astype(BF16)
    picked = dot(first, tokens, 1, 1)[:1]
    return jnp.where(picked > 0.5 * LAND, NEVER, 0.0)


def main_kernel(
    info_ref, place_ref, q_ref, kv_ref, gm_ref, gb_ref, hid_ref, tok_ref, lon_ref, up_ref,
    down_ref, upc_ref, downc_ref, x_ref, mask_ref, wqkv_ref, wout_ref, gain_ref,
    out_ref, gq_ref, own_ref, side_ref, top_ref, bottom_ref,
    keep_a_ref, send_a_ref, keep_b_ref, send_b_ref,
    kvh, hidh, bias, kcat, acc, mixed,
):
    up_ok, down_ok = place_ref[0] > 0, place_ref[0] < place_ref[1] - 1
    groups = (
        ((lon_ref, 0), (lon_ref, 2), (lon_ref, 1), (lon_ref, 3)),
        ((up_ref, 0), (up_ref, 1), (down_ref, 0), (down_ref, 1)),
        ((upc_ref, 0), (upc_ref, 1), (downc_ref, 0), (downc_ref, 1)),
    )
    for n, group in enumerate(groups):
        low = jnp.concatenate([ref[at] for ref, at in group], axis=0)
        normed, _ = norm_rows(low.astype(F32))
        hidden = (normed * gain_ref[...]).astype(BF16)
        hidh[n * 4 * AREA : (n + 1) * 4 * AREA] = hidden
        kvh[4 * n : 4 * n + 4] = dot(hidden, wqkv_ref[:, D:], 1, 0).astype(BF16).reshape(4, AREA, 2 * D)
        row = land_bias(low)
        for k in range(4):
            part = row[:, k * AREA : (k + 1) * AREA]
            if n > 0:
                part = jnp.where(up_ok if k < 2 else down_ok, part, NEVER)
            bias[4 + 4 * n + k] = jnp.broadcast_to(part, (8, AREA))
    own_row = land_bias(tok_ref[...].reshape(4 * AREA, D))
    for w in range(4):
        bias[w] = jnp.broadcast_to(own_row[:, w * AREA : (w + 1) * AREA], (8, AREA))
    acc[...] = jnp.zeros_like(acc)
    mixed[...] = jnp.zeros_like(mixed)
    gq_ref[...] = jnp.zeros_like(gq_ref)
    blocks = head_blocks()
    for slot in range(3):
        kcat[slot * AREA : (slot + 1) * AREA] = kv_ref[slot_window(info_ref, slot)]

    def slot_step(slot, carry):
        w = slot_window(info_ref, slot)

        @pl.when(info_ref[1 + w] > 0)
        def _():
            places = [slot_window(info_ref, k) for k in range(3)] + [4 + at for at in near_places(w)]
            for k in range(3, 8):
                kcat[k * AREA : (k + 1) * AREA] = kvh[places[k] - 4]
            bias_row = jnp.concatenate([bias[at][:1] for at in places], axis=1)
            for g in range(GROUPS):
                at_v = slice(D + g * GROUP, D + (g + 1) * GROUP)
                q_stack = stack_heads(q_ref[w, :, lanes(g)], blocks)
                gm_stack = stack_heads(gm_ref[w, :, lanes(g)], blocks)
                keys = kcat[:, lanes(g)]
                values = kcat[:, at_v]
                scores = dot(q_stack, keys, 1, 1) + bias_row
                weights = jnp.exp(scores - jnp.max(scores, axis=1, keepdims=True))
                probs = weights * (1.0 / jnp.sum(weights, axis=1, keepdims=True))
                low = probs.astype(BF16)
                out = unstack_heads(dot(low, values, 1, 0), blocks).astype(BF16)
                mixed[w, :, lanes(g)] = out
                out_stack = jnp.concatenate([out] * GROUP_HEADS, axis=0).astype(F32)
                delta = jnp.sum(out_stack * gm_stack.astype(F32), axis=1, keepdims=True)
                grad_probs = dot(gm_stack, values, 1, 1)
                grad_scores = (probs * (grad_probs - delta)).astype(BF16)
                grad = unstack_heads(dot(grad_scores, keys, 1, 0), blocks)
                gq_ref[w, :, lanes(g)] = (grad * HEAD_DIM ** -0.5).astype(BF16)
                grad_keys = dot(grad_scores, q_stack, 0, 0)
                grad_values = dot(low, gm_stack, 0, 0)
                for k in range(8):
                    rows = slice(k * AREA, (k + 1) * AREA)
                    acc[places[k], :, lanes(g)] += grad_keys[rows]
                    acc[places[k], :, at_v] += grad_values[rows]

        return carry

    lax.fori_loop(0, 3, slot_step, 0)
    flat = mixed[...].reshape(4 * AREA, D)
    ocean = token_mask(mask_ref[0].astype(F32))
    added = (dot(flat, wout_ref[...], 1, 0) * ocean).reshape(4, AREA, D)
    out_ref[0] = (x_ref[0].astype(F32) + grid_of([added[w] for w in range(4)])).astype(BF16)
    own_ref[...] = acc[:4]
    side_ref[...] = acc[4:8]
    low = acc[4:].astype(BF16)
    for k in range(2):
        top_ref[k], top_ref[2 + k] = low[4 + k], low[8 + k]
        bottom_ref[k], bottom_ref[2 + k] = low[6 + k], low[10 + k]
    grad_own = acc[:4].astype(BF16).reshape(4 * AREA, 2 * D)
    grad_halo = low.reshape(12 * AREA, 2 * D)
    gq = gq_ref[...].reshape(4 * AREA, D)
    lev = place_ref[2]
    for rel in range(4):
        at = pl.ds(pl.multiple_of((lev ^ rel) * 128, 128), 128)
        to_a, to_b = (keep_a_ref, keep_b_ref) if rel % 2 == 0 else (send_a_ref, send_b_ref)
        hid = hid_ref[:, at]
        to_a[rel // 2, :, :D] = dot(hid, gq, 0, 0).astype(BF16)
        to_a[rel // 2, :, D:] = dot(mixed[:, :, at].reshape(4 * AREA, 128), gb_ref[...], 0, 0).astype(BF16)
        to_b[rel // 2] = (dot(hid, grad_own, 0, 0) + dot(hidh[:, at], grad_halo, 0, 0)).astype(BF16)


def input_kernel(
    own_ref, up_ref, down_ref, lon_ref, gq_ref, tok_ref, cot_ref, wqkv_ref, gain_ref, ing_ref, gkv
):
    for w in range(4):
        lat_ref = up_ref if w < 2 else down_ref
        total = own_ref[w] + lat_ref[w % 2].astype(F32) + lon_ref[w].astype(F32)
        gkv[w * AREA : (w + 1) * AREA] = total.astype(BF16)
    grad_hidden = dot(gq_ref[...].reshape(4 * AREA, D), wqkv_ref[:, :D], 1, 1)
    grad_hidden = grad_hidden + dot(gkv[...], wqkv_ref[:, D:], 1, 1)
    normed, scaling = norm_rows(tok_ref[...].reshape(4 * AREA, D).astype(F32))
    scaled = grad_hidden * gain_ref[...]
    correction = (
        scaled
        - jnp.mean(scaled, axis=-1, keepdims=True)
        - normed * jnp.mean(scaled * normed, axis=-1, keepdims=True)
    )
    added = (scaling * correction).reshape(4, AREA, D)
    ing_ref[0] = (cot_ref[0].astype(F32) + grid_of([added[w] for w in range(4)])).astype(BF16)


def finish_kernel(whole_rows, place_ref, own_ref, *refs):
    others, (wqkv_ref, gain_ref, qkv_ref, out_ref, gg_ref) = refs[:-5], refs[-5:]
    lat, lat_count, lev = place_ref[0], place_ref[1], place_ref[2]
    for k, ref in enumerate((own_ref,) + tuple(others)):
        z = lax.rem(lat - k + lat_count, lat_count)
        value = ref[...].astype(F32)
        for x in range(value.shape[0]):
            qkv_ref[x, z, :, :D] = value[x, :, :D]
            qkv_ref[x, z, :, D:] = value[x, :, 2 * D :]
            out_ref[x, z] = value[x, :, D : 2 * D]
    if whole_rows:
        at = pl.ds(pl.multiple_of(lev * 128, 128), 128)
        product = wqkv_ref[at, :].astype(F32) * qkv_ref[...].reshape(128, 3 * D)
        sums = dot(jnp.ones((8, 3 * D), F32), product, 1, 1, EXACT)[:1]
        gg_ref[...] = sums / gain_ref[:, at]
    else:
        gg_ref[...] = jnp.zeros_like(gg_ref)


SMEM = pl.BlockSpec(memory_space=pltpu.SMEM)


def whole_block(dims):
    return pl.BlockSpec(dims, lambda i: (0,) * len(dims), pipeline_mode=pl.Buffered(1))


def call(kernel, outs, scalars, arrays, scratch=(), flops=0, name=None, smem_out=False):
    moved = sum(a.size * a.dtype.itemsize for a in arrays)
    moved += sum(o.size * o.dtype.itemsize for o in outs)
    out_specs = [whole_block(o.shape) for o in outs]
    if smem_out:
        out_specs[-1] = SMEM
    return pl.pallas_call(
        kernel,
        grid=(1,),
        out_shape=outs,
        in_specs=[SMEM] * len(scalars) + [whole_block(a.shape) for a in arrays],
        out_specs=out_specs,
        scratch_shapes=list(scratch),
        compiler_params=pltpu.CompilerParams(vmem_limit_bytes=62 * 1024 * 1024),
        cost_estimate=pl.CostEstimate(flops=flops, bytes_accessed=moved, transcendentals=0),
        name=name,
    )(*scalars, *arrays)


def shape(dims, dtype=BF16):
    return jax.ShapeDtypeStruct(dims, dtype)


def ring(count, step, periodic):
    return [
        (i, (i + step) % count) for i in range(count) if periodic or 0 <= i + step < count
    ]


def lon_halo(own):
    count = lax.axis_size("lon")
    if count == 2:
        return lax.ppermute(own, "lon", [(0, 1), (1, 0)])
    left = lax.ppermute(own[1::2], "lon", ring(count, 1, True))
    right = lax.ppermute(own[0::2], "lon", ring(count, -1, True))
    return jnp.stack([right, left], axis=1).reshape(own.shape)


def lon_return(side):
    count = lax.axis_size("lon")
    if count == 2:
        return lax.ppermute(side, "lon", [(0, 1), (1, 0)])
    from_left = lax.ppermute(side[0::2], "lon", ring(count, 1, True))
    from_right = lax.ppermute(side[1::2], "lon", ring(count, -1, True))
    return jnp.stack([from_left, from_right], axis=1).reshape(side.shape)


def lat_halo(top, bottom):
    count = lax.axis_size("lat")
    up = lax.ppermute(bottom, "lat", ring(count, 1, False))
    down = lax.ppermute(top, "lat", ring(count, -1, False))
    return up, down


def core_sum(keep, send):
    arrived = lax.ppermute(send, "lev", [(i, i ^ 1) for i in range(4)])
    return keep.astype(F32) + arrived.astype(F32)


def level_sum(parts):
    arrived = lax.ppermute(parts[1].astype(BF16), "lev", [(i, i ^ 2) for i in range(4)])
    return parts[0] + arrived.astype(F32)


def lon_sum(parts):
    lon, count = lax.axis_index("lon"), lax.axis_size("lon")
    own = lax.dynamic_index_in_dim(parts, lon, 0, False)
    for k in range(1, count):
        piece = lax.dynamic_index_in_dim(parts, (lon + k) % count, 0, False).astype(BF16)
        own = own + lax.ppermute(piece, "lon", ring(count, k, True)).astype(F32)
    return own


def plane_parts(own):
    lon, lon_count = lax.axis_index("lon"), lax.axis_size("lon")
    lat, lat_count = lax.axis_index("lat"), lax.axis_size("lat")
    parts = own.reshape(lat_count, -1, own.shape[1])
    own = lax.dynamic_index_in_dim(parts, lat, 0, False)
    low = parts.astype(BF16)
    for k in range(1, lat_count):
        piece = lax.dynamic_index_in_dim(low, (lat + k) % lat_count, 0, False)
        own = own + lax.ppermute(piece, "lat", ring(lat_count, k, True)).astype(F32)
    own = own.astype(BF16)
    across = [own] + [
        lax.ppermute(own, "lon", ring(lon_count, k, True)) for k in range(1, lon_count)
    ]
    if lon_count == 2:
        first = lon == 0
        across = [jnp.where(first, across[0], across[1]), jnp.where(first, across[1], across[0])]
        both = jnp.stack(across)
    else:
        both = jnp.roll(jnp.stack(across[:1] + across[:0:-1]), lon, axis=0)
    return [both] + [lax.ppermute(both, "lat", ring(lat_count, k, True)) for k in range(1, lat_count)]


def on_device(tokens_in, cotangent, qkv_weight, out_weight, norm_gain, ocean_mask):
    lat_count, lon_count = lax.axis_size("lat"), lax.axis_size("lon")
    gain = norm_gain.reshape(1, D)
    place = jnp.stack(
        [lax.axis_index("lat"), jnp.int32(lat_count), lax.axis_index("lev")]
    ).astype(jnp.int32)
    half = shape((2, AREA, D))
    four = shape((4, AREA, D))
    flat = shape((4 * AREA, D))
    wide = shape((4, AREA, 2 * D))
    tok, tok_top, tok_bottom = call(
        prep_kernel, [four, half, half], [], [tokens_in, ocean_mask], name="prep"
    )
    tok_lon = lon_halo(tok)
    tok_up, tok_down = lat_halo(tok_top, tok_bottom)
    q, kv, gm, gb, hid, info = call(
        own_kernel,
        [four, wide, four, flat, flat, shape((8,), jnp.int32)],
        [],
        [tok, cotangent, ocean_mask, qkv_weight, out_weight, gain],
        flops=2 * 256 * 512 * 2048,
        name="own",
        smem_out=True,
    )
    tok_upc, tok_downc = lat_halo(tok_lon[:2], tok_lon[2:])
    share = shape((2, 128, 2 * D))
    wide32 = shape((4, AREA, 2 * D), F32)
    layer_out, gq, own_kv, side_kv, top_kv, bottom_kv, keep_a, send_a, keep_b, send_b = call(
        main_kernel,
        [shape(tokens_in.shape), four, wide32, wide32, wide, wide, share, share, share, share],
        [info, place],
        [q, kv, gm, gb, hid, tok, tok_lon, tok_up, tok_down, tok_upc, tok_downc,
         tokens_in, ocean_mask, qkv_weight, out_weight, gain],
        [pltpu.VMEM((12, AREA, 2 * D), BF16), pltpu.VMEM((12 * AREA, D), BF16),
         pltpu.VMEM((16, 8, AREA), F32), pltpu.VMEM((KEYS, 2 * D), BF16),
         pltpu.VMEM((16, AREA, 2 * D), F32), pltpu.VMEM((4, AREA, D), BF16)],
        flops=2 * 768 * 512 * 1024 + 3 * 12 * 2 * 512 * 256 * 256 + 2 * 1024 * 512 * 2048,
        name="main",
    )
    part_a = level_sum(core_sum(keep_a, send_a))
    part_a = lon_sum(part_a.reshape(lon_count, -1, 2 * D))
    part_b = core_sum(keep_b, send_b)
    part_b = jnp.swapaxes(part_b.reshape(2, lon_count, -1, 2 * D), 0, 1)
    part_b = level_sum(lon_sum(part_b))
    up_kv, down_kv = lat_halo(top_kv, bottom_kv)
    side_kv = side_kv.reshape(2, 2, AREA, 2 * D)
    arrived = jnp.stack([up_kv[2:], down_kv[2:]], axis=1).astype(F32)
    side_kv = jnp.swapaxes(side_kv + arrived, 0, 1).astype(BF16).reshape(4, AREA, 2 * D)
    lon_kv = lon_return(side_kv)
    input_grad = call(
        input_kernel,
        [shape(tokens_in.shape)],
        [],
        [own_kv, up_kv, down_kv, lon_kv, gq, tok, cotangent, qkv_weight, gain],
        [pltpu.VMEM((4 * AREA, 2 * D), BF16)],
        flops=2 * 256 * 512 * 1536,
        name="input",
    )[0]
    parts = plane_parts(jnp.concatenate([part_a, part_b], axis=1))
    rows = parts[0].shape[1]
    whole_rows = rows % 8 == 0
    qkv_grad, out_grad, gain_grad = call(
        functools.partial(finish_kernel, whole_rows),
        [shape((lon_count, lat_count, rows, 3 * D), F32), shape((lon_count, lat_count, rows, D), F32),
         shape((1, 128), F32)],
        [place],
        parts + [qkv_weight, gain],
        name="finish",
    )
    qkv_grad = qkv_grad.reshape(128, 3 * D)
    out_grad = out_grad.reshape(128, D)
    if whole_rows:
        gain_grad = gain_grad.reshape(128)
    else:
        at = lax.axis_index("lev") * 128
        rows_in = lax.dynamic_slice_in_dim(qkv_weight, at, 128, 0).astype(F32)
        gain_grad = jnp.sum(rows_in * qkv_grad, axis=1)
        gain_grad = gain_grad / lax.dynamic_slice_in_dim(norm_gain, at, 128, 0)
    return layer_out, input_grad, qkv_grad, out_grad, gain_grad


def solution(mesh):
    placed = (
        P("lev", "lat", "lon", None),
        P("lev", "lat", "lon", None),
        P(),
        P(),
        P(),
        P("lev", "lat", "lon"),
    )
    return jax.shard_map(
        on_device,
        mesh=mesh,
        in_specs=placed,
        out_specs=(
            P("lev", "lat", "lon", None),
            P("lev", "lat", "lon", None),
            P("lev", None),
            P("lev", None),
            P("lev"),
        ),
        check_vma=False,
    )
```

```python
import jax
import jax.numpy as jnp
from jax import lax
from jax.experimental import pallas as pl
from jax.experimental.pallas import tpu as pltpu
from jax.sharding import PartitionSpec as P

HEADS = 8
WIN = 8
AREA = WIN * WIN
D = 512
HEAD_DIM = D // HEADS
GROUP = 256
GROUP_HEADS = GROUP // HEAD_DIM
GROUPS = D // GROUP
KEYS = 8 * AREA
LAND = 1000.0
NEVER = -1e9
FAR = 1e30
F32 = jnp.float32
BF16 = jnp.bfloat16
EXACT = lax.Precision.HIGHEST


def dot(a, b, ca, cb, precision=None):
    return lax.dot_general(
        a, b, (((ca,), (cb,)), ((), ())), preferred_element_type=F32, precision=precision
    )


def iota(shape, dim):
    return lax.broadcasted_iota(jnp.int32, shape, dim)


def window_of(grid, w):
    r, c = divmod(w, 2)
    part = grid[r * WIN : (r + 1) * WIN, c * WIN : (c + 1) * WIN, :]
    return part.reshape(AREA, grid.shape[-1])


def grid_of(windows):
    rows = []
    for r in range(2):
        parts = [windows[2 * r + c].reshape(WIN, WIN, -1) for c in range(2)]
        rows.append(jnp.concatenate(parts, axis=1))
    return jnp.concatenate(rows, axis=0)


def token_mask(mask):
    t = iota((4 * AREA, 2 * WIN), 0)
    lane = iota((4 * AREA, 2 * WIN), 1)
    w, i, j = t // AREA, (t % AREA) // WIN, t % WIN
    pick_row = (lane == WIN * (w // 2) + i).astype(F32)
    pick_col = (lane == WIN * (w % 2) + j).astype(F32)
    rows = dot(pick_row, mask, 1, 0)
    return jnp.sum(rows * pick_col, axis=1, keepdims=True)


def norm_rows(x):
    center = x - jnp.mean(x, axis=-1, keepdims=True)
    spread = jnp.mean(center * center, axis=-1, keepdims=True)
    scaling = lax.rsqrt(spread + 1e-05)
    return center * scaling, scaling


def head_blocks():
    row = iota((GROUP, GROUP), 0) // HEAD_DIM
    col = iota((GROUP, GROUP), 1) // HEAD_DIM
    return (row == col).astype(F32)


def stack_heads(part, blocks):
    return jnp.concatenate([part] * GROUP_HEADS, axis=0) * blocks.astype(part.dtype)


def unstack_heads(full, blocks):
    kept = full * blocks
    return sum(kept[h * AREA : (h + 1) * AREA] for h in range(GROUP_HEADS))


def lanes(g):
    return slice(g * GROUP, (g + 1) * GROUP)


def lat_side(row):
    return (row + lax.axis_index("lat") + 1) % 2


def load(pairs, sems):
    copies = [pltpu.make_async_copy(a, b, sems.at[k]) for k, (a, b) in enumerate(pairs)]
    for copy in copies:
        copy.start()
    return copies


def wait(copies):
    for copy in copies:
        copy.wait()


def prep_kernel(
    x_hbm, cot_hbm, mask_hbm, all_ref, first_ref, second_ref, gb_ref, x_ref, cot_ref, mask_ref, sems
):
    copies = load(((mask_hbm, mask_ref), (x_hbm, x_ref), (cot_hbm, cot_ref)), sems)
    copies[0].wait()
    ocean = token_mask(mask_ref[0].astype(F32))
    copies[1].wait()
    x = x_ref[0].astype(F32)
    parts = []
    for w in range(4):
        part = jnp.where(ocean[w * AREA : (w + 1) * AREA] > 0.5, window_of(x, w), LAND)
        parts.append(part.astype(BF16))
        all_ref[w] = parts[w]
    odd = lax.axis_index("lat") % 2 == 1
    for c in range(2):
        first_ref[c] = jnp.where(odd, parts[c], parts[2 + c])
        second_ref[c] = jnp.where(odd, parts[2 + c], parts[c])
    copies[2].wait()
    cot = cot_ref[0].astype(F32)
    for w in range(4):
        rows = slice(w * AREA, (w + 1) * AREA)
        gb_ref[w] = (window_of(cot, w) * ocean[rows]).astype(BF16)


def land_bias(tokens):
    first = (iota((8, D), 1) == 0).astype(BF16)
    picked = dot(first, tokens, 1, 1)[:1]
    return jnp.where(picked > 0.5 * LAND, NEVER, 0.0)


def hidden_of(tokens, gain_ref):
    normed, _ = norm_rows(tokens.astype(F32))
    return (normed * gain_ref[...]).astype(BF16)


def write_block(tokens, wqkv_ref, gain_ref, q_ref, kv_ref, hid_ref, bias_ref, info_ref):
    hidden = hidden_of(tokens, gain_ref)
    hid_ref[: 4 * AREA] = hidden
    projected = dot(hidden, wqkv_ref[...], 1, 0).astype(BF16)
    q_ref[...] = (projected[:, :D] * BF16(HEAD_DIM ** -0.5)).reshape(4, AREA, D)
    kv_ref[:4] = projected[:, D:].reshape(4, AREA, 2 * D)
    row = land_bias(tokens)
    alive = []
    for w in range(4):
        part = row[:, w * AREA : (w + 1) * AREA]
        bias_ref[w] = jnp.broadcast_to(part, (8, AREA))
        alive.append((jnp.max(part) > 0.5 * NEVER).astype(jnp.int32))
        info_ref[1 + w] = alive[w]
    info_ref[0] = jnp.where(
        alive[3] == 0, 3, jnp.where(alive[2] == 0, 2, jnp.where(alive[1] == 0, 1, 0))
    )


def own_kernel(
    tok_ref, wqkv_hbm, gain_hbm, q_ref, kv_ref, hid_ref, bias_ref, info_ref, wqkv_ref, gain_ref, sems
):
    copies = load(((gain_hbm, gain_ref), (wqkv_hbm, wqkv_ref)), sems)
    wait(copies)
    tokens = tok_ref[...].reshape(4 * AREA, D)
    write_block(tokens, wqkv_ref, gain_ref, q_ref, kv_ref, hid_ref, bias_ref, info_ref)


def lat_block(first_ref, second_ref, wkv_ref, gain_ref, kv_ref, hid_ref, bias_ref, at):
    lat, lat_count = lax.axis_index("lat"), lax.axis_size("lat")
    odd = lat % 2 == 1
    first_ok = jnp.logical_or(odd, lat < lat_count - 1)
    second_ok = jnp.where(odd, lat_count - 1 - lat, lat) > 0
    parts = [first_ref[0], first_ref[1], second_ref[0], second_ref[1]]
    tokens = jnp.concatenate(parts, axis=0)
    hidden = hidden_of(tokens, gain_ref)
    hid_ref[at * AREA : (at + 4) * AREA] = hidden
    kv_ref[at : at + 4] = dot(hidden, wkv_ref[...], 1, 0).astype(BF16).reshape(4, AREA, 2 * D)
    row = land_bias(tokens)
    for k in range(4):
        part = row[:, k * AREA : (k + 1) * AREA]
        part = jnp.where(first_ok if k < 2 else second_ok, part, NEVER)
        bias_ref[at + k] = jnp.broadcast_to(part, (8, AREA))


def near_kernel(
    lon_ref, first_ref, second_ref, wqkv_hbm, gain_hbm,
    q_ref, kv_ref, hid_ref, bias_ref, info_ref, wqkv_ref, gain_ref, sems,
):
    wait(load(((gain_hbm, gain_ref), (wqkv_hbm, wqkv_ref)), sems))
    tokens = lon_ref[...].reshape(4 * AREA, D)
    write_block(tokens, wqkv_ref, gain_ref, q_ref, kv_ref, hid_ref, bias_ref, info_ref)
    lat_block(first_ref, second_ref, wqkv_ref.at[:, D:], gain_ref, kv_ref, hid_ref, bias_ref, 4)


def main_kernel(
    pair, info_ref, infon_ref, q_own, q_near, kv_own, kv_near, hid_own, hid_near, bias_own,
    bias_near, gb_own, gb_near, first_ref, second_ref, wqkv_hbm, wout_hbm, gain_hbm,
    mixed_ref, gq_ref, own_ref, back1_ref, back2_ref, *rest,
):
    sums = rest[:-15]
    q, kv, hid, gb, bias, gm, kcat, acc, dkv, mixed, gq, wkv_ref, wout_ref, gain_ref, sems = rest[-15:]
    pairs = [
        (gain_hbm, gain_ref), (wqkv_hbm.at[:, D:], wkv_ref), (wout_hbm, wout_ref),
        (gb_own, gb.at[:4]), (q_own, q.at[:4]), (kv_own, kv.at[:4]), (kv_near, kv.at[4:12]),
        (hid_own, hid.at[: 4 * AREA]), (hid_near, hid.at[4 * AREA : 12 * AREA]),
        (bias_own, bias.at[:4]), (bias_near, bias.at[4:12]),
    ]
    if pair:
        pairs += [(q_near, q.at[4:]), (gb_near, gb.at[4:])]
    copies = load(pairs, sems)
    acc[...] = jnp.zeros_like(acc)
    mixed[...] = jnp.zeros_like(mixed)
    gq[...] = jnp.zeros_like(gq)
    blocks = head_blocks()
    wait(copies[:2])
    lat_block(first_ref, second_ref, wkv_ref, gain_ref, kv, hid, bias, 12)
    wait(copies[2:])
    blocks_held = 2 if pair else 1
    held = 4 * blocks_held
    gb_flat = gb[...].reshape(held * AREA, D)
    gm[...] = dot(gb_flat, wout_ref[...], 1, 1).astype(BF16).reshape(gm.shape)

    def window_at(b, slot):
        left_out = jnp.where(b == 0, info_ref[0], infon_ref[0])
        return slot + (slot >= left_out).astype(jnp.int32)

    def step(n, carry):
        b = n // 3
        w = window_at(b, n % 3)

        @pl.when(jnp.where(b == 0, info_ref[1 + w], infon_ref[1 + w]) > 0)
        def _():
            r, c = w // 2, w % 2
            mine, other, side = 4 * b, 4 * (1 - b), 2 * lat_side(r)
            places = [mine + window_at(b, k) for k in range(3)]
            places += [other + 1 - c, other + 3 - c]
            places += [8 + mine + side, 9 + mine + side, 8 + other + side + 1 - c]
            at = mine + w
            for k in range(8):
                kcat[k * AREA : (k + 1) * AREA] = kv[places[k]]
            bias_row = jnp.concatenate([bias[place][:1] for place in places], axis=1)
            spans = [slice(D + g * GROUP, D + (g + 1) * GROUP) for g in range(GROUPS)]
            both = range(GROUPS)
            q_stack = [stack_heads(q[at, :, lanes(g)], blocks) for g in both]
            gm_stack = [stack_heads(gm[at, :, lanes(g)], blocks) for g in both]
            scores = [dot(q_stack[g], kcat[:, lanes(g)], 1, 1) + bias_row for g in both]
            grad_probs = [dot(gm_stack[g], kcat[:, spans[g]], 1, 1) for g in both]
            weights = [jnp.exp(x - jnp.max(x, axis=1, keepdims=True)) for x in scores]
            probs = [x * (1.0 / jnp.sum(x, axis=1, keepdims=True)) for x in weights]
            low = [x.astype(BF16) for x in probs]
            out = [unstack_heads(dot(low[g], kcat[:, spans[g]], 1, 0), blocks).astype(BF16) for g in both]
            delta = [jnp.sum(probs[g] * grad_probs[g], axis=1, keepdims=True) for g in both]
            grad_scores = [(probs[g] * (grad_probs[g] - delta[g])).astype(BF16) for g in both]
            grad = [unstack_heads(dot(grad_scores[g], kcat[:, lanes(g)], 1, 0), blocks) for g in both]
            grad_keys = [dot(grad_scores[g], q_stack[g], 0, 0) for g in both]
            grad_values = [dot(low[g], gm_stack[g], 0, 0) for g in both]
            for g in both:
                mixed[at, :, lanes(g)] = out[g]
                gq[at, :, lanes(g)] = (grad[g] * HEAD_DIM ** -0.5).astype(BF16)
                for k in range(8):
                    rows = slice(k * AREA, (k + 1) * AREA)
                    acc[places[k], :, lanes(g)] += grad_keys[g][rows]
                    acc[places[k], :, spans[g]] += grad_values[g][rows]

        return carry

    lax.fori_loop(0, 3 * blocks_held, step, 0)
    dkv[...] = acc[...].astype(BF16)
    own_ref[...] = dkv[:4]
    gq_ref[...] = gq[:4]
    mixed_ref[...] = mixed[:4]
    back1_ref[:2] = dkv[8:10]
    back2_ref[:2] = dkv[10:12]
    lev = lax.axis_index("lev")

    def columns(rel):
        return pl.ds(pl.multiple_of((lev ^ rel) * 128, 128), 128)

    def hid_part(rel, windows):
        return hid[: windows * AREA, columns(rel)]

    def mix_part(rel):
        return mixed[:, :, columns(rel)].reshape(held * AREA, 128)

    def grad_part(at, width):
        return dkv[:, :, at : at + width].reshape(16 * AREA, width)

    gq_flat = gq[...].reshape(held * AREA, D)
    if pair:
        keep, send = sums
        odd, lon = lax.axis_index("lat") % 2, lax.axis_index("lon")

        def put(rel, at, value):
            to = keep if rel % 2 == 0 else send
            value = value.astype(BF16)
            for k in range(2):
                to[rel // 2, k ^ odd, :, at : at + D] = value[k * 64 : (k + 1) * 64]

        @pl.when(lon == 0)
        def _():
            for rel in range(4):
                put(rel, 0, dot(hid_part(rel, 8), gq_flat, 0, 0))
                put(rel, D, dot(mix_part(rel), gb_flat, 0, 0))

        @pl.when(lon == 1)
        def _():
            for rel in range(4):
                part = hid_part(rel, 16)
                put(rel, 0, dot(part, grad_part(0, D), 0, 0))
                put(rel, D, dot(part, grad_part(D, D), 0, 0))
    else:
        keep, send, side_ref = sums
        side_ref[...] = dkv[4:8]
        back1_ref[2:] = dkv[12:14]
        back2_ref[2:] = dkv[14:]
        for rel in range(4):
            to = keep if rel % 2 == 0 else send
            to[rel // 2, :, :D] = dot(hid_part(rel, 4), gq_flat, 0, 0).astype(BF16)
            to[rel // 2, :, D : 2 * D] = dot(mix_part(rel), gb_flat, 0, 0).astype(BF16)
            to[rel // 2, :, 2 * D :] = dot(hid_part(rel, 16), grad_part(0, 2 * D), 0, 0).astype(BF16)


def split_kernel(keep_ref, come_ref, own_ref, lev_ref, lat_ref, far_ref):
    for k, ref in enumerate((own_ref, lat_ref, lev_ref, far_ref)):
        total = keep_ref[k // 2, k % 2].astype(F32) + come_ref[k // 2, k % 2].astype(F32)
        ref[...] = total.astype(ref.dtype)


def input_kernel(
    pair, own_ref, back1_ref, back2_ref, gq_ref, tok_ref, mixed_ref, *rest,
):
    refs = rest if pair else rest[1:]
    cot_hbm, x_hbm, mask_hbm, wqkv_hbm, wout_hbm, gain_hbm, out_ref, ing_ref = refs[:8]
    gkv, cot_ref, x_ref, mask_ref, wqkv_ref, wout_ref, gain_ref, sems = refs[8:]
    pairs = (
        (x_hbm, x_ref), (mask_hbm, mask_ref), (wout_hbm, wout_ref), (gain_hbm, gain_ref),
        (wqkv_hbm, wqkv_ref), (cot_hbm, cot_ref),
    )
    copies = load(pairs, sems)
    odd = lax.axis_index("lat") % 2 == 1
    for w in range(4):
        one, two = back1_ref[w % 2].astype(F32), back2_ref[w % 2].astype(F32)
        lat_part = jnp.where(odd, one, two) if w < 2 else jnp.where(odd, two, one)
        total = own_ref[w].astype(F32) + lat_part
        if not pair:
            total = total + rest[0][w].astype(F32)
        gkv[w * AREA : (w + 1) * AREA] = total.astype(BF16)
    normed, scaling = norm_rows(tok_ref[...].reshape(4 * AREA, D).astype(F32))
    wait(copies)
    ocean = token_mask(mask_ref[0].astype(F32))
    added = (dot(mixed_ref[...].reshape(4 * AREA, D), wout_ref[...], 1, 0) * ocean).reshape(4, AREA, D)
    out_ref[0] = (x_ref[0].astype(F32) + grid_of([added[w] for w in range(4)])).astype(BF16)
    grad_hidden = dot(gq_ref[...].reshape(4 * AREA, D), wqkv_ref[:, :D], 1, 1)
    grad_hidden = grad_hidden + dot(gkv[...], wqkv_ref[:, D:], 1, 1)
    scaled = grad_hidden * gain_ref[...]
    correction = (
        scaled
        - jnp.mean(scaled, axis=-1, keepdims=True)
        - normed * jnp.mean(scaled * normed, axis=-1, keepdims=True)
    )
    added = (scaling * correction).reshape(4, AREA, D)
    ing_ref[0] = (cot_ref[0].astype(F32) + grid_of([added[w] for w in range(4)])).astype(BF16)


def gain_row(rows_ref, gain_ref, qkv_ref):
    at = pl.ds(pl.multiple_of(lax.axis_index("lev") * 128, 128), 128)
    product = rows_ref[...].astype(F32) * qkv_ref[...]
    return dot(jnp.ones((8, 3 * D), F32), product, 1, 1, EXACT)[:1] / gain_ref[:, at]


def load_rows(wqkv_hbm, rows_ref, gain_hbm, gain_ref, sems):
    at = pl.ds(pl.multiple_of(lax.axis_index("lev") * 128, 128), 128)
    return load(((wqkv_hbm.at[at, :], rows_ref), (gain_hbm, gain_ref)), sems)


def finish_rows_kernel(
    own_ref, far_ref, wqkv_hbm, gain_hbm, qkv_ref, out_ref, gg_ref, rows_ref, gain_ref, sems
):
    copies = load_rows(wqkv_hbm, rows_ref, gain_hbm, gain_ref, sems)
    half = own_ref.shape[0]
    first = lax.axis_index("lon") % 2 == 0
    own, far = own_ref[...], far_ref[...]
    for k in range(2):
        value = (jnp.where(first, own, far) if k == 0 else jnp.where(first, far, own)).astype(F32)
        rows = slice(k * half, (k + 1) * half)
        qkv_ref[rows, :D] = value[:, :D]
        qkv_ref[rows, D:] = value[:, 2 * D :]
        out_ref[rows] = value[:, D : 2 * D]
    wait(copies)
    gg_ref[...] = gain_row(rows_ref, gain_ref, qkv_ref)


def finish_pair_kernel(
    own_ref, lat_ref, lon_ref, far_ref, wqkv_hbm, gain_hbm, qkv_ref, out_ref, gg_ref,
    rows_ref, gain_ref, sems,
):
    copies = load_rows(wqkv_hbm, rows_ref, gain_hbm, gain_ref, sems)
    odd = lax.axis_index("lat") % 2 == 1
    first = lax.axis_index("lon") == 0
    for k in range(2):
        rows = slice(64 * k, 64 * k + 64)
        mine = odd if k == 1 else jnp.logical_not(odd)
        near = jnp.where(mine, own_ref[...], lat_ref[...]).astype(F32)
        away = jnp.where(mine, lon_ref[...], far_ref[...]).astype(F32)
        low, high = jnp.where(first, near, away), jnp.where(first, away, near)
        qkv_ref[rows, :D] = low[:, :D]
        out_ref[rows] = low[:, D:]
        qkv_ref[rows, D:] = high
    wait(copies)
    gg_ref[...] = gain_row(rows_ref, gain_ref, qkv_ref)


SMEM = pl.BlockSpec(memory_space=pltpu.SMEM)
VMEM = pl.BlockSpec(memory_space=pltpu.VMEM)
ANY = pl.BlockSpec(memory_space=pl.ANY)
DMAS = pltpu.SemaphoreType.DMA


def call(name, kernel, outs, scalars, arrays, far, scratch, mebibytes, flops=0, out_specs=None):
    moved = sum(a.size * a.dtype.itemsize for a in (*arrays, *far, *outs))
    return pl.pallas_call(
        kernel,
        out_shape=outs,
        in_specs=[SMEM] * len(scalars) + [VMEM] * len(arrays) + [ANY] * len(far),
        out_specs=out_specs or [VMEM] * len(outs),
        scratch_shapes=list(scratch),
        compiler_params=pltpu.CompilerParams(vmem_limit_bytes=mebibytes * 1024 * 1024),
        cost_estimate=pl.CostEstimate(flops=flops, bytes_accessed=moved, transcendentals=0),
        name=name,
    )(*scalars, *arrays, *far)


def shape(dims, dtype=BF16):
    return jax.ShapeDtypeStruct(dims, dtype)


def ring(count, step, periodic):
    return [
        (i, (i + step) % count) for i in range(count) if periodic or 0 <= i + step < count
    ]


def lon_halo(own):
    count = lax.axis_size("lon")
    if count == 2:
        return lax.ppermute(own, "lon", [(0, 1), (1, 0)])
    left = lax.ppermute(own[1::2], "lon", ring(count, 1, True))
    right = lax.ppermute(own[0::2], "lon", ring(count, -1, True))
    return jnp.stack([right, left], axis=1).reshape(own.shape)


def lon_return(side):
    count = lax.axis_size("lon")
    if count == 2:
        return lax.ppermute(side, "lon", [(0, 1), (1, 0)])
    from_left = lax.ppermute(side[0::2], "lon", ring(count, 1, True))
    from_right = lax.ppermute(side[1::2], "lon", ring(count, -1, True))
    return jnp.stack([from_left, from_right], axis=1).reshape(side.shape)


def lat_swaps(first, second):
    count = lax.axis_size("lat")
    swaps = []
    for start, value in ((0, first), (1, second)):
        pairs = [(i, i + 1) for i in range(start, count - 1, 2)]
        swaps.append(lax.ppermute(value, "lat", pairs + [(b, a) for a, b in pairs]))
    return swaps


def swap(value, axis, bit):
    return lax.ppermute(value, axis, [(i, i ^ bit) for i in range(lax.axis_size(axis))])


def halve(parts, axis, bit):
    at = (lax.axis_index(axis) // bit) % 2
    sent = lax.dynamic_index_in_dim(parts, 1 - at, 0, False).astype(BF16)
    kept = lax.dynamic_index_in_dim(parts, at, 0, False)
    return kept + swap(sent, axis, bit).astype(F32)


def rejoin(half, axis, bit):
    first = (lax.axis_index(axis) // bit) % 2 == 0
    far = swap(half, axis, bit)
    return jnp.concatenate([jnp.where(first, half, far), jnp.where(first, far, half)], axis=0)


def bits(axis):
    count = lax.axis_size(axis)
    return [1 << k for k in range(count.bit_length() - 1)]


def gradient_sum(keep, send):
    width = keep.shape[2] // 2
    total = keep.astype(F32) + swap(send, "lev", 1).astype(F32)
    part_a = total[0, :, :width] + swap(total[1, :, :width].astype(BF16), "lev", 2).astype(F32)
    part_b = total[:, :, width:]
    for bit in bits("lon"):
        rows = part_a.shape[0] // 2
        part_a = halve(part_a.reshape(2, rows, width), "lon", bit)
        part_b = halve(jnp.swapaxes(part_b.reshape(2, 2, rows, width), 0, 1), "lon", bit)
    part_b = part_b[0] + swap(part_b[1].astype(BF16), "lev", 2).astype(F32)
    return jnp.concatenate([part_a, part_b], axis=1)


def plane_sum(part):
    for bit in bits("lat"):
        part = halve(part.reshape(2, part.shape[0] // 2, -1), "lat", bit)
    part = part.astype(BF16)
    for bit in reversed(bits("lat")):
        part = rejoin(part, "lat", bit)
    for bit in reversed(bits("lon")[1:]):
        part = rejoin(part, "lon", bit)
    return part, swap(part, "lon", 1)


def pair_sum(keep, send):
    count = lax.axis_size("lat")
    width = keep.shape[-1]
    come = swap(send, "lev", 1)
    piece = shape(keep.shape[2:])
    own, to_lev, to_lat, to_far = call(
        "split", split_kernel, [shape(piece.shape, F32), piece, piece, piece], [], [keep, come], [], [], 8
    )
    from_far = lax.ppermute(to_far, ("lat", "lev"), [(i, i ^ 6) for i in range(4 * count)])
    from_lat = swap(to_lat, "lat", 1)
    from_lev = swap(to_lev, "lev", 2)
    own = own + from_lev.astype(F32) + from_lat.astype(F32) + from_far.astype(F32)
    own = own.astype(BF16)
    for bit in bits("lat")[1:]:
        own = (own.astype(F32) + swap(own, "lat", bit).astype(F32)).astype(BF16)
    return own


def pair_spread(own):
    count = lax.axis_size("lat")
    by_far = lax.ppermute(own, ("lon", "lat"), [(i, i ^ (count + 1)) for i in range(2 * count)])
    return own, swap(own, "lat", 1), swap(own, "lon", 1), by_far


def on_device(tokens_in, cotangent, qkv_weight, out_weight, norm_gain, ocean_mask):
    pair = lax.axis_size("lon") == 2
    gain = norm_gain.reshape(1, D)
    half = shape((2, AREA, D))
    four = shape((4, AREA, D))
    wide = shape((4, AREA, 2 * D))
    info_shape = shape((8,), jnp.int32)
    vmem = lambda *dims: pltpu.VMEM(dims, BF16)
    vmem32 = lambda *dims: pltpu.VMEM(dims, F32)
    grid = vmem(*tokens_in.shape)
    mask = pltpu.VMEM(ocean_mask.shape, jnp.int32)
    weight, gains = vmem(*qkv_weight.shape), vmem32(1, D)
    tok, tok_first, tok_second, gb = call(
        "prep", prep_kernel, [four, half, half, four], [], [], [tokens_in, cotangent, ocean_mask],
        [grid, grid, mask, DMAS((3,))], 8,
    )
    tok_lon = lon_halo(tok)
    tok_first, tok_second = lat_swaps(tok_first, tok_second)
    tok, tok_first, tok_second, gb = lax.optimization_barrier((tok, tok_first, tok_second, gb))
    gb_near = lon_halo(gb) if pair else gb
    q, kv, hid, bias, info = call(
        "own", own_kernel,
        [four, wide, shape((4 * AREA, D)), shape((4, 8, AREA), F32), info_shape],
        [], [tok], [qkv_weight, gain], [weight, gains, DMAS((2,))], 16,
        flops=2 * 256 * 512 * 1536, out_specs=[VMEM] * 4 + [SMEM],
    )
    tok_lon, hid = lax.optimization_barrier((tok_lon, hid))
    rows = tok_lon.reshape(2, 2, AREA, D)
    odd = lax.axis_index("lat") % 2
    corner_first, corner_second = lat_swaps(
        lax.dynamic_index_in_dim(rows, 1 - odd, 0, False),
        lax.dynamic_index_in_dim(rows, odd, 0, False),
    )
    q_near, kv_near, hid_near, bias_near, info_near = call(
        "near", near_kernel,
        [four, shape((8, AREA, 2 * D)), shape((8 * AREA, D)), shape((8, 8, AREA), F32), info_shape],
        [], [tok_lon, tok_first, tok_second], [qkv_weight, gain], [weight, gains, DMAS((2,))], 20,
        flops=2 * 512 * 512 * 1280, out_specs=[VMEM] * 4 + [SMEM],
    )
    held = 8 if pair else 4
    back = shape((2 if pair else 4, AREA, 2 * D))
    share = shape((2, 2, 64, 2 * D) if pair else (2, 128, 4 * D))
    mixed, gq, own_kv, back_first, back_second, keep, send, *side = call(
        "main", lambda *refs: main_kernel(pair, *refs),
        [four, four, wide, back, back, share, share] + ([] if pair else [wide]),
        [info, info_near],
        [q, q_near, kv, kv_near, hid, hid_near, bias, bias_near, gb, gb_near, corner_first, corner_second],
        [qkv_weight, out_weight, gain],
        [vmem(held, AREA, D), vmem(16, AREA, 2 * D), vmem(16 * AREA, D), vmem(held, AREA, D),
         vmem32(16, 8, AREA), vmem(held, AREA, D), vmem(KEYS, 2 * D), vmem32(16, AREA, 2 * D),
         vmem(16, AREA, 2 * D), vmem(held, AREA, D), vmem(held, AREA, D), vmem(D, 2 * D),
         vmem(D, D), gains, DMAS((13,))],
        40, flops=3 * 16 * 2 * 512 * 256 * 256 + 2 * 1024 * 512 * 1024,
    )
    if pair:
        total = pair_sum(keep, send)
        back_first, back_second = lat_swaps(back_first, back_second)
        total, back_first, back_second = lax.optimization_barrier((total, back_first, back_second))
        sums = pair_spread(total)
        lon_kv = []
        finish = finish_pair_kernel
    else:
        part = gradient_sum(keep, send)
        back_first, back_second = lat_swaps(back_first, back_second)
        one, two = back_first[2:].astype(F32), back_second[2:].astype(F32)
        rows = jnp.stack([jnp.where(odd == 1, one, two), jnp.where(odd == 1, two, one)])
        side_kv = (side[0].reshape(rows.shape).astype(F32) + rows).astype(BF16)
        lon_kv = [lon_return(side_kv.reshape(wide.shape))]
        sums = plane_sum(part)
        finish = finish_rows_kernel
    layer_out, input_grad = call(
        "input", lambda *refs: input_kernel(pair, *refs),
        [shape(tokens_in.shape), shape(tokens_in.shape)], [],
        [own_kv, back_first, back_second, gq, tok, mixed] + lon_kv,
        [cotangent, tokens_in, ocean_mask, qkv_weight, out_weight, gain],
        [vmem(4 * AREA, 2 * D), grid, grid, mask, weight, vmem(D, D), gains, DMAS((6,))],
        24, flops=2 * 256 * 512 * 1536,
    )
    qkv_grad, out_grad, gain_grad = call(
        "finish", finish,
        [shape((128, 3 * D), F32), shape((128, D), F32), shape((1, 128), F32)], [],
        list(sums), [qkv_weight, gain], [vmem(128, 3 * D), gains, DMAS((2,))], 16,
    )
    return layer_out, input_grad, qkv_grad, out_grad, gain_grad.reshape(128)


def solution(mesh):
    placed = (
        P("lev", "lat", "lon", None),
        P("lev", "lat", "lon", None),
        P(),
        P(),
        P(),
        P("lev", "lat", "lon"),
    )
    return jax.shard_map(
        on_device,
        mesh=mesh,
        in_specs=placed,
        out_specs=(
            P("lev", "lat", "lon", None),
            P("lev", "lat", "lon", None),
            P("lev", None),
            P("lev", None),
            P("lev"),
        ),
        check_vma=False,
    )
```

```python
import jax
import jax.numpy as jnp
from jax import lax
from jax.experimental import pallas as pl
from jax.experimental.pallas import tpu as pltpu
from jax.sharding import PartitionSpec as P

HEADS = 8
WIN = 8
AREA = WIN * WIN
D = 512
HEAD_DIM = D // HEADS
GROUP = 256
GROUP_HEADS = GROUP // HEAD_DIM
GROUPS = D // GROUP
KEYS = 8 * AREA
LAND = 1000.0
NEVER = -1e9
FAR = 1e30
F32 = jnp.float32
BF16 = jnp.bfloat16
EXACT = lax.Precision.HIGHEST


def dot(a, b, ca, cb, precision=None):
    return lax.dot_general(
        a, b, (((ca,), (cb,)), ((), ())), preferred_element_type=F32, precision=precision
    )


def iota(shape, dim):
    return lax.broadcasted_iota(jnp.int32, shape, dim)


def window_of(grid, w):
    r, c = divmod(w, 2)
    part = grid[r * WIN : (r + 1) * WIN, c * WIN : (c + 1) * WIN, :]
    return part.reshape(AREA, grid.shape[-1])


def grid_of(windows):
    rows = []
    for r in range(2):
        parts = [windows[2 * r + c].reshape(WIN, WIN, -1) for c in range(2)]
        rows.append(jnp.concatenate(parts, axis=1))
    return jnp.concatenate(rows, axis=0)


def token_mask(mask):
    t = iota((4 * AREA, 2 * WIN), 0)
    lane = iota((4 * AREA, 2 * WIN), 1)
    w, i, j = t // AREA, (t % AREA) // WIN, t % WIN
    pick_row = (lane == WIN * (w // 2) + i).astype(F32)
    pick_col = (lane == WIN * (w % 2) + j).astype(F32)
    rows = dot(pick_row, mask, 1, 0)
    return jnp.sum(rows * pick_col, axis=1, keepdims=True)


def norm_rows(x):
    center = x - jnp.mean(x, axis=-1, keepdims=True)
    spread = jnp.mean(center * center, axis=-1, keepdims=True)
    scaling = lax.rsqrt(spread + 1e-05)
    return center * scaling, scaling


def head_blocks():
    row = iota((GROUP, GROUP), 0) // HEAD_DIM
    col = iota((GROUP, GROUP), 1) // HEAD_DIM
    return (row == col).astype(F32)


def stack_heads(part, blocks):
    return jnp.concatenate([part] * GROUP_HEADS, axis=0) * blocks.astype(part.dtype)


def unstack_heads(full, blocks):
    kept = full * blocks
    return sum(kept[h * AREA : (h + 1) * AREA] for h in range(GROUP_HEADS))


def lanes(g):
    return slice(g * GROUP, (g + 1) * GROUP)


def lat_side(row):
    return (row + lax.axis_index("lat") + 1) % 2


def load(pairs, sems):
    copies = [pltpu.make_async_copy(a, b, sems.at[k]) for k, (a, b) in enumerate(pairs)]
    for copy in copies:
        copy.start()
    return copies


def wait(copies):
    for copy in copies:
        copy.wait()


def prep_kernel(
    x_hbm, mask_hbm, all_ref, first_ref, second_ref, x_ref, mask_ref, sems
):
    copies = load(((mask_hbm, mask_ref), (x_hbm, x_ref)), sems)
    copies[0].wait()
    ocean = token_mask(mask_ref[0].astype(F32))
    copies[1].wait()
    x = x_ref[0].astype(F32)
    parts = []
    for w in range(4):
        part = jnp.where(ocean[w * AREA : (w + 1) * AREA] > 0.5, window_of(x, w), LAND)
        parts.append(part.astype(BF16))
        all_ref[w] = parts[w]
    odd = lax.axis_index("lat") % 2 == 1
    for c in range(2):
        first_ref[c] = jnp.where(odd, parts[c], parts[2 + c])
        second_ref[c] = jnp.where(odd, parts[2 + c], parts[c])


def land_bias(tokens):
    first = (iota((8, D), 1) == 0).astype(BF16)
    picked = dot(first, tokens, 1, 1)[:1]
    return jnp.where(picked > 0.5 * LAND, NEVER, 0.0)


def hidden_of(tokens, gain_ref):
    normed, _ = norm_rows(tokens.astype(F32))
    return (normed * gain_ref[...]).astype(BF16)


def write_block(tokens, wqkv_ref, gain_ref, q_ref, kv_ref, hid_ref, bias_ref, info_ref):
    hidden = hidden_of(tokens, gain_ref)
    hid_ref[: 4 * AREA] = hidden
    projected = dot(hidden, wqkv_ref[...], 1, 0).astype(BF16)
    q_ref[...] = (projected[:, :D] * BF16(HEAD_DIM ** -0.5)).reshape(4, AREA, D)
    kv_ref[:4] = projected[:, D:].reshape(4, AREA, 2 * D)
    row = land_bias(tokens)
    alive = []
    for w in range(4):
        part = row[:, w * AREA : (w + 1) * AREA]
        bias_ref[w] = jnp.broadcast_to(part, (8, AREA))
        alive.append((jnp.max(part) > 0.5 * NEVER).astype(jnp.int32))
        info_ref[1 + w] = alive[w]
    info_ref[0] = jnp.where(
        alive[3] == 0, 3, jnp.where(alive[2] == 0, 2, jnp.where(alive[1] == 0, 1, 0))
    )


def own_kernel(
    tok_ref, cot_hbm, mask_hbm, wqkv_hbm, gain_hbm,
    q_ref, kv_ref, hid_ref, gb_ref, bias_ref, info_ref, cot_ref, mask_ref, wqkv_ref, gain_ref, sems,
):
    pairs = ((mask_hbm, mask_ref), (cot_hbm, cot_ref), (gain_hbm, gain_ref), (wqkv_hbm, wqkv_ref))
    copies = load(pairs, sems)
    wait(copies[:2])
    ocean = token_mask(mask_ref[0].astype(F32))
    cot = cot_ref[0].astype(F32)
    for w in range(4):
        gb_ref[w] = (window_of(cot, w) * ocean[w * AREA : (w + 1) * AREA]).astype(BF16)
    wait(copies[2:])
    tokens = tok_ref[...].reshape(4 * AREA, D)
    write_block(tokens, wqkv_ref, gain_ref, q_ref, kv_ref, hid_ref, bias_ref, info_ref)


def lat_block(first_ref, second_ref, wkv_ref, gain_ref, kv_ref, hid_ref, bias_ref, at):
    lat, lat_count = lax.axis_index("lat"), lax.axis_size("lat")
    odd = lat % 2 == 1
    first_ok = jnp.logical_or(odd, lat < lat_count - 1)
    second_ok = jnp.where(odd, lat_count - 1 - lat, lat) > 0
    parts = [first_ref[0], first_ref[1], second_ref[0], second_ref[1]]
    tokens = jnp.concatenate(parts, axis=0)
    hidden = hidden_of(tokens, gain_ref)
    hid_ref[at * AREA : (at + 4) * AREA] = hidden
    kv_ref[at : at + 4] = dot(hidden, wkv_ref[...], 1, 0).astype(BF16).reshape(4, AREA, 2 * D)
    row = land_bias(tokens)
    for k in range(4):
        part = row[:, k * AREA : (k + 1) * AREA]
        part = jnp.where(first_ok if k < 2 else second_ok, part, NEVER)
        bias_ref[at + k] = jnp.broadcast_to(part, (8, AREA))


def near_kernel(
    lon_ref, first_ref, second_ref, wqkv_hbm, gain_hbm,
    q_ref, kv_ref, hid_ref, bias_ref, info_ref, wqkv_ref, gain_ref, sems,
):
    wait(load(((gain_hbm, gain_ref), (wqkv_hbm, wqkv_ref)), sems))
    tokens = lon_ref[...].reshape(4 * AREA, D)
    write_block(tokens, wqkv_ref, gain_ref, q_ref, kv_ref, hid_ref, bias_ref, info_ref)
    lat_block(first_ref, second_ref, wqkv_ref.at[:, D:], gain_ref, kv_ref, hid_ref, bias_ref, 4)


def main_kernel(
    pair, info_ref, infon_ref, q_own, q_near, kv_own, kv_near, hid_own, hid_near, bias_own,
    bias_near, gb_own, gb_near, first_ref, second_ref, wqkv_hbm, wout_hbm, gain_hbm,
    mixed, gq, dkv, hid, gb, back1_ref, back2_ref, *rest,
):
    q, kv, bias, gm, kcat, acc, wkv_ref, wout_ref, gain_ref, sems = rest[-10:]
    pairs = [
        (gain_hbm, gain_ref), (wqkv_hbm.at[:, D:], wkv_ref), (wout_hbm, wout_ref),
        (gb_own, gb.at[:4]), (q_own, q.at[:4]), (kv_own, kv.at[:4]), (kv_near, kv.at[4:12]),
        (hid_own, hid.at[: 4 * AREA]), (hid_near, hid.at[4 * AREA : 12 * AREA]),
        (bias_own, bias.at[:4]), (bias_near, bias.at[4:12]),
    ]
    if pair:
        pairs += [(q_near, q.at[4:]), (gb_near, gb.at[4:])]
    copies = load(pairs, sems)
    acc[...] = jnp.zeros_like(acc)
    mixed[...] = jnp.zeros_like(mixed)
    gq[...] = jnp.zeros_like(gq)
    blocks = head_blocks()
    wait(copies[:2])
    lat_block(first_ref, second_ref, wkv_ref, gain_ref, kv, hid, bias, 12)
    wait(copies[2:])
    blocks_held = 2 if pair else 1
    held = 4 * blocks_held
    gb_flat = gb[...].reshape(held * AREA, D)
    gm[...] = dot(gb_flat, wout_ref[...], 1, 1).astype(BF16).reshape(gm.shape)

    def window_at(b, slot):
        left_out = jnp.where(b == 0, info_ref[0], infon_ref[0])
        return slot + (slot >= left_out).astype(jnp.int32)

    def step(n, carry):
        b = n // 3
        w = window_at(b, n % 3)

        @pl.when(jnp.where(b == 0, info_ref[1 + w], infon_ref[1 + w]) > 0)
        def _():
            r, c = w // 2, w % 2
            mine, other, side = 4 * b, 4 * (1 - b), 2 * lat_side(r)
            places = [mine + window_at(b, k) for k in range(3)]
            places += [other + 1 - c, other + 3 - c]
            places += [8 + mine + side, 9 + mine + side, 8 + other + side + 1 - c]
            at = mine + w
            for k in range(8):
                kcat[k * AREA : (k + 1) * AREA] = kv[places[k]]
            bias_row = jnp.concatenate([bias[place][:1] for place in places], axis=1)
            spans = [slice(D + g * GROUP, D + (g + 1) * GROUP) for g in range(GROUPS)]
            both = range(GROUPS)
            q_stack = [stack_heads(q[at, :, lanes(g)], blocks) for g in both]
            gm_stack = [stack_heads(gm[at, :, lanes(g)], blocks) for g in both]
            scores = [dot(q_stack[g], kcat[:, lanes(g)], 1, 1) + bias_row for g in both]
            grad_probs = [dot(gm_stack[g], kcat[:, spans[g]], 1, 1) for g in both]
            weights = [jnp.exp(x - jnp.max(x, axis=1, keepdims=True)) for x in scores]
            probs = [x * (1.0 / jnp.sum(x, axis=1, keepdims=True)) for x in weights]
            low = [x.astype(BF16) for x in probs]
            out = [unstack_heads(dot(low[g], kcat[:, spans[g]], 1, 0), blocks).astype(BF16) for g in both]
            delta = [jnp.sum(probs[g] * grad_probs[g], axis=1, keepdims=True) for g in both]
            grad_scores = [(probs[g] * (grad_probs[g] - delta[g])).astype(BF16) for g in both]
            grad = [unstack_heads(dot(grad_scores[g], kcat[:, lanes(g)], 1, 0), blocks) for g in both]
            grad_keys = [dot(grad_scores[g], q_stack[g], 0, 0) for g in both]
            grad_values = [dot(low[g], gm_stack[g], 0, 0) for g in both]
            for g in both:
                mixed[at, :, lanes(g)] = out[g]
                gq[at, :, lanes(g)] = (grad[g] * HEAD_DIM ** -0.5).astype(BF16)
                for k in range(8):
                    rows = slice(k * AREA, (k + 1) * AREA)
                    acc[places[k], :, lanes(g)] += grad_keys[g][rows]
                    acc[places[k], :, spans[g]] += grad_values[g][rows]

        return carry

    lax.fori_loop(0, 3 * blocks_held, step, 0)
    dkv[...] = acc[...].astype(BF16)
    shares = dot(dkv[8 if pair else 4 : 12 if pair else 16].reshape(-1, 2 * D), wkv_ref[...], 1, 1).astype(BF16)
    shares = shares.reshape(-1, AREA, D)
    if pair:
        back1_ref[...] = shares[:2]
        back2_ref[...] = shares[2:4]
    else:
        rest[0][...] = shares[:4]
        for ref, at in ((back1_ref, 4), (back2_ref, 6)):
            ref[:2] = shares[at : at + 2]
            ref[2:] = shares[at + 4 : at + 6]


def sums_kernel(pair, hid, dkv, gq, mixed, gb, keep, send):
    held = 8 if pair else 4
    gb_flat = gb[...].reshape(held * AREA, D)
    lev = lax.axis_index("lev")

    def columns(rel):
        return pl.ds(pl.multiple_of((lev ^ rel) * 128, 128), 128)

    def hid_part(rel, windows):
        return hid[: windows * AREA, columns(rel)]

    def mix_part(rel):
        return mixed[:, :, columns(rel)].reshape(held * AREA, 128)

    def grad_part(at, width):
        return dkv[:, :, at : at + width].reshape(16 * AREA, width)

    gq_flat = gq[...].reshape(held * AREA, D)
    if pair:
        odd, lon = lax.axis_index("lat") % 2, lax.axis_index("lon")

        def put(rel, at, value):
            to = keep if rel % 2 == 0 else send
            value = value.astype(BF16)
            for k in range(2):
                to[rel // 2, k ^ odd, :, at : at + D] = value[k * 64 : (k + 1) * 64]

        @pl.when(lon == 0)
        def _():
            for rel in range(4):
                put(rel, 0, dot(hid_part(rel, 8), gq_flat, 0, 0))
                put(rel, D, dot(mix_part(rel), gb_flat, 0, 0))

        @pl.when(lon == 1)
        def _():
            for rel in range(4):
                part = hid_part(rel, 16)
                put(rel, 0, dot(part, grad_part(0, D), 0, 0))
                put(rel, D, dot(part, grad_part(D, D), 0, 0))
    else:
        for rel in range(4):
            to = keep if rel % 2 == 0 else send
            to[rel // 2, :, :D] = dot(hid_part(rel, 4), gq_flat, 0, 0).astype(BF16)
            to[rel // 2, :, D : 2 * D] = dot(mix_part(rel), gb_flat, 0, 0).astype(BF16)
            to[rel // 2, :, 2 * D :] = dot(hid_part(rel, 16), grad_part(0, 2 * D), 0, 0).astype(BF16)


def split_kernel(keep_ref, come_ref, own_ref, lev_ref, lat_ref, far_ref):
    for k, ref in enumerate((own_ref, lat_ref, lev_ref, far_ref)):
        total = keep_ref[k // 2, k % 2].astype(F32) + come_ref[k // 2, k % 2].astype(F32)
        ref[...] = total.astype(ref.dtype)


def input_kernel(pair, dkv, back1_ref, back2_ref, gq, tok_ref, mixed, *rest):
    refs = rest if pair else rest[1:]
    cot_hbm, x_hbm, mask_hbm, wqkv_hbm, wout_hbm, gain_hbm, out_ref, ing_ref = refs[:8]
    cot_ref, x_ref, mask_ref, wqkv_ref, wout_ref, gain_ref, sems = refs[8:]
    pairs = (
        (x_hbm, x_ref), (mask_hbm, mask_ref), (wout_hbm, wout_ref), (gain_hbm, gain_ref),
        (wqkv_hbm, wqkv_ref), (cot_hbm, cot_ref),
    )
    copies = load(pairs, sems)
    odd = lax.axis_index("lat") % 2 == 1
    shares = []
    for w in range(4):
        one, two = back1_ref[w % 2].astype(F32), back2_ref[w % 2].astype(F32)
        share = jnp.where(odd, one, two) if w < 2 else jnp.where(odd, two, one)
        shares.append(share if pair else share + rest[0][w].astype(F32))
    normed, scaling = norm_rows(tok_ref[...].reshape(4 * AREA, D).astype(F32))
    wait(copies)
    ocean = token_mask(mask_ref[0].astype(F32))
    added = (dot(mixed[:4].reshape(4 * AREA, D), wout_ref[...], 1, 0) * ocean).reshape(4, AREA, D)
    out_ref[0] = (x_ref[0].astype(F32) + grid_of([added[w] for w in range(4)])).astype(BF16)
    grad_hidden = jnp.concatenate(shares, axis=0)
    grad_hidden = grad_hidden + dot(gq[:4].reshape(4 * AREA, D), wqkv_ref[:, :D], 1, 1)
    grad_hidden = grad_hidden + dot(dkv[:4].reshape(4 * AREA, 2 * D), wqkv_ref[:, D:], 1, 1)
    scaled = grad_hidden * gain_ref[...]
    correction = (
        scaled
        - jnp.mean(scaled, axis=-1, keepdims=True)
        - normed * jnp.mean(scaled * normed, axis=-1, keepdims=True)
    )
    added = (scaling * correction).reshape(4, AREA, D)
    ing_ref[0] = (cot_ref[0].astype(F32) + grid_of([added[w] for w in range(4)])).astype(BF16)


def gain_row(rows_ref, gain_ref, qkv_ref):
    at = pl.ds(pl.multiple_of(lax.axis_index("lev") * 128, 128), 128)
    product = rows_ref[...].astype(F32) * qkv_ref[...]
    return dot(jnp.ones((8, 3 * D), F32), product, 1, 1, EXACT)[:1] / gain_ref[:, at]


def load_rows(wqkv_hbm, rows_ref, gain_hbm, gain_ref, sems):
    at = pl.ds(pl.multiple_of(lax.axis_index("lev") * 128, 128), 128)
    return load(((wqkv_hbm.at[at, :], rows_ref), (gain_hbm, gain_ref)), sems)


def finish_rows_kernel(
    own_ref, far_ref, wqkv_hbm, gain_hbm, qkv_ref, out_ref, gg_ref, rows_ref, gain_ref, sems
):
    copies = load_rows(wqkv_hbm, rows_ref, gain_hbm, gain_ref, sems)
    half = own_ref.shape[0]
    first = lax.axis_index("lon") % 2 == 0
    own, far = own_ref[...], far_ref[...]
    for k in range(2):
        value = (jnp.where(first, own, far) if k == 0 else jnp.where(first, far, own)).astype(F32)
        rows = slice(k * half, (k + 1) * half)
        qkv_ref[rows, :D] = value[:, :D]
        qkv_ref[rows, D:] = value[:, 2 * D :]
        out_ref[rows] = value[:, D : 2 * D]
    wait(copies)
    gg_ref[...] = gain_row(rows_ref, gain_ref, qkv_ref)


def finish_pair_kernel(
    own_ref, lat_ref, lon_ref, far_ref, wqkv_hbm, gain_hbm, qkv_ref, out_ref, gg_ref,
    rows_ref, gain_ref, sems,
):
    copies = load_rows(wqkv_hbm, rows_ref, gain_hbm, gain_ref, sems)
    odd = lax.axis_index("lat") % 2 == 1
    first = lax.axis_index("lon") == 0
    for k in range(2):
        rows = slice(64 * k, 64 * k + 64)
        mine = odd if k == 1 else jnp.logical_not(odd)
        near = jnp.where(mine, own_ref[...], lat_ref[...]).astype(F32)
        away = jnp.where(mine, lon_ref[...], far_ref[...]).astype(F32)
        low, high = jnp.where(first, near, away), jnp.where(first, away, near)
        qkv_ref[rows, :D] = low[:, :D]
        out_ref[rows] = low[:, D:]
        qkv_ref[rows, D:] = high
    wait(copies)
    gg_ref[...] = gain_row(rows_ref, gain_ref, qkv_ref)


SMEM = pl.BlockSpec(memory_space=pltpu.SMEM)
VMEM = pl.BlockSpec(memory_space=pltpu.VMEM)
ANY = pl.BlockSpec(memory_space=pl.ANY)
DMAS = pltpu.SemaphoreType.DMA


def call(name, kernel, outs, scalars, arrays, far, scratch, mebibytes, flops=0, out_specs=None):
    moved = sum(a.size * a.dtype.itemsize for a in (*arrays, *far, *outs))
    return pl.pallas_call(
        kernel,
        out_shape=outs,
        in_specs=[SMEM] * len(scalars) + [VMEM] * len(arrays) + [ANY] * len(far),
        out_specs=out_specs or [VMEM] * len(outs),
        scratch_shapes=list(scratch),
        compiler_params=pltpu.CompilerParams(vmem_limit_bytes=mebibytes * 1024 * 1024),
        cost_estimate=pl.CostEstimate(flops=flops, bytes_accessed=moved, transcendentals=0),
        name=name,
    )(*scalars, *arrays, *far)


def shape(dims, dtype=BF16):
    return jax.ShapeDtypeStruct(dims, dtype)


def ring(count, step, periodic):
    return [
        (i, (i + step) % count) for i in range(count) if periodic or 0 <= i + step < count
    ]


def lon_halo(own):
    count = lax.axis_size("lon")
    if count == 2:
        return lax.ppermute(own, "lon", [(0, 1), (1, 0)])
    left = lax.ppermute(own[1::2], "lon", ring(count, 1, True))
    right = lax.ppermute(own[0::2], "lon", ring(count, -1, True))
    return jnp.stack([right, left], axis=1).reshape(own.shape)


def lon_return(side):
    count = lax.axis_size("lon")
    if count == 2:
        return lax.ppermute(side, "lon", [(0, 1), (1, 0)])
    from_left = lax.ppermute(side[0::2], "lon", ring(count, 1, True))
    from_right = lax.ppermute(side[1::2], "lon", ring(count, -1, True))
    return jnp.stack([from_left, from_right], axis=1).reshape(side.shape)


def lat_swaps(first, second):
    count = lax.axis_size("lat")
    swaps = []
    for start, value in ((0, first), (1, second)):
        pairs = [(i, i + 1) for i in range(start, count - 1, 2)]
        swaps.append(lax.ppermute(value, "lat", pairs + [(b, a) for a, b in pairs]))
    return swaps


def swap(value, axis, bit):
    return lax.ppermute(value, axis, [(i, i ^ bit) for i in range(lax.axis_size(axis))])


def halve(parts, axis, bit):
    at = (lax.axis_index(axis) // bit) % 2
    sent = lax.dynamic_index_in_dim(parts, 1 - at, 0, False).astype(BF16)
    kept = lax.dynamic_index_in_dim(parts, at, 0, False)
    return kept + swap(sent, axis, bit).astype(F32)


def rejoin(half, axis, bit):
    first = (lax.axis_index(axis) // bit) % 2 == 0
    far = swap(half, axis, bit)
    return jnp.concatenate([jnp.where(first, half, far), jnp.where(first, far, half)], axis=0)


def bits(axis):
    count = lax.axis_size(axis)
    return [1 << k for k in range(count.bit_length() - 1)]


def gradient_sum(keep, send):
    width = keep.shape[2] // 2
    total = keep.astype(F32) + swap(send, "lev", 1).astype(F32)
    part_a = total[0, :, :width] + swap(total[1, :, :width].astype(BF16), "lev", 2).astype(F32)
    part_b = total[:, :, width:]
    for bit in bits("lon"):
        rows = part_a.shape[0] // 2
        part_a = halve(part_a.reshape(2, rows, width), "lon", bit)
        part_b = halve(jnp.swapaxes(part_b.reshape(2, 2, rows, width), 0, 1), "lon", bit)
    part_b = part_b[0] + swap(part_b[1].astype(BF16), "lev", 2).astype(F32)
    return jnp.concatenate([part_a, part_b], axis=1)


def plane_sum(part):
    for bit in bits("lat"):
        part = halve(part.reshape(2, part.shape[0] // 2, -1), "lat", bit)
    part = part.astype(BF16)
    for bit in reversed(bits("lat")):
        part = rejoin(part, "lat", bit)
    for bit in reversed(bits("lon")[1:]):
        part = rejoin(part, "lon", bit)
    return part, swap(part, "lon", 1)


def pair_sum(keep, send):
    count = lax.axis_size("lat")
    width = keep.shape[-1]
    come = swap(send, "lev", 1)
    piece = shape(keep.shape[2:])
    own, to_lev, to_lat, to_far = call(
        "split", split_kernel, [shape(piece.shape, F32), piece, piece, piece], [], [keep, come], [], [], 8
    )
    from_far = lax.ppermute(to_far, ("lat", "lev"), [(i, i ^ 6) for i in range(4 * count)])
    from_lat = swap(to_lat, "lat", 1)
    from_lev = swap(to_lev, "lev", 2)
    own = own + from_lev.astype(F32) + from_lat.astype(F32) + from_far.astype(F32)
    return own.astype(BF16)


def pair_spread(own):
    for bit in bits("lat")[1:]:
        own = (own.astype(F32) + swap(own, "lat", bit).astype(F32)).astype(BF16)
    count = lax.axis_size("lat")
    by_far = lax.ppermute(own, ("lon", "lat"), [(i, i ^ (count + 1)) for i in range(2 * count)])
    return own, swap(own, "lat", 1), swap(own, "lon", 1), by_far


def on_device(tokens_in, cotangent, qkv_weight, out_weight, norm_gain, ocean_mask):
    pair = lax.axis_size("lon") == 2
    gain = norm_gain.reshape(1, D)
    half = shape((2, AREA, D))
    four = shape((4, AREA, D))
    wide = shape((4, AREA, 2 * D))
    info_shape = shape((8,), jnp.int32)
    vmem = lambda *dims: pltpu.VMEM(dims, BF16)
    vmem32 = lambda *dims: pltpu.VMEM(dims, F32)
    grid = vmem(*tokens_in.shape)
    mask = pltpu.VMEM(ocean_mask.shape, jnp.int32)
    weight, gains = vmem(*qkv_weight.shape), vmem32(1, D)
    tok, tok_first, tok_second = call(
        "prep", prep_kernel, [four, half, half], [], [], [tokens_in, ocean_mask],
        [grid, mask, DMAS((2,))], 8,
    )
    tok_lon = lon_halo(tok)
    tok_first, tok_second = lat_swaps(tok_first, tok_second)
    q, kv, hid, gb, bias, info = call(
        "own", own_kernel,
        [four, wide, shape((4 * AREA, D)), four, shape((4, 8, AREA), F32), info_shape],
        [], [tok], [cotangent, ocean_mask, qkv_weight, gain], [grid, mask, weight, gains, DMAS((4,))], 16,
        flops=2 * 256 * 512 * 1536, out_specs=[VMEM] * 5 + [SMEM],
    )
    tok_lon, tok_first, tok_second, gb = lax.optimization_barrier((tok_lon, tok_first, tok_second, gb))
    rows = tok_lon.reshape(2, 2, AREA, D)
    odd = lax.axis_index("lat") % 2
    corner_first, corner_second = lat_swaps(
        lax.dynamic_index_in_dim(rows, 1 - odd, 0, False),
        lax.dynamic_index_in_dim(rows, odd, 0, False),
    )
    gb_near = lon_halo(gb) if pair else gb
    q_near, kv_near, hid_near, bias_near, info_near = call(
        "near", near_kernel,
        [four, shape((8, AREA, 2 * D)), shape((8 * AREA, D)), shape((8, 8, AREA), F32), info_shape],
        [], [tok_lon, tok_first, tok_second], [qkv_weight, gain], [weight, gains, DMAS((2,))], 20,
        flops=2 * 512 * 512 * 1280, out_specs=[VMEM] * 4 + [SMEM],
    )
    held = 8 if pair else 4
    back = shape((2 if pair else 4, AREA, D))
    held_shape, all_shape = shape((held, AREA, D)), shape((16, AREA, 2 * D))
    mixed, gq, dkv, hid_all, gb_all, back_first, back_second, *side = call(
        "main", lambda *refs: main_kernel(pair, *refs),
        [held_shape, held_shape, all_shape, shape((16 * AREA, D)), held_shape, back, back]
        + ([] if pair else [four]),
        [info, info_near],
        [q, q_near, kv, kv_near, hid, hid_near, bias, bias_near, gb, gb_near, corner_first, corner_second],
        [qkv_weight, out_weight, gain],
        [vmem(held, AREA, D), vmem(16, AREA, 2 * D), vmem32(16, 8, AREA), vmem(held, AREA, D),
         vmem(KEYS, 2 * D), vmem32(16, AREA, 2 * D), vmem(D, 2 * D), vmem(D, D), gains, DMAS((13,))],
        36, flops=3 * 16 * 2 * 512 * 256 * 256,
    )
    back_first, back_second = lat_swaps(back_first, back_second)
    share = shape((2, 2, 64, 2 * D) if pair else (2, 128, 4 * D))
    keep, send = call(
        "sums", lambda *refs: sums_kernel(pair, *refs), [share, share], [],
        [hid_all, dkv, gq, mixed, gb_all], [], [], 24, flops=2 * 1024 * 512 * 1024,
    )
    if pair:
        total = pair_sum(keep, send)
        total, back_first, back_second = lax.optimization_barrier((total, back_first, back_second))
        sums = pair_spread(total)
        lon_share = []
        finish = finish_pair_kernel
    else:
        part = gradient_sum(keep, send)
        one, two = back_first[2:].astype(F32), back_second[2:].astype(F32)
        rows = jnp.stack([jnp.where(odd == 1, one, two), jnp.where(odd == 1, two, one)])
        side = (side[0].reshape(rows.shape).astype(F32) + rows).astype(BF16)
        lon_share = [lon_return(side.reshape(four.shape))]
        sums = plane_sum(part)
        finish = finish_rows_kernel
    layer_out, input_grad = call(
        "input", lambda *refs: input_kernel(pair, *refs),
        [shape(tokens_in.shape), shape(tokens_in.shape)], [],
        [dkv, back_first, back_second, gq, tok, mixed] + lon_share,
        [cotangent, tokens_in, ocean_mask, qkv_weight, out_weight, gain],
        [grid, grid, mask, weight, vmem(D, D), gains, DMAS((6,))],
        24, flops=2 * 256 * 512 * 1536,
    )
    qkv_grad, out_grad, gain_grad = call(
        "finish", finish,
        [shape((128, 3 * D), F32), shape((128, D), F32), shape((1, 128), F32)], [],
        list(sums), [qkv_weight, gain], [vmem(128, 3 * D), gains, DMAS((2,))], 16,
    )
    return layer_out, input_grad, qkv_grad, out_grad, gain_grad.reshape(128)


def solution(mesh):
    placed = (
        P("lev", "lat", "lon", None),
        P("lev", "lat", "lon", None),
        P(),
        P(),
        P(),
        P("lev", "lat", "lon"),
    )
    return jax.shard_map(
        on_device,
        mesh=mesh,
        in_specs=placed,
        out_specs=(
            P("lev", "lat", "lon", None),
            P("lev", "lat", "lon", None),
            P("lev", None),
            P("lev", None),
            P("lev"),
        ),
        check_vma=False,
    )
```

```python
import jax
import jax.numpy as jnp
from jax import lax
from jax.experimental import pallas as pl
from jax.experimental.pallas import tpu as pltpu
from jax.sharding import PartitionSpec as P

HEADS = 8
WIN = 8
AREA = WIN * WIN
D = 512
HEAD_DIM = D // HEADS
GROUP = 256
GROUP_HEADS = GROUP // HEAD_DIM
GROUPS = D // GROUP
KEYS = 8 * AREA
LAND = 1000.0
NEVER = -1e9
FAR = 1e30
F32 = jnp.float32
BF16 = jnp.bfloat16
EXACT = lax.Precision.HIGHEST


def dot(a, b, ca, cb, precision=None):
    return lax.dot_general(
        a, b, (((ca,), (cb,)), ((), ())), preferred_element_type=F32, precision=precision
    )


def iota(shape, dim):
    return lax.broadcasted_iota(jnp.int32, shape, dim)


def window_of(grid, w):
    r, c = divmod(w, 2)
    part = grid[r * WIN : (r + 1) * WIN, c * WIN : (c + 1) * WIN, :]
    return part.reshape(AREA, grid.shape[-1])


def grid_of(windows):
    rows = []
    for r in range(2):
        parts = [windows[2 * r + c].reshape(WIN, WIN, -1) for c in range(2)]
        rows.append(jnp.concatenate(parts, axis=1))
    return jnp.concatenate(rows, axis=0)


def token_mask(mask):
    t = iota((4 * AREA, 2 * WIN), 0)
    lane = iota((4 * AREA, 2 * WIN), 1)
    w, i, j = t // AREA, (t % AREA) // WIN, t % WIN
    pick_row = (lane == WIN * (w // 2) + i).astype(F32)
    pick_col = (lane == WIN * (w % 2) + j).astype(F32)
    rows = dot(pick_row, mask, 1, 0)
    return jnp.sum(rows * pick_col, axis=1, keepdims=True)


def norm_rows(x):
    center = x - jnp.mean(x, axis=-1, keepdims=True)
    spread = jnp.mean(center * center, axis=-1, keepdims=True)
    scaling = lax.rsqrt(spread + 1e-05)
    return center * scaling, scaling


def head_blocks():
    row = iota((GROUP, GROUP), 0) // HEAD_DIM
    col = iota((GROUP, GROUP), 1) // HEAD_DIM
    return (row == col).astype(F32)


def stack_heads(part, blocks):
    return jnp.concatenate([part] * GROUP_HEADS, axis=0) * blocks.astype(part.dtype)


def unstack_heads(full, blocks):
    kept = full * blocks
    return sum(kept[h * AREA : (h + 1) * AREA] for h in range(GROUP_HEADS))


def lanes(g):
    return slice(g * GROUP, (g + 1) * GROUP)


def lat_side(row):
    return (row + lax.axis_index("lat") + 1) % 2


def load(pairs, sems):
    copies = [pltpu.make_async_copy(a, b, sems.at[k]) for k, (a, b) in enumerate(pairs)]
    for copy in copies:
        copy.start()
    return copies


def wait(copies):
    for copy in copies:
        copy.wait()


def prep_kernel(
    x_hbm, mask_hbm, all_ref, first_ref, second_ref, x_ref, mask_ref, sems
):
    copies = load(((mask_hbm, mask_ref), (x_hbm, x_ref)), sems)
    copies[0].wait()
    ocean = token_mask(mask_ref[0].astype(F32))
    copies[1].wait()
    x = x_ref[0].astype(F32)
    parts = []
    for w in range(4):
        part = jnp.where(ocean[w * AREA : (w + 1) * AREA] > 0.5, window_of(x, w), LAND)
        parts.append(part.astype(BF16))
        all_ref[w] = parts[w]
    odd = lax.axis_index("lat") % 2 == 1
    for c in range(2):
        first_ref[c] = jnp.where(odd, parts[c], parts[2 + c])
        second_ref[c] = jnp.where(odd, parts[2 + c], parts[c])


def land_bias(tokens):
    first = (iota((8, D), 1) == 0).astype(BF16)
    picked = dot(first, tokens, 1, 1)[:1]
    return jnp.where(picked > 0.5 * LAND, NEVER, 0.0)


def hidden_of(tokens, gain_ref):
    normed, _ = norm_rows(tokens.astype(F32))
    return (normed * gain_ref[...]).astype(BF16)


def write_block(tokens, wqkv_ref, gain_ref, q_ref, kv_ref, hid_ref, bias_ref, info_ref):
    hidden = hidden_of(tokens, gain_ref)
    hid_ref[: 4 * AREA] = hidden
    projected = dot(hidden, wqkv_ref[...], 1, 0).astype(BF16)
    q_ref[...] = (projected[:, :D] * BF16(HEAD_DIM ** -0.5)).reshape(4, AREA, D)
    kv_ref[:4] = projected[:, D:].reshape(4, AREA, 2 * D)
    row = land_bias(tokens)
    alive = []
    for w in range(4):
        part = row[:, w * AREA : (w + 1) * AREA]
        bias_ref[w] = jnp.broadcast_to(part, (8, AREA))
        alive.append((jnp.max(part) > 0.5 * NEVER).astype(jnp.int32))
        info_ref[1 + w] = alive[w]
    info_ref[0] = jnp.where(
        alive[3] == 0, 3, jnp.where(alive[2] == 0, 2, jnp.where(alive[1] == 0, 1, 0))
    )


def own_kernel(
    tok_ref, cot_hbm, mask_hbm, wqkv_hbm, wout_hbm, gain_hbm,
    q_ref, kv_ref, hid_ref, gb_ref, bias_ref, wqkv_ref, wout_ref, gain_ref, info_ref,
    cot_ref, mask_ref, sems,
):
    pairs = (
        (mask_hbm, mask_ref), (cot_hbm, cot_ref), (gain_hbm, gain_ref), (wqkv_hbm, wqkv_ref),
        (wout_hbm, wout_ref),
    )
    copies = load(pairs, sems)
    wait(copies[:2])
    ocean = token_mask(mask_ref[0].astype(F32))
    cot = cot_ref[0].astype(F32)
    for w in range(4):
        gb_ref[w] = (window_of(cot, w) * ocean[w * AREA : (w + 1) * AREA]).astype(BF16)
    wait(copies[2:4])
    tokens = tok_ref[...].reshape(4 * AREA, D)
    write_block(tokens, wqkv_ref, gain_ref, q_ref, kv_ref, hid_ref, bias_ref, info_ref)
    wait(copies[4:])


def lat_block(first_ref, second_ref, wkv_ref, gain_ref, kv_ref, hid_ref, bias_ref, at):
    lat, lat_count = lax.axis_index("lat"), lax.axis_size("lat")
    odd = lat % 2 == 1
    first_ok = jnp.logical_or(odd, lat < lat_count - 1)
    second_ok = jnp.where(odd, lat_count - 1 - lat, lat) > 0
    parts = [first_ref[0], first_ref[1], second_ref[0], second_ref[1]]
    tokens = jnp.concatenate(parts, axis=0)
    hidden = hidden_of(tokens, gain_ref)
    hid_ref[at * AREA : (at + 4) * AREA] = hidden
    kv_ref[at : at + 4] = dot(hidden, wkv_ref[...], 1, 0).astype(BF16).reshape(4, AREA, 2 * D)
    row = land_bias(tokens)
    for k in range(4):
        part = row[:, k * AREA : (k + 1) * AREA]
        part = jnp.where(first_ok if k < 2 else second_ok, part, NEVER)
        bias_ref[at + k] = jnp.broadcast_to(part, (8, AREA))


def near_kernel(
    lon_ref, first_ref, second_ref, wqkv_ref, gain_ref, q_ref, kv_ref, hid_ref, bias_ref, info_ref
):
    tokens = lon_ref[...].reshape(4 * AREA, D)
    write_block(tokens, wqkv_ref, gain_ref, q_ref, kv_ref, hid_ref, bias_ref, info_ref)
    lat_block(first_ref, second_ref, wqkv_ref.at[:, D:], gain_ref, kv_ref, hid_ref, bias_ref, 4)


def main_kernel(block, last, *refs):
    refs = list(refs)
    take = lambda n: [refs.pop(0) for _ in range(n)]
    info_ref, infon_ref = take(2)
    wqkv_ref, wout_ref, gain_ref, q, gb = take(5)
    if block == 0:
        first_ref, second_ref, kv_own, kv_near, hid_own, hid_near, bias_own, bias_near = take(8)
    else:
        kv, bias, _ = take(3)
    acc, mixed, gq = take(3)
    if block == 0:
        hid, kv, bias = take(3)
    if last:
        dkv, back1_ref, back2_ref = take(3)
        side_ref = None if block else take(1)[0]
    gm, kcat, *sems = refs
    wkv_ref = wqkv_ref.at[:, D:]
    if block == 0:
        pairs = (
            (kv_own, kv.at[:4]), (kv_near, kv.at[4:12]),
            (hid_own, hid.at[: 4 * AREA]), (hid_near, hid.at[4 * AREA : 12 * AREA]),
            (bias_own, bias.at[:4]), (bias_near, bias.at[4:12]),
        )
        copies = load(pairs, sems[0])
        acc[...] = jnp.zeros_like(acc)
        lat_block(first_ref, second_ref, wkv_ref, gain_ref, kv, hid, bias, 12)
        wait(copies)
    mixed[...] = jnp.zeros_like(mixed)
    gq[...] = jnp.zeros_like(gq)
    blocks = head_blocks()
    gm[...] = dot(gb[...].reshape(4 * AREA, D), wout_ref[...], 1, 1).astype(BF16).reshape(gm.shape)
    info = infon_ref if block else info_ref

    def window_at(slot):
        return slot + (slot >= info[0]).astype(jnp.int32)

    def step(slot, carry):
        at = window_at(slot)

        @pl.when(info[1 + at] > 0)
        def _():
            r, c = at // 2, at % 2
            mine, other, side = 4 * block, 4 * (1 - block), 2 * lat_side(r)
            places = [mine + window_at(k) for k in range(3)]
            places += [other + 1 - c, other + 3 - c]
            places += [8 + mine + side, 9 + mine + side, 8 + other + side + 1 - c]
            for k in range(8):
                kcat[k * AREA : (k + 1) * AREA] = kv[places[k]]
            bias_row = jnp.concatenate([bias[place][:1] for place in places], axis=1)
            spans = [slice(D + g * GROUP, D + (g + 1) * GROUP) for g in range(GROUPS)]
            both = range(GROUPS)
            q_stack = [stack_heads(q[at, :, lanes(g)], blocks) for g in both]
            gm_stack = [stack_heads(gm[at, :, lanes(g)], blocks) for g in both]
            scores = [dot(q_stack[g], kcat[:, lanes(g)], 1, 1) + bias_row for g in both]
            grad_probs = [dot(gm_stack[g], kcat[:, spans[g]], 1, 1) for g in both]
            weights = [jnp.exp(x - jnp.max(x, axis=1, keepdims=True)) for x in scores]
            probs = [x * (1.0 / jnp.sum(x, axis=1, keepdims=True)) for x in weights]
            low = [x.astype(BF16) for x in probs]
            out = [unstack_heads(dot(low[g], kcat[:, spans[g]], 1, 0), blocks).astype(BF16) for g in both]
            delta = [jnp.sum(probs[g] * grad_probs[g], axis=1, keepdims=True) for g in both]
            grad_scores = [(probs[g] * (grad_probs[g] - delta[g])).astype(BF16) for g in both]
            grad = [unstack_heads(dot(grad_scores[g], kcat[:, lanes(g)], 1, 0), blocks) for g in both]
            grad_keys = [dot(grad_scores[g], q_stack[g], 0, 0) for g in both]
            grad_values = [dot(low[g], gm_stack[g], 0, 0) for g in both]
            for g in both:
                mixed[at, :, lanes(g)] = out[g]
                gq[at, :, lanes(g)] = (grad[g] * HEAD_DIM ** -0.5).astype(BF16)
                for k in range(8):
                    rows = slice(k * AREA, (k + 1) * AREA)
                    acc[places[k], :, lanes(g)] += grad_keys[g][rows]
                    acc[places[k], :, spans[g]] += grad_values[g][rows]

        return carry

    lax.fori_loop(0, 3, step, 0)
    if not last:
        return
    dkv[...] = acc[...].astype(BF16)
    near = dkv[8:12] if block else dkv[4:]
    shares = dot(near.reshape(-1, 2 * D), wkv_ref[...], 1, 1).astype(BF16).reshape(-1, AREA, D)
    if block:
        back1_ref[...] = shares[:2]
        back2_ref[...] = shares[2:4]
    else:
        side_ref[...] = shares[:4]
        for ref, at in ((back1_ref, 4), (back2_ref, 6)):
            ref[:2] = shares[at : at + 2]
            ref[2:] = shares[at + 4 : at + 6]


def sums_kernel(pair, hid, dkv, *refs):
    held = [refs[k : k + 3] for k in range(0, len(refs) - 2, 3)]
    keep, send = refs[-2:]
    flat = lambda ref: ref[...].reshape(4 * AREA, D)
    lev = lax.axis_index("lev")

    def columns(rel):
        return pl.ds(pl.multiple_of((lev ^ rel) * 128, 128), 128)

    def grad_part(at, width):
        return dkv[:, :, at : at + width].reshape(16 * AREA, width)

    def query_sum(rel):
        parts = [
            dot(hid[4 * b * AREA : 4 * (b + 1) * AREA, columns(rel)], flat(gq), 0, 0)
            for b, (gq, _, _) in enumerate(held)
        ]
        return sum(parts[1:], parts[0])

    def out_sum(rel):
        parts = [
            dot(mixed[:, :, columns(rel)].reshape(4 * AREA, 128), flat(gb), 0, 0) for _, mixed, gb in held
        ]
        return sum(parts[1:], parts[0])

    if pair:
        odd, lon = lax.axis_index("lat") % 2, lax.axis_index("lon")

        def put(rel, at, value):
            to = keep if rel % 2 == 0 else send
            value = value.astype(BF16)
            for k in range(2):
                to[rel // 2, k ^ odd, :, at : at + D] = value[k * 64 : (k + 1) * 64]

        @pl.when(lon == 0)
        def _():
            for rel in range(4):
                put(rel, 0, query_sum(rel))
                put(rel, D, out_sum(rel))

        @pl.when(lon == 1)
        def _():
            for rel in range(4):
                part = hid[:, columns(rel)]
                put(rel, 0, dot(part, grad_part(0, D), 0, 0))
                put(rel, D, dot(part, grad_part(D, D), 0, 0))
    else:
        for rel in range(4):
            to = keep if rel % 2 == 0 else send
            to[rel // 2, :, :D] = query_sum(rel).astype(BF16)
            to[rel // 2, :, D : 2 * D] = out_sum(rel).astype(BF16)
            to[rel // 2, :, 2 * D :] = dot(hid[:, columns(rel)], grad_part(0, 2 * D), 0, 0).astype(BF16)


def split_kernel(keep_ref, come_ref, own_ref, lev_ref, lat_ref, far_ref):
    for k, ref in enumerate((own_ref, lat_ref, lev_ref, far_ref)):
        total = keep_ref[k // 2, k % 2].astype(F32) + come_ref[k // 2, k % 2].astype(F32)
        ref[...] = total.astype(ref.dtype)


def input_kernel(pair, dkv, back1_ref, back2_ref, gq, tok_ref, mixed, *rest):
    refs = rest if pair else rest[1:]
    wqkv_ref, wout_ref, gain_ref, cot_hbm, x_hbm, mask_hbm, out_ref, ing_ref = refs[:8]
    cot_ref, x_ref, mask_ref, sems = refs[8:]
    copies = load(((x_hbm, x_ref), (mask_hbm, mask_ref), (cot_hbm, cot_ref)), sems)
    odd = lax.axis_index("lat") % 2 == 1
    shares = []
    for w in range(4):
        one, two = back1_ref[w % 2].astype(F32), back2_ref[w % 2].astype(F32)
        share = jnp.where(odd, one, two) if w < 2 else jnp.where(odd, two, one)
        shares.append(share if pair else share + rest[0][w].astype(F32))
    normed, scaling = norm_rows(tok_ref[...].reshape(4 * AREA, D).astype(F32))
    wait(copies)
    ocean = token_mask(mask_ref[0].astype(F32))
    added = (dot(mixed[:4].reshape(4 * AREA, D), wout_ref[...], 1, 0) * ocean).reshape(4, AREA, D)
    out_ref[0] = (x_ref[0].astype(F32) + grid_of([added[w] for w in range(4)])).astype(BF16)
    grad_hidden = jnp.concatenate(shares, axis=0)
    grad_hidden = grad_hidden + dot(gq[:4].reshape(4 * AREA, D), wqkv_ref[:, :D], 1, 1)
    grad_hidden = grad_hidden + dot(dkv[:4].reshape(4 * AREA, 2 * D), wqkv_ref[:, D:], 1, 1)
    scaled = grad_hidden * gain_ref[...]
    correction = (
        scaled
        - jnp.mean(scaled, axis=-1, keepdims=True)
        - normed * jnp.mean(scaled * normed, axis=-1, keepdims=True)
    )
    added = (scaling * correction).reshape(4, AREA, D)
    ing_ref[0] = (cot_ref[0].astype(F32) + grid_of([added[w] for w in range(4)])).astype(BF16)


def gain_row(wqkv_ref, gain_ref, qkv_ref):
    at = pl.ds(pl.multiple_of(lax.axis_index("lev") * 128, 128), 128)
    product = wqkv_ref[at, :].astype(F32) * qkv_ref[...]
    return dot(jnp.ones((8, 3 * D), F32), product, 1, 1, EXACT)[:1] / gain_ref[:, at]


def finish_rows_kernel(
    own_ref, far_ref, wqkv_ref, gain_ref, qkv_ref, out_ref, gg_ref
):
    half = own_ref.shape[0]
    first = lax.axis_index("lon") % 2 == 0
    own, far = own_ref[...], far_ref[...]
    for k in range(2):
        value = (jnp.where(first, own, far) if k == 0 else jnp.where(first, far, own)).astype(F32)
        rows = slice(k * half, (k + 1) * half)
        qkv_ref[rows, :D] = value[:, :D]
        qkv_ref[rows, D:] = value[:, 2 * D :]
        out_ref[rows] = value[:, D : 2 * D]
    gg_ref[...] = gain_row(wqkv_ref, gain_ref, qkv_ref)


def finish_pair_kernel(
    own_ref, lat_ref, lon_ref, far_ref, wqkv_ref, gain_ref, qkv_ref, out_ref, gg_ref
):
    odd = lax.axis_index("lat") % 2 == 1
    first = lax.axis_index("lon") == 0
    for k in range(2):
        rows = slice(64 * k, 64 * k + 64)
        mine = odd if k == 1 else jnp.logical_not(odd)
        near = jnp.where(mine, own_ref[...], lat_ref[...]).astype(F32)
        away = jnp.where(mine, lon_ref[...], far_ref[...]).astype(F32)
        low, high = jnp.where(first, near, away), jnp.where(first, away, near)
        qkv_ref[rows, :D] = low[:, :D]
        out_ref[rows] = low[:, D:]
        qkv_ref[rows, D:] = high
    gg_ref[...] = gain_row(wqkv_ref, gain_ref, qkv_ref)


SMEM = pl.BlockSpec(memory_space=pltpu.SMEM)
VMEM = pl.BlockSpec(memory_space=pltpu.VMEM)
ANY = pl.BlockSpec(memory_space=pl.ANY)
HBM = pl.BlockSpec(memory_space=pltpu.HBM)
DMAS = pltpu.SemaphoreType.DMA


def call(
    name, kernel, outs, scalars, arrays, loose, far, scratch, mebibytes, flops=0, out_specs=None, aliases=None
):
    moved = sum(a.size * a.dtype.itemsize for a in (*arrays, *loose, *far, *outs))
    specs = [SMEM] * len(scalars) + [VMEM] * len(arrays) + [ANY] * len(loose) + [HBM] * len(far)
    return pl.pallas_call(
        kernel,
        out_shape=outs,
        in_specs=specs,
        out_specs=out_specs or [VMEM] * len(outs),
        scratch_shapes=list(scratch),
        input_output_aliases=aliases or {},
        compiler_params=pltpu.CompilerParams(vmem_limit_bytes=mebibytes * 1024 * 1024),
        cost_estimate=pl.CostEstimate(flops=flops, bytes_accessed=moved, transcendentals=0),
        name=name,
    )(*scalars, *arrays, *loose, *far)


def shape(dims, dtype=BF16):
    return jax.ShapeDtypeStruct(dims, dtype)


def ring(count, step, periodic):
    return [
        (i, (i + step) % count) for i in range(count) if periodic or 0 <= i + step < count
    ]


def lon_halo(own):
    count = lax.axis_size("lon")
    if count == 2:
        return lax.ppermute(own, "lon", [(0, 1), (1, 0)])
    left = lax.ppermute(own[1::2], "lon", ring(count, 1, True))
    right = lax.ppermute(own[0::2], "lon", ring(count, -1, True))
    return jnp.stack([right, left], axis=1).reshape(own.shape)


def lon_return(side):
    count = lax.axis_size("lon")
    if count == 2:
        return lax.ppermute(side, "lon", [(0, 1), (1, 0)])
    from_left = lax.ppermute(side[0::2], "lon", ring(count, 1, True))
    from_right = lax.ppermute(side[1::2], "lon", ring(count, -1, True))
    return jnp.stack([from_left, from_right], axis=1).reshape(side.shape)


def lat_swap(value, start):
    pairs = [(i, i + 1) for i in range(start, lax.axis_size("lat") - 1, 2)]
    return lax.ppermute(value, "lat", pairs + [(b, a) for a, b in pairs])


def lat_swaps(first, second):
    return lat_swap(first, 0), lat_swap(second, 1)


def corner_swap(value, start):
    count = lax.axis_size("lat")
    pairs = [(i, i + 1) for i in range(start, count - 1, 2)]
    pairs = [(a + k * count, b + (1 - k) * count) for a, b in pairs for k in range(2)]
    return lax.ppermute(value, ("lon", "lat"), pairs + [(b, a) for a, b in pairs])


def swap(value, axis, bit):
    return lax.ppermute(value, axis, [(i, i ^ bit) for i in range(lax.axis_size(axis))])


def halve(parts, axis, bit):
    at = (lax.axis_index(axis) // bit) % 2
    sent = lax.dynamic_index_in_dim(parts, 1 - at, 0, False).astype(BF16)
    kept = lax.dynamic_index_in_dim(parts, at, 0, False)
    return kept + swap(sent, axis, bit).astype(F32)


def rejoin(half, axis, bit):
    first = (lax.axis_index(axis) // bit) % 2 == 0
    far = swap(half, axis, bit)
    return jnp.concatenate([jnp.where(first, half, far), jnp.where(first, far, half)], axis=0)


def bits(axis):
    count = lax.axis_size(axis)
    return [1 << k for k in range(count.bit_length() - 1)]


def gradient_sum(keep, send):
    width = keep.shape[2] // 2
    total = keep.astype(F32) + swap(send, "lev", 1).astype(F32)
    part_a = total[0, :, :width] + swap(total[1, :, :width].astype(BF16), "lev", 2).astype(F32)
    part_b = total[:, :, width:]
    for bit in bits("lon"):
        rows = part_a.shape[0] // 2
        part_a = halve(part_a.reshape(2, rows, width), "lon", bit)
        part_b = halve(jnp.swapaxes(part_b.reshape(2, 2, rows, width), 0, 1), "lon", bit)
    part_b = part_b[0] + swap(part_b[1].astype(BF16), "lev", 2).astype(F32)
    return jnp.concatenate([part_a, part_b], axis=1)


def plane_sum(part):
    for bit in bits("lat"):
        part = halve(part.reshape(2, part.shape[0] // 2, -1), "lat", bit)
    part = part.astype(BF16)
    for bit in reversed(bits("lat")):
        part = rejoin(part, "lat", bit)
    for bit in reversed(bits("lon")[1:]):
        part = rejoin(part, "lon", bit)
    return part, swap(part, "lon", 1)


def pair_sum(keep, send):
    count = lax.axis_size("lat")
    width = keep.shape[-1]
    come = swap(send, "lev", 1)
    piece = shape(keep.shape[2:])
    own, to_lev, to_lat, to_far = call(
        "split", split_kernel, [shape(piece.shape, F32), piece, piece, piece], [], [keep, come], [], [], [], 8
    )
    from_far = lax.ppermute(to_far, ("lat", "lev"), [(i, i ^ 6) for i in range(4 * count)])
    from_lat = swap(to_lat, "lat", 1)
    from_lev = swap(to_lev, "lev", 2)
    own = own + from_lev.astype(F32) + from_lat.astype(F32) + from_far.astype(F32)
    return own.astype(BF16)


def lat_sum(own):
    for bit in bits("lat")[1:]:
        own = (own.astype(F32) + swap(own, "lat", bit).astype(F32)).astype(BF16)
    return own


def pair_spread(own):
    count = lax.axis_size("lat")
    by_far = lax.ppermute(own, ("lon", "lat"), [(i, i ^ (count + 1)) for i in range(2 * count)])
    return own, swap(own, "lat", 1), swap(own, "lon", 1), by_far


def on_device(tokens_in, cotangent, qkv_weight, out_weight, norm_gain, ocean_mask):
    pair = lax.axis_size("lon") == 2
    gain = norm_gain.reshape(1, D)
    half = shape((2, AREA, D))
    four = shape((4, AREA, D))
    wide = shape((4, AREA, 2 * D))
    info_shape = shape((8,), jnp.int32)
    vmem = lambda *dims: pltpu.VMEM(dims, BF16)
    grid = vmem(*tokens_in.shape)
    mask = pltpu.VMEM(ocean_mask.shape, jnp.int32)
    tok, tok_first, tok_second = call(
        "prep", prep_kernel, [four, half, half], [], [], [], [tokens_in, ocean_mask],
        [grid, mask, DMAS((2,))], 8, flops=10 ** 10,
    )
    tok_lon = lon_halo(tok)
    odd = lax.axis_index("lat") % 2
    if pair:
        corner_first, corner_second = corner_swap(tok_first, 0), corner_swap(tok_second, 1)
    tok_first, tok_second = lat_swaps(tok_first, tok_second)
    q, kv, hid, gb, bias, wqkv, wout, gain, info = call(
        "own", own_kernel,
        [four, wide, shape((4 * AREA, D)), four, shape((4, 8, AREA), F32), shape(qkv_weight.shape),
         shape(out_weight.shape), shape(gain.shape, F32), info_shape],
        [], [tok], [], [cotangent, ocean_mask, qkv_weight, out_weight, gain], [grid, mask, DMAS((5,))], 16,
        flops=2 * 256 * 512 * 1536, out_specs=[VMEM] * 8 + [SMEM],
    )
    if pair:
        gb_near = lon_halo(gb)
    else:
        rows = tok_lon.reshape(2, 2, AREA, D)
        corner_first, corner_second = lat_swaps(
            lax.dynamic_index_in_dim(rows, 1 - odd, 0, False),
            lax.dynamic_index_in_dim(rows, odd, 0, False),
        )
    q_near, kv_near, hid_near, bias_near, info_near = call(
        "near", near_kernel,
        [four, shape((8, AREA, 2 * D)), shape((8 * AREA, D)), shape((8, 8, AREA), F32), info_shape],
        [], [tok_lon, tok_first, tok_second, wqkv, gain], [], [], [], 20,
        flops=2 * 512 * 512 * 1280, out_specs=[VMEM] * 4 + [SMEM],
    )
    all_shape, all32 = shape((16, AREA, 2 * D)), shape((16, AREA, 2 * D), F32)
    back = shape((2 if pair else 4, AREA, D))
    ends = [all_shape, back, back] + ([] if pair else [four])
    weights = [wqkv, wout, gain]
    scratch = [vmem(4, AREA, D), vmem(KEYS, 2 * D)]
    flops = 3 * 12 * 2 * 512 * 256 * 256
    acc, mixed, gq, hid_all, kv_all, bias_all, *rest = call(
        "main", lambda *refs: main_kernel(0, not pair, *refs),
        [all32, four, four, shape((16 * AREA, D)), all_shape, shape((16, 8, AREA), F32)]
        + ([] if pair else ends),
        [info, info_near], weights + [q, gb, corner_first, corner_second],
        [kv, kv_near, hid, hid_near, bias, bias_near], [], scratch + [DMAS((6,))], 28, flops=flops,
    )
    parts = [gq, mixed, gb]
    if pair:
        _, mixed_near, gq_near, *rest = call(
            "other", lambda *refs: main_kernel(1, True, *refs), [all32, four, four] + ends,
            [info, info_near], weights + [q_near, gb_near, kv_all, bias_all, acc], [], [],
            scratch, 28, flops=flops, aliases={9: 0},
        )
        parts += [gq_near, mixed_near, gb_near]
    dkv, back_first, back_second, *side = rest
    share = shape((2, 2, 64, 2 * D) if pair else (2, 128, 4 * D))
    keep, send = call(
        "sums", lambda *refs: sums_kernel(pair, *refs), [share, share], [],
        [hid_all, dkv] + parts, [], [], [], 24, flops=2 * 1024 * 512 * 1024,
    )
    if pair:
        total = pair_sum(keep, send)
        back_second = lat_swap(back_second, 1)
        total, back_first, back_second = lax.optimization_barrier((total, back_first, back_second))
        back_first = lat_swap(back_first, 0)
        total = lat_sum(total)
        total, back_first = lax.optimization_barrier((total, back_first))
        sums = pair_spread(total)
        lon_share = []
        finish = finish_pair_kernel
    else:
        part = gradient_sum(keep, send)
        back_first, back_second = lat_swaps(back_first, back_second)
        one, two = back_first[2:].astype(F32), back_second[2:].astype(F32)
        rows = jnp.stack([jnp.where(odd == 1, one, two), jnp.where(odd == 1, two, one)])
        side = (side[0].reshape(rows.shape).astype(F32) + rows).astype(BF16)
        lon_share = [lon_return(side.reshape(four.shape))]
        sums = plane_sum(part)
        finish = finish_rows_kernel
    layer_out, input_grad = call(
        "input", lambda *refs: input_kernel(pair, *refs),
        [shape(tokens_in.shape), shape(tokens_in.shape)], [],
        [dkv, back_first, back_second, gq, tok, mixed] + lon_share + weights, [],
        [cotangent, tokens_in, ocean_mask], [grid, grid, mask, DMAS((3,))], 24, flops=2 * 256 * 512 * 1536,
    )
    qkv_grad, out_grad, gain_grad = call(
        "finish", finish,
        [shape((128, 3 * D), F32), shape((128, D), F32), shape((1, 128), F32)], [],
        [*sums, wqkv, gain], [], [], [], 16,
    )
    return layer_out, input_grad, qkv_grad, out_grad, gain_grad.reshape(128)


def solution(mesh):
    placed = (
        P("lev", "lat", "lon", None),
        P("lev", "lat", "lon", None),
        P(),
        P(),
        P(),
        P("lev", "lat", "lon"),
    )
    return jax.shard_map(
        on_device,
        mesh=mesh,
        in_specs=placed,
        out_specs=(
            P("lev", "lat", "lon", None),
            P("lev", "lat", "lon", None),
            P("lev", None),
            P("lev", None),
            P("lev"),
        ),
        check_vma=False,
    )
```

```python
import jax
import jax.numpy as jnp
from jax import lax
from jax.experimental import pallas as pl
from jax.experimental.pallas import tpu as pltpu
from jax.sharding import PartitionSpec as P

HEADS = 8
WIN = 8
AREA = WIN * WIN
D = 512
HEAD_DIM = D // HEADS
GROUP = 256
GROUP_HEADS = GROUP // HEAD_DIM
GROUPS = D // GROUP
KEYS = 8 * AREA
LAND = 1000.0
NEVER = -1e9
FAR = 1e30
F32 = jnp.float32
BF16 = jnp.bfloat16
EXACT = lax.Precision.HIGHEST


def dot(a, b, ca, cb, precision=None):
    return lax.dot_general(
        a, b, (((ca,), (cb,)), ((), ())), preferred_element_type=F32, precision=precision
    )


def iota(shape, dim):
    return lax.broadcasted_iota(jnp.int32, shape, dim)


def window_of(grid, w):
    r, c = divmod(w, 2)
    part = grid[r * WIN : (r + 1) * WIN, c * WIN : (c + 1) * WIN, :]
    return part.reshape(AREA, grid.shape[-1])


def grid_of(windows):
    rows = []
    for r in range(2):
        parts = [windows[2 * r + c].reshape(WIN, WIN, -1) for c in range(2)]
        rows.append(jnp.concatenate(parts, axis=1))
    return jnp.concatenate(rows, axis=0)


def token_mask(mask):
    t = iota((4 * AREA, 2 * WIN), 0)
    lane = iota((4 * AREA, 2 * WIN), 1)
    w, i, j = t // AREA, (t % AREA) // WIN, t % WIN
    pick_row = (lane == WIN * (w // 2) + i).astype(F32)
    pick_col = (lane == WIN * (w % 2) + j).astype(F32)
    rows = dot(pick_row, mask, 1, 0)
    return jnp.sum(rows * pick_col, axis=1, keepdims=True)


def norm_rows(x):
    center = x - jnp.mean(x, axis=-1, keepdims=True)
    spread = jnp.mean(center * center, axis=-1, keepdims=True)
    scaling = lax.rsqrt(spread + 1e-05)
    return center * scaling, scaling


def head_blocks():
    row = iota((GROUP, GROUP), 0) // HEAD_DIM
    col = iota((GROUP, GROUP), 1) // HEAD_DIM
    return (row == col).astype(F32)


def stack_heads(part, blocks):
    return jnp.concatenate([part] * GROUP_HEADS, axis=0) * blocks.astype(part.dtype)


def unstack_heads(full, blocks):
    kept = full * blocks
    return sum(kept[h * AREA : (h + 1) * AREA] for h in range(GROUP_HEADS))


def lanes(g):
    return slice(g * GROUP, (g + 1) * GROUP)


def lat_side(row):
    return (row + lax.axis_index("lat") + 1) % 2


def load(pairs, sems):
    copies = [pltpu.make_async_copy(a, b, sems.at[k]) for k, (a, b) in enumerate(pairs)]
    for copy in copies:
        copy.start()
    return copies


def wait(copies):
    for copy in copies:
        copy.wait()


def prep_kernel(
    x_hbm, mask_hbm, all_ref, first_ref, second_ref, x_ref, mask_ref, sems
):
    copies = load(((mask_hbm, mask_ref), (x_hbm, x_ref)), sems)
    copies[0].wait()
    ocean = token_mask(mask_ref[0].astype(F32))
    copies[1].wait()
    x = x_ref[0].astype(F32)
    parts = []
    for w in range(4):
        part = jnp.where(ocean[w * AREA : (w + 1) * AREA] > 0.5, window_of(x, w), LAND)
        parts.append(part.astype(BF16))
        all_ref[w] = parts[w]
    odd = lax.axis_index("lat") % 2 == 1
    for c in range(2):
        first_ref[c] = jnp.where(odd, parts[c], parts[2 + c])
        second_ref[c] = jnp.where(odd, parts[2 + c], parts[c])


def land_bias(tokens):
    first = (iota((8, D), 1) == 0).astype(BF16)
    picked = dot(first, tokens, 1, 1)[:1]
    return jnp.where(picked > 0.5 * LAND, NEVER, 0.0)


def hidden_of(tokens, gain_ref):
    normed, _ = norm_rows(tokens.astype(F32))
    return (normed * gain_ref[...]).astype(BF16)


def write_block(tokens, wqkv_ref, gain_ref, q_ref, kv_ref, hid_ref, bias_ref, info_ref):
    hidden = hidden_of(tokens, gain_ref)
    hid_ref[: 4 * AREA] = hidden
    projected = dot(hidden, wqkv_ref[...], 1, 0).astype(BF16)
    q_ref[...] = (projected[:, :D] * BF16(HEAD_DIM ** -0.5)).reshape(4, AREA, D)
    kv_ref[:4] = projected[:, D:].reshape(4, AREA, 2 * D)
    row = land_bias(tokens)
    alive = []
    for w in range(4):
        part = row[:, w * AREA : (w + 1) * AREA]
        bias_ref[w] = jnp.broadcast_to(part, (8, AREA))
        alive.append((jnp.max(part) > 0.5 * NEVER).astype(jnp.int32))
        info_ref[1 + w] = alive[w]
    info_ref[0] = jnp.where(
        alive[3] == 0, 3, jnp.where(alive[2] == 0, 2, jnp.where(alive[1] == 0, 1, 0))
    )


def own_kernel(
    tok_ref, cot_hbm, mask_hbm, wqkv_hbm, wout_hbm, gain_hbm,
    q_ref, kv_ref, hid_ref, gb_ref, bias_ref, wqkv_ref, wout_ref, gain_ref, info_ref,
    cot_ref, mask_ref, sems,
):
    pairs = (
        (mask_hbm, mask_ref), (cot_hbm, cot_ref), (gain_hbm, gain_ref), (wqkv_hbm, wqkv_ref),
        (wout_hbm, wout_ref),
    )
    copies = load(pairs, sems)
    wait(copies[:2])
    ocean = token_mask(mask_ref[0].astype(F32))
    cot = cot_ref[0].astype(F32)
    for w in range(4):
        gb_ref[w] = (window_of(cot, w) * ocean[w * AREA : (w + 1) * AREA]).astype(BF16)
    wait(copies[2:4])
    tokens = tok_ref[...].reshape(4 * AREA, D)
    write_block(tokens, wqkv_ref, gain_ref, q_ref, kv_ref, hid_ref, bias_ref, info_ref)
    wait(copies[4:])


def lat_block(first_ref, second_ref, wkv_ref, gain_ref, kv_ref, hid_ref, bias_ref, at):
    lat, lat_count = lax.axis_index("lat"), lax.axis_size("lat")
    odd = lat % 2 == 1
    first_ok = jnp.logical_or(odd, lat < lat_count - 1)
    second_ok = jnp.where(odd, lat_count - 1 - lat, lat) > 0
    parts = [first_ref[0], first_ref[1], second_ref[0], second_ref[1]]
    tokens = jnp.concatenate(parts, axis=0)
    hidden = hidden_of(tokens, gain_ref)
    hid_ref[at * AREA : (at + 4) * AREA] = hidden
    kv_ref[at : at + 4] = dot(hidden, wkv_ref[...], 1, 0).astype(BF16).reshape(4, AREA, 2 * D)
    row = land_bias(tokens)
    for k in range(4):
        part = row[:, k * AREA : (k + 1) * AREA]
        part = jnp.where(first_ok if k < 2 else second_ok, part, NEVER)
        bias_ref[at + k] = jnp.broadcast_to(part, (8, AREA))


def near_kernel(
    lon_ref, first_ref, second_ref, wqkv_ref, gain_ref, q_ref, kv_ref, hid_ref, bias_ref, info_ref
):
    tokens = lon_ref[...].reshape(4 * AREA, D)
    write_block(tokens, wqkv_ref, gain_ref, q_ref, kv_ref, hid_ref, bias_ref, info_ref)
    lat_block(first_ref, second_ref, wqkv_ref.at[:, D:], gain_ref, kv_ref, hid_ref, bias_ref, 4)


def main_kernel(block, last, *refs):
    refs = list(refs)
    take = lambda n: [refs.pop(0) for _ in range(n)]
    info_ref, infon_ref = take(2)
    wqkv_ref, wout_ref, gain_ref, q, gb = take(5)
    if block == 0:
        first_ref, second_ref, kv_own, kv_near, hid_own, hid_near, bias_own, bias_near = take(8)
    else:
        kv, bias, _ = take(3)
    acc, mixed, gq = take(3)
    if block == 0:
        hid, kv, bias = take(3)
    if last:
        dkv, back1_ref, back2_ref = take(3)
        side_ref = None if block else take(1)[0]
    gm, kcat, *sems = refs
    wkv_ref = wqkv_ref.at[:, D:]
    if block == 0:
        pairs = (
            (kv_own, kv.at[:4]), (kv_near, kv.at[4:12]),
            (hid_own, hid.at[: 4 * AREA]), (hid_near, hid.at[4 * AREA : 12 * AREA]),
            (bias_own, bias.at[:4]), (bias_near, bias.at[4:12]),
        )
        copies = load(pairs, sems[0])
        acc[...] = jnp.zeros_like(acc)
        lat_block(first_ref, second_ref, wkv_ref, gain_ref, kv, hid, bias, 12)
        wait(copies)
    mixed[...] = jnp.zeros_like(mixed)
    gq[...] = jnp.zeros_like(gq)
    blocks = head_blocks()
    gm[...] = dot(gb[...].reshape(4 * AREA, D), wout_ref[...], 1, 1).astype(BF16).reshape(gm.shape)
    info = infon_ref if block else info_ref

    def window_at(slot):
        return slot + (slot >= info[0]).astype(jnp.int32)

    def attend(slot, all_keys, all_values, with_out, with_query):
        at = window_at(slot)

        @pl.when(info[1 + at] > 0)
        def _():
            r, c = at // 2, at % 2
            mine, other, side = 4 * block, 4 * (1 - block), 2 * lat_side(r)
            near = [mine + window_at(k) for k in range(3)] + [8 + mine + side, 9 + mine + side]
            away = [other + 1 - c, other + 3 - c, 8 + other + side + 1 - c]
            places = away + near if block else near + away
            few = 3 if block else 5
            key_count, value_count = 8 if all_keys else few, 8 if all_values else few
            for k in range(8):
                kcat[k * AREA : (k + 1) * AREA] = kv[places[k]]
            bias_row = jnp.concatenate([bias[place][:1] for place in places], axis=1)
            spans = [slice(D + g * GROUP, D + (g + 1) * GROUP) for g in range(GROUPS)]
            both = range(GROUPS)
            q_stack = [stack_heads(q[at, :, lanes(g)], blocks) for g in both]
            gm_stack = [stack_heads(gm[at, :, lanes(g)], blocks) for g in both]
            scores = [dot(q_stack[g], kcat[:, lanes(g)], 1, 1) + bias_row for g in both]
            grad_probs = [dot(gm_stack[g], kcat[:, spans[g]], 1, 1) for g in both]
            weights = [jnp.exp(x - jnp.max(x, axis=1, keepdims=True)) for x in scores]
            inverse = [1.0 / jnp.sum(x, axis=1, keepdims=True) for x in weights]
            low = [(x * y).astype(BF16) for x, y in zip(weights, inverse)]
            delta = [jnp.sum(weights[g] * grad_probs[g], axis=1, keepdims=True) * inverse[g] for g in both]
            grad_scores = [
                (weights[g] * ((grad_probs[g] - delta[g]) * inverse[g])).astype(BF16) for g in both
            ]
            if with_out:
                out = [unstack_heads(dot(low[g], kcat[:, spans[g]], 1, 0), blocks) for g in both]
            if with_query:
                grad = [unstack_heads(dot(grad_scores[g], kcat[:, lanes(g)], 1, 0), blocks) for g in both]
            grad_keys = [dot(grad_scores[g][:, : key_count * AREA], q_stack[g], 0, 0) for g in both]
            grad_values = [dot(low[g][:, : value_count * AREA], gm_stack[g], 0, 0) for g in both]
            for g in both:
                if with_out:
                    mixed[at, :, lanes(g)] = out[g].astype(BF16)
                if with_query:
                    gq[at, :, lanes(g)] = (grad[g] * HEAD_DIM ** -0.5).astype(BF16)
                for k in range(8):
                    rows = slice(k * AREA, (k + 1) * AREA)
                    if k < key_count:
                        acc[places[k], :, lanes(g)] += grad_keys[g][rows]
                    if k < value_count:
                        acc[places[k], :, spans[g]] += grad_values[g][rows]

    def sweep(*wanted):
        def step(slot, carry):
            attend(slot, *wanted)
            return carry

        lax.fori_loop(0, 3, step, 0)

    if block == 0 and last:
        sweep(True, True, True, True)
    else:
        lon = lax.axis_index("lon")
        pl.when(lon == 0)(lambda: sweep(True, False, block == 0, True))
        pl.when(lon == 1)(lambda: sweep(False, True, True, block == 0))
    if not last:
        return
    dkv[...] = acc[...].astype(BF16)
    near = dkv[8:12] if block else dkv[4:]
    shares = dot(near.reshape(-1, 2 * D), wkv_ref[...], 1, 1).astype(BF16).reshape(-1, AREA, D)
    if block:
        back1_ref[...] = shares[:2]
        back2_ref[...] = shares[2:4]
    else:
        side_ref[...] = shares[:4]
        for ref, at in ((back1_ref, 4), (back2_ref, 6)):
            ref[:2] = shares[at : at + 2]
            ref[2:] = shares[at + 4 : at + 6]


def sums_kernel(pair, hid, dkv, *refs):
    held = [refs[k : k + 3] for k in range(0, len(refs) - 2, 3)]
    keep, send = refs[-2:]
    flat = lambda ref: ref[...].reshape(4 * AREA, D)
    lev = lax.axis_index("lev")

    def columns(rel):
        return pl.ds(pl.multiple_of((lev ^ rel) * 128, 128), 128)

    def grad_part(at, width):
        return dkv[:, :, at : at + width].reshape(16 * AREA, width)

    def query_sum(rel):
        parts = [
            dot(hid[4 * b * AREA : 4 * (b + 1) * AREA, columns(rel)], flat(gq), 0, 0)
            for b, (gq, _, _) in enumerate(held)
        ]
        return sum(parts[1:], parts[0])

    def out_sum(rel):
        parts = [
            dot(mixed[:, :, columns(rel)].reshape(4 * AREA, 128), flat(gb), 0, 0) for _, mixed, gb in held
        ]
        return sum(parts[1:], parts[0])

    if pair:
        odd, lon = lax.axis_index("lat") % 2, lax.axis_index("lon")

        def put(rel, at, value):
            to = keep if rel % 2 == 0 else send
            value = value.astype(BF16)
            for k in range(2):
                to[rel // 2, k ^ odd, :, at : at + D] = value[k * 64 : (k + 1) * 64]

        @pl.when(lon == 0)
        def _():
            for rel in range(4):
                put(rel, 0, query_sum(rel))
                put(rel, D, dot(hid[:, columns(rel)], grad_part(0, D), 0, 0))

        @pl.when(lon == 1)
        def _():
            for rel in range(4):
                put(rel, 0, out_sum(rel))
                put(rel, D, dot(hid[:, columns(rel)], grad_part(D, D), 0, 0))

    else:
        for rel in range(4):
            to = keep if rel % 2 == 0 else send
            to[rel // 2, :, :D] = query_sum(rel).astype(BF16)
            to[rel // 2, :, D : 2 * D] = out_sum(rel).astype(BF16)
            to[rel // 2, :, 2 * D :] = dot(hid[:, columns(rel)], grad_part(0, 2 * D), 0, 0).astype(BF16)


def split_kernel(keep_ref, come_ref, far_ref, lat_ref, lev_ref, own_ref):
    for k, ref in enumerate((own_ref, lat_ref, lev_ref, far_ref)):
        total = keep_ref[k // 2, k % 2].astype(F32) + come_ref[k // 2, k % 2].astype(F32)
        ref[...] = total.astype(ref.dtype)


def input_kernel(pair, dkv, back1_ref, back2_ref, gq, tok_ref, mixed, *rest):
    refs = rest if pair else rest[1:]
    wqkv_ref, wout_ref, gain_ref, cot_hbm, x_hbm, mask_hbm, out_ref, ing_ref = refs[:8]
    cot_ref, x_ref, mask_ref, sems = refs[8:]
    copies = load(((x_hbm, x_ref), (mask_hbm, mask_ref), (cot_hbm, cot_ref)), sems)
    odd = lax.axis_index("lat") % 2 == 1
    shares = []
    for w in range(4):
        one, two = back1_ref[w % 2].astype(F32), back2_ref[w % 2].astype(F32)
        share = jnp.where(odd, one, two) if w < 2 else jnp.where(odd, two, one)
        shares.append(share if pair else share + rest[0][w].astype(F32))
    normed, scaling = norm_rows(tok_ref[...].reshape(4 * AREA, D).astype(F32))
    wait(copies)
    ocean = token_mask(mask_ref[0].astype(F32))
    added = (dot(mixed[:4].reshape(4 * AREA, D), wout_ref[...], 1, 0) * ocean).reshape(4, AREA, D)
    out_ref[0] = (x_ref[0].astype(F32) + grid_of([added[w] for w in range(4)])).astype(BF16)
    grad_hidden = jnp.concatenate(shares, axis=0)
    grad_hidden = grad_hidden + dot(gq[:4].reshape(4 * AREA, D), wqkv_ref[:, :D], 1, 1)
    grad_hidden = grad_hidden + dot(dkv[:4].reshape(4 * AREA, 2 * D), wqkv_ref[:, D:], 1, 1)
    scaled = grad_hidden * gain_ref[...]
    correction = (
        scaled
        - jnp.mean(scaled, axis=-1, keepdims=True)
        - normed * jnp.mean(scaled * normed, axis=-1, keepdims=True)
    )
    added = (scaling * correction).reshape(4, AREA, D)
    ing_ref[0] = (cot_ref[0].astype(F32) + grid_of([added[w] for w in range(4)])).astype(BF16)


def gain_row(wqkv_ref, gain_ref, qkv_ref):
    at = pl.ds(pl.multiple_of(lax.axis_index("lev") * 128, 128), 128)
    product = wqkv_ref[at, :].astype(F32) * qkv_ref[...]
    return dot(jnp.ones((8, 3 * D), F32), product, 1, 1, EXACT)[:1] / gain_ref[:, at]


def finish_rows_kernel(
    own_ref, far_ref, wqkv_ref, gain_ref, qkv_ref, out_ref, gg_ref
):
    half = own_ref.shape[0]
    first = lax.axis_index("lon") % 2 == 0
    own, far = own_ref[...], far_ref[...]
    for k in range(2):
        value = (jnp.where(first, own, far) if k == 0 else jnp.where(first, far, own)).astype(F32)
        rows = slice(k * half, (k + 1) * half)
        qkv_ref[rows, :D] = value[:, :D]
        qkv_ref[rows, D:] = value[:, 2 * D :]
        out_ref[rows] = value[:, D : 2 * D]
    gg_ref[...] = gain_row(wqkv_ref, gain_ref, qkv_ref)


def finish_pair_kernel(
    own_ref, lat_ref, lon_ref, far_ref, wqkv_ref, gain_ref, qkv_ref, out_ref, gg_ref
):
    odd = lax.axis_index("lat") % 2 == 1
    first = lax.axis_index("lon") == 0
    for k in range(2):
        rows = slice(64 * k, 64 * k + 64)
        mine = odd if k == 1 else jnp.logical_not(odd)
        near = jnp.where(mine, own_ref[...], lat_ref[...]).astype(F32)
        away = jnp.where(mine, lon_ref[...], far_ref[...]).astype(F32)
        low, high = jnp.where(first, near, away), jnp.where(first, away, near)
        qkv_ref[rows, : 2 * D] = low
        out_ref[rows] = high[:, :D]
        qkv_ref[rows, 2 * D :] = high[:, D:]
    gg_ref[...] = gain_row(wqkv_ref, gain_ref, qkv_ref)


SMEM = pl.BlockSpec(memory_space=pltpu.SMEM)
VMEM = pl.BlockSpec(memory_space=pltpu.VMEM)
ANY = pl.BlockSpec(memory_space=pl.ANY)
HBM = pl.BlockSpec(memory_space=pltpu.HBM)
DMAS = pltpu.SemaphoreType.DMA


def call(
    name, kernel, outs, scalars, arrays, loose, far, scratch, mebibytes, flops=0, out_specs=None, aliases=None
):
    moved = sum(a.size * a.dtype.itemsize for a in (*arrays, *loose, *far, *outs))
    specs = [SMEM] * len(scalars) + [VMEM] * len(arrays) + [ANY] * len(loose) + [HBM] * len(far)
    return pl.pallas_call(
        kernel,
        out_shape=outs,
        in_specs=specs,
        out_specs=out_specs or [VMEM] * len(outs),
        scratch_shapes=list(scratch),
        input_output_aliases=aliases or {},
        compiler_params=pltpu.CompilerParams(vmem_limit_bytes=mebibytes * 1024 * 1024),
        cost_estimate=pl.CostEstimate(flops=flops, bytes_accessed=moved, transcendentals=0),
        name=name,
    )(*scalars, *arrays, *loose, *far)


def shape(dims, dtype=BF16):
    return jax.ShapeDtypeStruct(dims, dtype)


def ring(count, step, periodic):
    return [
        (i, (i + step) % count) for i in range(count) if periodic or 0 <= i + step < count
    ]


def lon_halo(own):
    count = lax.axis_size("lon")
    if count == 2:
        return lax.ppermute(own, "lon", [(0, 1), (1, 0)])
    left = lax.ppermute(own[1::2], "lon", ring(count, 1, True))
    right = lax.ppermute(own[0::2], "lon", ring(count, -1, True))
    return jnp.stack([right, left], axis=1).reshape(own.shape)


def lon_return(side):
    count = lax.axis_size("lon")
    if count == 2:
        return lax.ppermute(side, "lon", [(0, 1), (1, 0)])
    from_left = lax.ppermute(side[0::2], "lon", ring(count, 1, True))
    from_right = lax.ppermute(side[1::2], "lon", ring(count, -1, True))
    return jnp.stack([from_left, from_right], axis=1).reshape(side.shape)


def lat_swap(value, start):
    pairs = [(i, i + 1) for i in range(start, lax.axis_size("lat") - 1, 2)]
    return lax.ppermute(value, "lat", pairs + [(b, a) for a, b in pairs])


def lat_swaps(first, second):
    return lat_swap(first, 0), lat_swap(second, 1)


def corner_swap(value, start):
    count = lax.axis_size("lat")
    pairs = [(i, i + 1) for i in range(start, count - 1, 2)]
    pairs = [(a + k * count, b + (1 - k) * count) for a, b in pairs for k in range(2)]
    return lax.ppermute(value, ("lon", "lat"), pairs + [(b, a) for a, b in pairs])


def swap(value, axis, bit):
    return lax.ppermute(value, axis, [(i, i ^ bit) for i in range(lax.axis_size(axis))])


def halve(parts, axis, bit):
    at = (lax.axis_index(axis) // bit) % 2
    sent = lax.dynamic_index_in_dim(parts, 1 - at, 0, False).astype(BF16)
    kept = lax.dynamic_index_in_dim(parts, at, 0, False)
    return kept + swap(sent, axis, bit).astype(F32)


def rejoin(half, axis, bit):
    first = (lax.axis_index(axis) // bit) % 2 == 0
    far = swap(half, axis, bit)
    return jnp.concatenate([jnp.where(first, half, far), jnp.where(first, far, half)], axis=0)


def bits(axis):
    count = lax.axis_size(axis)
    return [1 << k for k in range(count.bit_length() - 1)]


def gradient_sum(keep, send):
    width = keep.shape[2] // 2
    total = keep.astype(F32) + swap(send, "lev", 1).astype(F32)
    part_a = total[0, :, :width] + swap(total[1, :, :width].astype(BF16), "lev", 2).astype(F32)
    part_b = total[:, :, width:]
    for bit in bits("lon"):
        rows = part_a.shape[0] // 2
        part_a = halve(part_a.reshape(2, rows, width), "lon", bit)
        part_b = halve(jnp.swapaxes(part_b.reshape(2, 2, rows, width), 0, 1), "lon", bit)
    part_b = part_b[0] + swap(part_b[1].astype(BF16), "lev", 2).astype(F32)
    return jnp.concatenate([part_a, part_b], axis=1)


def plane_sum(part):
    for bit in bits("lat"):
        part = halve(part.reshape(2, part.shape[0] // 2, -1), "lat", bit)
    part = part.astype(BF16)
    for bit in reversed(bits("lat")):
        part = rejoin(part, "lat", bit)
    for bit in reversed(bits("lon")[1:]):
        part = rejoin(part, "lon", bit)
    return part, swap(part, "lon", 1)


def pair_sum(keep, send):
    count = lax.axis_size("lat")
    width = keep.shape[-1]
    come = swap(send, "lev", 1)
    piece = shape(keep.shape[2:])
    to_far, to_lat, to_lev, own = call(
        "split", split_kernel, [piece, piece, piece, shape(piece.shape, F32)], [], [keep, come], [], [], [], 8
    )
    from_far = lax.ppermute(to_far, ("lat", "lev"), [(i, i ^ 6) for i in range(4 * count)])
    from_lat = swap(to_lat, "lat", 1)
    from_lev = swap(to_lev, "lev", 2)
    own = own + from_lev.astype(F32) + from_lat.astype(F32) + from_far.astype(F32)
    return own.astype(BF16)


def lat_sum(own):
    for bit in bits("lat")[1:]:
        own = (own.astype(F32) + swap(own, "lat", bit).astype(F32)).astype(BF16)
    return own


def pair_spread(own):
    count = lax.axis_size("lat")
    by_far = lax.ppermute(own, ("lon", "lat"), [(i, i ^ (count + 1)) for i in range(2 * count)])
    return own, swap(own, "lat", 1), swap(own, "lon", 1), by_far


def on_device(tokens_in, cotangent, qkv_weight, out_weight, norm_gain, ocean_mask):
    pair = lax.axis_size("lon") == 2
    gain = norm_gain.reshape(1, D)
    half = shape((2, AREA, D))
    four = shape((4, AREA, D))
    wide = shape((4, AREA, 2 * D))
    info_shape = shape((8,), jnp.int32)
    vmem = lambda *dims: pltpu.VMEM(dims, BF16)
    grid = vmem(*tokens_in.shape)
    mask = pltpu.VMEM(ocean_mask.shape, jnp.int32)
    tok, tok_first, tok_second = call(
        "prep", prep_kernel, [four, half, half], [], [], [], [tokens_in, ocean_mask],
        [grid, mask, DMAS((2,))], 8, flops=10 ** 10,
    )
    tok_lon = lon_halo(tok)
    odd = lax.axis_index("lat") % 2
    if pair:
        corner_first, corner_second = corner_swap(tok_first, 0), corner_swap(tok_second, 1)
    tok_first, tok_second = lat_swaps(tok_first, tok_second)
    q, kv, hid, gb, bias, wqkv, wout, gain, info = call(
        "own", own_kernel,
        [four, wide, shape((4 * AREA, D)), four, shape((4, 8, AREA), F32), shape(qkv_weight.shape),
         shape(out_weight.shape), shape(gain.shape, F32), info_shape],
        [], [tok], [], [cotangent, ocean_mask, qkv_weight, out_weight, gain], [grid, mask, DMAS((5,))], 16,
        flops=2 * 256 * 512 * 1536, out_specs=[VMEM] * 8 + [SMEM],
    )
    if pair:
        gb_near = lon_halo(gb)
    else:
        rows = tok_lon.reshape(2, 2, AREA, D)
        corner_first, corner_second = lat_swaps(
            lax.dynamic_index_in_dim(rows, 1 - odd, 0, False),
            lax.dynamic_index_in_dim(rows, odd, 0, False),
        )
    q_near, kv_near, hid_near, bias_near, info_near = call(
        "near", near_kernel,
        [four, shape((8, AREA, 2 * D)), shape((8 * AREA, D)), shape((8, 8, AREA), F32), info_shape],
        [], [tok_lon, tok_first, tok_second, wqkv, gain], [], [], [], 20,
        flops=2 * 512 * 512 * 1280, out_specs=[VMEM] * 4 + [SMEM],
    )
    all_shape, all32 = shape((16, AREA, 2 * D)), shape((16, AREA, 2 * D), F32)
    back = shape((2 if pair else 4, AREA, D))
    ends = [all_shape, back, back] + ([] if pair else [four])
    weights = [wqkv, wout, gain]
    scratch = [vmem(4, AREA, D), vmem(KEYS, 2 * D)]
    flops = 3 * 12 * 2 * 512 * 256 * 256
    acc, mixed, gq, hid_all, kv_all, bias_all, *rest = call(
        "main", lambda *refs: main_kernel(0, not pair, *refs),
        [all32, four, four, shape((16 * AREA, D)), all_shape, shape((16, 8, AREA), F32)]
        + ([] if pair else ends),
        [info, info_near], weights + [q, gb, corner_first, corner_second],
        [kv, kv_near, hid, hid_near, bias, bias_near], [], scratch + [DMAS((6,))], 28, flops=flops,
    )
    parts = [gq, mixed, gb]
    if pair:
        _, mixed_near, gq_near, *rest = call(
            "other", lambda *refs: main_kernel(1, True, *refs), [all32, four, four] + ends,
            [info, info_near], weights + [q_near, gb_near, kv_all, bias_all, acc], [], [],
            scratch, 28, flops=flops, aliases={9: 0},
        )
        parts += [gq_near, mixed_near, gb_near]
    dkv, back_first, back_second, *side = rest
    share = shape((2, 2, 64, 2 * D) if pair else (2, 128, 4 * D))
    keep, send = call(
        "sums", lambda *refs: sums_kernel(pair, *refs), [share, share], [],
        [hid_all, dkv] + parts, [], [], [], 24, flops=2 * 1024 * 512 * 1024,
    )
    if pair:
        total = pair_sum(keep, send)
        back_second = lat_swap(back_second, 1)
        total, back_first, back_second = lax.optimization_barrier((total, back_first, back_second))
        back_first = lat_swap(back_first, 0)
        total = lat_sum(total)
        total, back_first = lax.optimization_barrier((total, back_first))
        sums = pair_spread(total)
        lon_share = []
        finish = finish_pair_kernel
    else:
        part = gradient_sum(keep, send)
        back_first, back_second = lat_swaps(back_first, back_second)
        one, two = back_first[2:].astype(F32), back_second[2:].astype(F32)
        rows = jnp.stack([jnp.where(odd == 1, one, two), jnp.where(odd == 1, two, one)])
        side = (side[0].reshape(rows.shape).astype(F32) + rows).astype(BF16)
        lon_share = [lon_return(side.reshape(four.shape))]
        sums = plane_sum(part)
        finish = finish_rows_kernel
    layer_out, input_grad = call(
        "input", lambda *refs: input_kernel(pair, *refs),
        [shape(tokens_in.shape), shape(tokens_in.shape)], [],
        [dkv, back_first, back_second, gq, tok, mixed] + lon_share + weights, [],
        [cotangent, tokens_in, ocean_mask], [grid, grid, mask, DMAS((3,))], 24, flops=2 * 256 * 512 * 1536,
    )
    qkv_grad, out_grad, gain_grad = call(
        "finish", finish,
        [shape((128, 3 * D), F32), shape((128, D), F32), shape((1, 128), F32)], [],
        [*sums, wqkv, gain], [], [], [], 16,
    )
    return layer_out, input_grad, qkv_grad, out_grad, gain_grad.reshape(128)


def solution(mesh):
    placed = (
        P("lev", "lat", "lon", None),
        P("lev", "lat", "lon", None),
        P(),
        P(),
        P(),
        P("lev", "lat", "lon"),
    )
    return jax.shard_map(
        on_device,
        mesh=mesh,
        in_specs=placed,
        out_specs=(
            P("lev", "lat", "lon", None),
            P("lev", "lat", "lon", None),
            P("lev", None),
            P("lev", None),
            P("lev"),
        ),
        check_vma=False,
    )
```

```python
import jax
import jax.numpy as jnp
from jax import lax
from jax.experimental import pallas as pl
from jax.experimental.pallas import tpu as pltpu
from jax.sharding import PartitionSpec as P

HEADS = 8
WIN = 8
AREA = WIN * WIN
D = 512
HEAD_DIM = D // HEADS
GROUP = 256
GROUP_HEADS = GROUP // HEAD_DIM
GROUPS = D // GROUP
KEYS = 8 * AREA
LAND = 1000.0
NEVER = -1e9
FAR = 1e30
F32 = jnp.float32
BF16 = jnp.bfloat16
EXACT = lax.Precision.HIGHEST


def dot(a, b, ca, cb, precision=None):
    return lax.dot_general(
        a, b, (((ca,), (cb,)), ((), ())), preferred_element_type=F32, precision=precision
    )


def iota(shape, dim):
    return lax.broadcasted_iota(jnp.int32, shape, dim)


def window_of(grid, w):
    r, c = divmod(w, 2)
    part = grid[r * WIN : (r + 1) * WIN, c * WIN : (c + 1) * WIN, :]
    return part.reshape(AREA, grid.shape[-1])


def grid_of(windows):
    rows = []
    for r in range(2):
        parts = [windows[2 * r + c].reshape(WIN, WIN, -1) for c in range(2)]
        rows.append(jnp.concatenate(parts, axis=1))
    return jnp.concatenate(rows, axis=0)


def token_mask(mask):
    t = iota((4 * AREA, 2 * WIN), 0)
    lane = iota((4 * AREA, 2 * WIN), 1)
    w, i, j = t // AREA, (t % AREA) // WIN, t % WIN
    pick_row = (lane == WIN * (w // 2) + i).astype(F32)
    pick_col = (lane == WIN * (w % 2) + j).astype(F32)
    rows = dot(pick_row, mask, 1, 0)
    return jnp.sum(rows * pick_col, axis=1, keepdims=True)


def norm_rows(x):
    center = x - jnp.mean(x, axis=-1, keepdims=True)
    spread = jnp.mean(center * center, axis=-1, keepdims=True)
    scaling = lax.rsqrt(spread + 1e-05)
    return center * scaling, scaling


def head_blocks():
    row = iota((GROUP, GROUP), 0) // HEAD_DIM
    col = iota((GROUP, GROUP), 1) // HEAD_DIM
    return (row == col).astype(F32)


def stack_heads(part, blocks):
    return jnp.concatenate([part] * GROUP_HEADS, axis=0) * blocks.astype(part.dtype)


def unstack_heads(full, blocks):
    kept = full * blocks
    return sum(kept[h * AREA : (h + 1) * AREA] for h in range(GROUP_HEADS))


def lanes(g):
    return slice(g * GROUP, (g + 1) * GROUP)


def lat_side(row):
    return (row + lax.axis_index("lat") + 1) % 2


def load(pairs, sems):
    copies = [pltpu.make_async_copy(a, b, sems.at[k]) for k, (a, b) in enumerate(pairs)]
    for copy in copies:
        copy.start()
    return copies


def wait(copies):
    for copy in copies:
        copy.wait()


def prep_kernel(
    x_hbm, mask_hbm, all_ref, first_ref, second_ref, x_ref, mask_ref, sems
):
    copies = load(((mask_hbm, mask_ref), (x_hbm, x_ref)), sems)
    copies[0].wait()
    ocean = token_mask(mask_ref[0].astype(F32))
    copies[1].wait()
    x = x_ref[0].astype(F32)
    parts = []
    for w in range(4):
        part = jnp.where(ocean[w * AREA : (w + 1) * AREA] > 0.5, window_of(x, w), LAND)
        parts.append(part.astype(BF16))
        all_ref[w] = parts[w]
    odd = lax.axis_index("lat") % 2 == 1
    for c in range(2):
        first_ref[c] = jnp.where(odd, parts[c], parts[2 + c])
        second_ref[c] = jnp.where(odd, parts[2 + c], parts[c])


def land_bias(tokens):
    first = (iota((8, D), 1) == 0).astype(BF16)
    picked = dot(first, tokens, 1, 1)[:1]
    return jnp.where(picked > 0.5 * LAND, NEVER, 0.0)


def hidden_of(tokens, gain_ref):
    normed, _ = norm_rows(tokens.astype(F32))
    return (normed * gain_ref[...]).astype(BF16)


def write_block(tokens, wqkv_ref, gain_ref, q_ref, kv_ref, hid_ref, bias_ref, info_ref):
    hidden = hidden_of(tokens, gain_ref)
    hid_ref[: 4 * AREA] = hidden
    projected = dot(hidden, wqkv_ref[...], 1, 0).astype(BF16)
    q_ref[...] = (projected[:, :D] * BF16(HEAD_DIM ** -0.5)).reshape(4, AREA, D)
    kv_ref[:4] = projected[:, D:].reshape(4, AREA, 2 * D)
    row = land_bias(tokens)
    alive = []
    for w in range(4):
        part = row[:, w * AREA : (w + 1) * AREA]
        bias_ref[w] = jnp.broadcast_to(part, (8, AREA))
        alive.append((jnp.max(part) > 0.5 * NEVER).astype(jnp.int32))
        info_ref[1 + w] = alive[w]
    info_ref[0] = jnp.where(
        alive[3] == 0, 3, jnp.where(alive[2] == 0, 2, jnp.where(alive[1] == 0, 1, 0))
    )


def own_kernel(
    tok_ref, wqkv_ref, gain_ref, cot_hbm, mask_hbm,
    q_ref, kv_ref, hid_ref, gb_ref, bias_ref, info_ref, cot_ref, mask_ref, sems,
):
    copies = load(((mask_hbm, mask_ref), (cot_hbm, cot_ref)), sems)
    tokens = tok_ref[...].reshape(4 * AREA, D)
    write_block(tokens, wqkv_ref, gain_ref, q_ref, kv_ref, hid_ref, bias_ref, info_ref)
    wait(copies)
    ocean = token_mask(mask_ref[0].astype(F32))
    cot = cot_ref[0].astype(F32)
    for w in range(4):
        gb_ref[w] = (window_of(cot, w) * ocean[w * AREA : (w + 1) * AREA]).astype(BF16)


def lat_block(first_ref, second_ref, wkv_ref, gain_ref, kv_ref, hid_ref, bias_ref, at):
    lat, lat_count = lax.axis_index("lat"), lax.axis_size("lat")
    odd = lat % 2 == 1
    first_ok = jnp.logical_or(odd, lat < lat_count - 1)
    second_ok = jnp.where(odd, lat_count - 1 - lat, lat) > 0
    parts = [first_ref[0], first_ref[1], second_ref[0], second_ref[1]]
    tokens = jnp.concatenate(parts, axis=0)
    hidden = hidden_of(tokens, gain_ref)
    hid_ref[at * AREA : (at + 4) * AREA] = hidden
    kv_ref[at : at + 4] = dot(hidden, wkv_ref[...], 1, 0).astype(BF16).reshape(4, AREA, 2 * D)
    row = land_bias(tokens)
    for k in range(4):
        part = row[:, k * AREA : (k + 1) * AREA]
        part = jnp.where(first_ok if k < 2 else second_ok, part, NEVER)
        bias_ref[at + k] = jnp.broadcast_to(part, (8, AREA))


def near_kernel(
    lon_ref, first_ref, second_ref, wqkv_ref, gain_ref, q_ref, kv_ref, hid_ref, bias_ref, info_ref
):
    tokens = lon_ref[...].reshape(4 * AREA, D)
    write_block(tokens, wqkv_ref, gain_ref, q_ref, kv_ref, hid_ref, bias_ref, info_ref)
    lat_block(first_ref, second_ref, wqkv_ref.at[:, D:], gain_ref, kv_ref, hid_ref, bias_ref, 4)


def main_kernel(block, last, *refs):
    refs = list(refs)
    take = lambda n: [refs.pop(0) for _ in range(n)]
    info_ref, infon_ref = take(2)
    wqkv_ref, wout_ref, gain_ref, q, gb = take(5)
    if block == 0:
        first_ref, second_ref, kv_own, kv_near, hid_own, hid_near, bias_own, bias_near = take(8)
    else:
        kv, bias, _ = take(3)
    acc, mixed, gq = take(3)
    if block == 0:
        hid, kv, bias = take(3)
    if last:
        dkv, back1_ref, back2_ref = take(3)
        side_ref = None if block else take(1)[0]
    gm, kcat, *sems = refs
    wkv_ref = wqkv_ref.at[:, D:]
    if block == 0:
        pairs = (
            (kv_own, kv.at[:4]), (kv_near, kv.at[4:12]),
            (hid_own, hid.at[: 4 * AREA]), (hid_near, hid.at[4 * AREA : 12 * AREA]),
            (bias_own, bias.at[:4]), (bias_near, bias.at[4:12]),
        )
        copies = load(pairs, sems[0])
        acc[...] = jnp.zeros_like(acc)
        lat_block(first_ref, second_ref, wkv_ref, gain_ref, kv, hid, bias, 12)
        wait(copies)
    mixed[...] = jnp.zeros_like(mixed)
    gq[...] = jnp.zeros_like(gq)
    blocks = head_blocks()
    gm[...] = dot(gb[...].reshape(4 * AREA, D), wout_ref[...], 1, 1).astype(BF16).reshape(gm.shape)
    info = infon_ref if block else info_ref

    def window_at(slot):
        return slot + (slot >= info[0]).astype(jnp.int32)

    def attend(slot, all_keys, all_values, with_out, with_query):
        at = window_at(slot)

        @pl.when(info[1 + at] > 0)
        def _():
            r, c = at // 2, at % 2
            mine, other, side = 4 * block, 4 * (1 - block), 2 * lat_side(r)
            near = [mine + window_at(k) for k in range(3)] + [8 + mine + side, 9 + mine + side]
            away = [other + 1 - c, other + 3 - c, 8 + other + side + 1 - c]
            places = away + near if block else near + away
            few = 3 if block else 5
            key_count, value_count = 8 if all_keys else few, 8 if all_values else few
            for k in range(8):
                kcat[k * AREA : (k + 1) * AREA] = kv[places[k]]
            bias_row = jnp.concatenate([bias[place][:1] for place in places], axis=1)
            spans = [slice(D + g * GROUP, D + (g + 1) * GROUP) for g in range(GROUPS)]
            both = range(GROUPS)
            q_stack = [stack_heads(q[at, :, lanes(g)], blocks) for g in both]
            gm_stack = [stack_heads(gm[at, :, lanes(g)], blocks) for g in both]
            scores = [dot(q_stack[g], kcat[:, lanes(g)], 1, 1) + bias_row for g in both]
            grad_probs = [dot(gm_stack[g], kcat[:, spans[g]], 1, 1) for g in both]
            weights = [jnp.exp(x - jnp.max(x, axis=1, keepdims=True)) for x in scores]
            inverse = [1.0 / jnp.sum(x, axis=1, keepdims=True) for x in weights]
            low = [(x * y).astype(BF16) for x, y in zip(weights, inverse)]
            delta = [jnp.sum(weights[g] * grad_probs[g], axis=1, keepdims=True) * inverse[g] for g in both]
            grad_scores = [
                (weights[g] * ((grad_probs[g] - delta[g]) * inverse[g])).astype(BF16) for g in both
            ]
            if with_out:
                out = [unstack_heads(dot(low[g], kcat[:, spans[g]], 1, 0), blocks) for g in both]
            if with_query:
                grad = [unstack_heads(dot(grad_scores[g], kcat[:, lanes(g)], 1, 0), blocks) for g in both]
            grad_keys = [dot(grad_scores[g][:, : key_count * AREA], q_stack[g], 0, 0) for g in both]
            grad_values = [dot(low[g][:, : value_count * AREA], gm_stack[g], 0, 0) for g in both]
            for g in both:
                if with_out:
                    mixed[at, :, lanes(g)] = out[g].astype(BF16)
                if with_query:
                    gq[at, :, lanes(g)] = (grad[g] * HEAD_DIM ** -0.5).astype(BF16)
                for k in range(8):
                    rows = slice(k * AREA, (k + 1) * AREA)
                    if k < key_count:
                        acc[places[k], :, lanes(g)] += grad_keys[g][rows]
                    if k < value_count:
                        acc[places[k], :, spans[g]] += grad_values[g][rows]

    def sweep(*wanted):
        def step(slot, carry):
            attend(slot, *wanted)
            return carry

        lax.fori_loop(0, 3, step, 0)

    if block == 0 and last:
        sweep(True, True, True, True)
    else:
        lon = lax.axis_index("lon")
        pl.when(lon == 0)(lambda: sweep(True, False, block == 0, True))
        pl.when(lon == 1)(lambda: sweep(False, True, True, block == 0))
    if not last:
        return
    dkv[...] = acc[...].astype(BF16)
    near = dkv[8:12] if block else dkv[4:]
    shares = dot(near.reshape(-1, 2 * D), wkv_ref[...], 1, 1).astype(BF16).reshape(-1, AREA, D)
    if block:
        back1_ref[...] = shares[:2]
        back2_ref[...] = shares[2:4]
    else:
        side_ref[...] = shares[:4]
        for ref, at in ((back1_ref, 4), (back2_ref, 6)):
            ref[:2] = shares[at : at + 2]
            ref[2:] = shares[at + 4 : at + 6]


def sums_kernel(pair, other, hid, dkv, *refs):
    held = [refs[k : k + 3] for k in range(0, len(refs) - 1, 3)]
    to = refs[-1]
    flat = lambda ref: ref[...].reshape(4 * AREA, D)
    lev = lax.axis_index("lev")

    def columns(rel):
        return pl.ds(pl.multiple_of((lev ^ rel) * 128, 128), 128)

    def grad_part(at, width):
        return dkv[:, :, at : at + width].reshape(16 * AREA, width)

    def query_sum(rel):
        parts = [
            dot(hid[4 * b * AREA : 4 * (b + 1) * AREA, columns(rel)], flat(gq), 0, 0)
            for b, (gq, _, _) in enumerate(held)
        ]
        return sum(parts[1:], parts[0])

    def out_sum(rel):
        parts = [
            dot(mixed[:, :, columns(rel)].reshape(4 * AREA, 128), flat(gb), 0, 0) for _, mixed, gb in held
        ]
        return sum(parts[1:], parts[0])

    if pair:
        odd, lon = lax.axis_index("lat") % 2, lax.axis_index("lon")

        def put(rel, at, value):
            value = value.astype(BF16)
            for k in range(2):
                to[rel // 2, k ^ odd, :, at : at + D] = value[k * 64 : (k + 1) * 64]

        @pl.when(lon == 0)
        def _():
            for rel in (other, 2 + other):
                put(rel, 0, query_sum(rel))
                put(rel, D, dot(hid[:, columns(rel)], grad_part(0, D), 0, 0))

        @pl.when(lon == 1)
        def _():
            for rel in (other, 2 + other):
                put(rel, 0, out_sum(rel))
                put(rel, D, dot(hid[:, columns(rel)], grad_part(D, D), 0, 0))

    else:
        for rel in (other, 2 + other):
            to[rel // 2, :, :D] = query_sum(rel).astype(BF16)
            to[rel // 2, :, D : 2 * D] = out_sum(rel).astype(BF16)
            to[rel // 2, :, 2 * D :] = dot(hid[:, columns(rel)], grad_part(0, 2 * D), 0, 0).astype(BF16)


def split_kernel(keep_ref, come_ref, far_ref, lat_ref, lev_ref, own_ref):
    for k, ref in enumerate((own_ref, lat_ref, lev_ref, far_ref)):
        total = keep_ref[k // 2, k % 2].astype(F32) + come_ref[k // 2, k % 2].astype(F32)
        ref[...] = total.astype(ref.dtype)


def input_kernel(pair, dkv, back1_ref, back2_ref, gq, tok_ref, mixed, *rest):
    refs = rest if pair else rest[1:]
    wqkv_ref, wout_ref, gain_ref, cot_hbm, x_hbm, mask_hbm, out_ref, ing_ref = refs[:8]
    cot_ref, x_ref, mask_ref, sems = refs[8:]
    copies = load(((x_hbm, x_ref), (mask_hbm, mask_ref), (cot_hbm, cot_ref)), sems)
    odd = lax.axis_index("lat") % 2 == 1
    shares = []
    for w in range(4):
        one, two = back1_ref[w % 2].astype(F32), back2_ref[w % 2].astype(F32)
        share = jnp.where(odd, one, two) if w < 2 else jnp.where(odd, two, one)
        shares.append(share if pair else share + rest[0][w].astype(F32))
    normed, scaling = norm_rows(tok_ref[...].reshape(4 * AREA, D).astype(F32))
    wait(copies)
    ocean = token_mask(mask_ref[0].astype(F32))
    added = (dot(mixed[:4].reshape(4 * AREA, D), wout_ref[...], 1, 0) * ocean).reshape(4, AREA, D)
    out_ref[0] = (x_ref[0].astype(F32) + grid_of([added[w] for w in range(4)])).astype(BF16)
    grad_hidden = jnp.concatenate(shares, axis=0)
    grad_hidden = grad_hidden + dot(gq[:4].reshape(4 * AREA, D), wqkv_ref[:, :D], 1, 1)
    grad_hidden = grad_hidden + dot(dkv[:4].reshape(4 * AREA, 2 * D), wqkv_ref[:, D:], 1, 1)
    scaled = grad_hidden * gain_ref[...]
    correction = (
        scaled
        - jnp.mean(scaled, axis=-1, keepdims=True)
        - normed * jnp.mean(scaled * normed, axis=-1, keepdims=True)
    )
    added = (scaling * correction).reshape(4, AREA, D)
    ing_ref[0] = (cot_ref[0].astype(F32) + grid_of([added[w] for w in range(4)])).astype(BF16)


def gain_row(wqkv_ref, gain_ref, qkv_ref):
    at = pl.ds(pl.multiple_of(lax.axis_index("lev") * 128, 128), 128)
    product = wqkv_ref[at, :].astype(F32) * qkv_ref[...]
    return dot(jnp.ones((8, 3 * D), F32), product, 1, 1, EXACT)[:1] / gain_ref[:, at]


def finish_rows_kernel(
    own_ref, far_ref, wqkv_ref, gain_ref, qkv_ref, out_ref, gg_ref
):
    half = own_ref.shape[0]
    first = lax.axis_index("lon") % 2 == 0
    own, far = own_ref[...], far_ref[...]
    for k in range(2):
        value = (jnp.where(first, own, far) if k == 0 else jnp.where(first, far, own)).astype(F32)
        rows = slice(k * half, (k + 1) * half)
        qkv_ref[rows, :D] = value[:, :D]
        qkv_ref[rows, D:] = value[:, 2 * D :]
        out_ref[rows] = value[:, D : 2 * D]
    gg_ref[...] = gain_row(wqkv_ref, gain_ref, qkv_ref)


def finish_pair_kernel(
    own_ref, lat_ref, lon_ref, far_ref, wqkv_ref, gain_ref, qkv_ref, out_ref, gg_ref
):
    odd = lax.axis_index("lat") % 2 == 1
    first = lax.axis_index("lon") == 0
    for k in range(2):
        rows = slice(64 * k, 64 * k + 64)
        mine = odd if k == 1 else jnp.logical_not(odd)
        near = jnp.where(mine, own_ref[...], lat_ref[...]).astype(F32)
        away = jnp.where(mine, lon_ref[...], far_ref[...]).astype(F32)
        low, high = jnp.where(first, near, away), jnp.where(first, away, near)
        qkv_ref[rows, : 2 * D] = low
        out_ref[rows] = high[:, :D]
        qkv_ref[rows, 2 * D :] = high[:, D:]
    gg_ref[...] = gain_row(wqkv_ref, gain_ref, qkv_ref)


SMEM = pl.BlockSpec(memory_space=pltpu.SMEM)
VMEM = pl.BlockSpec(memory_space=pltpu.VMEM)
ANY = pl.BlockSpec(memory_space=pl.ANY)
HBM = pl.BlockSpec(memory_space=pltpu.HBM)
DMAS = pltpu.SemaphoreType.DMA


def call(
    name, kernel, outs, scalars, arrays, loose, far, scratch, mebibytes, flops=0, out_specs=None, aliases=None
):
    moved = sum(a.size * a.dtype.itemsize for a in (*arrays, *loose, *far, *outs))
    specs = [SMEM] * len(scalars) + [VMEM] * len(arrays) + [ANY] * len(loose) + [HBM] * len(far)
    return pl.pallas_call(
        kernel,
        out_shape=outs,
        in_specs=specs,
        out_specs=out_specs or [VMEM] * len(outs),
        scratch_shapes=list(scratch),
        input_output_aliases=aliases or {},
        compiler_params=pltpu.CompilerParams(vmem_limit_bytes=mebibytes * 1024 * 1024),
        cost_estimate=pl.CostEstimate(flops=flops, bytes_accessed=moved, transcendentals=0),
        name=name,
    )(*scalars, *arrays, *loose, *far)


def shape(dims, dtype=BF16):
    return jax.ShapeDtypeStruct(dims, dtype)


def ring(count, step, periodic):
    return [
        (i, (i + step) % count) for i in range(count) if periodic or 0 <= i + step < count
    ]


def lon_halo(own):
    count = lax.axis_size("lon")
    if count == 2:
        return lax.ppermute(own, "lon", [(0, 1), (1, 0)])
    left = lax.ppermute(own[1::2], "lon", ring(count, 1, True))
    right = lax.ppermute(own[0::2], "lon", ring(count, -1, True))
    return jnp.stack([right, left], axis=1).reshape(own.shape)


def lon_return(side):
    count = lax.axis_size("lon")
    if count == 2:
        return lax.ppermute(side, "lon", [(0, 1), (1, 0)])
    from_left = lax.ppermute(side[0::2], "lon", ring(count, 1, True))
    from_right = lax.ppermute(side[1::2], "lon", ring(count, -1, True))
    return jnp.stack([from_left, from_right], axis=1).reshape(side.shape)


def lat_swap(value, start):
    pairs = [(i, i + 1) for i in range(start, lax.axis_size("lat") - 1, 2)]
    return lax.ppermute(value, "lat", pairs + [(b, a) for a, b in pairs])


def lat_swaps(first, second):
    return lat_swap(first, 0), lat_swap(second, 1)


def corner_swap(value, start):
    count = lax.axis_size("lat")
    pairs = [(i, i + 1) for i in range(start, count - 1, 2)]
    pairs = [(a + k * count, b + (1 - k) * count) for a, b in pairs for k in range(2)]
    return lax.ppermute(value, ("lon", "lat"), pairs + [(b, a) for a, b in pairs])


def swap(value, axis, bit):
    return lax.ppermute(value, axis, [(i, i ^ bit) for i in range(lax.axis_size(axis))])


def halve(parts, axis, bit):
    at = (lax.axis_index(axis) // bit) % 2
    sent = lax.dynamic_index_in_dim(parts, 1 - at, 0, False).astype(BF16)
    kept = lax.dynamic_index_in_dim(parts, at, 0, False)
    return kept + swap(sent, axis, bit).astype(F32)


def rejoin(half, axis, bit):
    first = (lax.axis_index(axis) // bit) % 2 == 0
    far = swap(half, axis, bit)
    return jnp.concatenate([jnp.where(first, half, far), jnp.where(first, far, half)], axis=0)


def bits(axis):
    count = lax.axis_size(axis)
    return [1 << k for k in range(count.bit_length() - 1)]


def gradient_sum(keep, send):
    width = keep.shape[2] // 2
    total = keep.astype(F32) + swap(send, "lev", 1).astype(F32)
    part_a = total[0, :, :width] + swap(total[1, :, :width].astype(BF16), "lev", 2).astype(F32)
    part_b = total[:, :, width:]
    for bit in bits("lon"):
        rows = part_a.shape[0] // 2
        part_a = halve(part_a.reshape(2, rows, width), "lon", bit)
        part_b = halve(jnp.swapaxes(part_b.reshape(2, 2, rows, width), 0, 1), "lon", bit)
    part_b = part_b[0] + swap(part_b[1].astype(BF16), "lev", 2).astype(F32)
    return jnp.concatenate([part_a, part_b], axis=1)


def plane_sum(part):
    for bit in bits("lat"):
        part = halve(part.reshape(2, part.shape[0] // 2, -1), "lat", bit)
    part = part.astype(BF16)
    for bit in reversed(bits("lat")):
        part = rejoin(part, "lat", bit)
    for bit in reversed(bits("lon")[1:]):
        part = rejoin(part, "lon", bit)
    return part, swap(part, "lon", 1)


def pair_sum(keep, send):
    count = lax.axis_size("lat")
    width = keep.shape[-1]
    come = swap(send, "lev", 1)
    piece = shape(keep.shape[2:])
    to_far, to_lat, to_lev, own = call(
        "split", split_kernel, [piece, piece, piece, shape(piece.shape, F32)], [], [keep, come], [], [], [], 8
    )
    from_far = lax.ppermute(to_far, ("lat", "lev"), [(i, i ^ 6) for i in range(4 * count)])
    from_lat = swap(to_lat, "lat", 1)
    from_lev = swap(to_lev, "lev", 2)
    own = own + from_lev.astype(F32) + from_lat.astype(F32) + from_far.astype(F32)
    return own.astype(BF16)


def lat_sum(own):
    for bit in bits("lat")[1:]:
        own = (own.astype(F32) + swap(own, "lat", bit).astype(F32)).astype(BF16)
    return own


def pair_spread(own):
    count = lax.axis_size("lat")
    by_far = lax.ppermute(own, ("lon", "lat"), [(i, i ^ (count + 1)) for i in range(2 * count)])
    return own, swap(own, "lat", 1), swap(own, "lon", 1), by_far


def on_device(tokens_in, cotangent, qkv_weight, out_weight, norm_gain, ocean_mask):
    pair = lax.axis_size("lon") == 2
    gain = norm_gain.reshape(1, D)
    half = shape((2, AREA, D))
    four = shape((4, AREA, D))
    wide = shape((4, AREA, 2 * D))
    info_shape = shape((8,), jnp.int32)
    vmem = lambda *dims: pltpu.VMEM(dims, BF16)
    grid = vmem(*tokens_in.shape)
    mask = pltpu.VMEM(ocean_mask.shape, jnp.int32)
    tok, tok_first, tok_second = call(
        "prep", prep_kernel, [four, half, half], [], [], [], [tokens_in, ocean_mask],
        [grid, mask, DMAS((2,))], 8, flops=10 ** 10,
    )
    tok_lon = lon_halo(tok)
    odd = lax.axis_index("lat") % 2
    if pair:
        corner_first, corner_second = corner_swap(tok_first, 0), corner_swap(tok_second, 1)
    tok_first, tok_second = lat_swaps(tok_first, tok_second)
    q, kv, hid, gb, bias, info = call(
        "own", own_kernel,
        [four, wide, shape((4 * AREA, D)), four, shape((4, 8, AREA), F32), info_shape],
        [], [tok, qkv_weight, gain], [], [cotangent, ocean_mask], [grid, mask, DMAS((2,))], 16,
        flops=2 * 256 * 512 * 1536, out_specs=[VMEM] * 5 + [SMEM],
    )
    wqkv, wout = qkv_weight, out_weight
    if pair:
        gb_near = lon_halo(gb)
    else:
        rows = tok_lon.reshape(2, 2, AREA, D)
        corner_first, corner_second = lat_swaps(
            lax.dynamic_index_in_dim(rows, 1 - odd, 0, False),
            lax.dynamic_index_in_dim(rows, odd, 0, False),
        )
    q_near, kv_near, hid_near, bias_near, info_near = call(
        "near", near_kernel,
        [four, shape((8, AREA, 2 * D)), shape((8 * AREA, D)), shape((8, 8, AREA), F32), info_shape],
        [], [tok_lon, tok_first, tok_second, wqkv, gain], [], [], [], 20,
        flops=2 * 512 * 512 * 1280, out_specs=[VMEM] * 4 + [SMEM],
    )
    all_shape, all32 = shape((16, AREA, 2 * D)), shape((16, AREA, 2 * D), F32)
    back = shape((2 if pair else 4, AREA, D))
    ends = [all_shape, back, back] + ([] if pair else [four])
    weights = [wqkv, wout, gain]
    scratch = [vmem(4, AREA, D), vmem(KEYS, 2 * D)]
    flops = 3 * 12 * 2 * 512 * 256 * 256
    acc, mixed, gq, hid_all, kv_all, bias_all, *rest = call(
        "main", lambda *refs: main_kernel(0, not pair, *refs),
        [all32, four, four, shape((16 * AREA, D)), all_shape, shape((16, 8, AREA), F32)]
        + ([] if pair else ends),
        [info, info_near], weights + [q, gb, corner_first, corner_second],
        [kv, kv_near, hid, hid_near, bias, bias_near], [], scratch + [DMAS((6,))], 28, flops=flops,
    )
    parts = [gq, mixed, gb]
    if pair:
        _, mixed_near, gq_near, *rest = call(
            "other", lambda *refs: main_kernel(1, True, *refs), [all32, four, four] + ends,
            [info, info_near], weights + [q_near, gb_near, kv_all, bias_all, acc], [], [],
            scratch, 28, flops=flops, aliases={9: 0},
        )
        parts += [gq_near, mixed_near, gb_near]
    dkv, back_first, back_second, *side = rest
    share = shape((2, 2, 64, 2 * D) if pair else (2, 128, 4 * D))
    send, keep = [
        call(
            name, lambda *refs, other=other: sums_kernel(pair, other, *refs), [share], [],
            [hid_all, dkv] + parts, [], [], [], 24, flops=1024 * 512 * 1024,
        )[0]
        for name, other in (("sent", 1), ("kept", 0))
    ]
    if pair:
        total = pair_sum(keep, send)
        back_second = lat_swap(back_second, 1)
        total, back_first, back_second = lax.optimization_barrier((total, back_first, back_second))
        back_first = lat_swap(back_first, 0)
        total = lat_sum(total)
        total, back_first = lax.optimization_barrier((total, back_first))
        sums = pair_spread(total)
        lon_share = []
        finish = finish_pair_kernel
    else:
        part = gradient_sum(keep, send)
        back_first, back_second = lat_swaps(back_first, back_second)
        one, two = back_first[2:].astype(F32), back_second[2:].astype(F32)
        rows = jnp.stack([jnp.where(odd == 1, one, two), jnp.where(odd == 1, two, one)])
        side = (side[0].reshape(rows.shape).astype(F32) + rows).astype(BF16)
        lon_share = [lon_return(side.reshape(four.shape))]
        sums = plane_sum(part)
        finish = finish_rows_kernel
    layer_out, input_grad = call(
        "input", lambda *refs: input_kernel(pair, *refs),
        [shape(tokens_in.shape), shape(tokens_in.shape)], [],
        [dkv, back_first, back_second, gq, tok, mixed] + lon_share + weights, [],
        [cotangent, tokens_in, ocean_mask], [grid, grid, mask, DMAS((3,))], 24, flops=2 * 256 * 512 * 1536,
    )
    qkv_grad, out_grad, gain_grad = call(
        "finish", finish,
        [shape((128, 3 * D), F32), shape((128, D), F32), shape((1, 128), F32)], [],
        [*sums, wqkv, gain], [], [], [], 16,
    )
    return layer_out, input_grad, qkv_grad, out_grad, gain_grad.reshape(128)


def solution(mesh):
    placed = (
        P("lev", "lat", "lon", None),
        P("lev", "lat", "lon", None),
        P(),
        P(),
        P(),
        P("lev", "lat", "lon"),
    )
    return jax.shard_map(
        on_device,
        mesh=mesh,
        in_specs=placed,
        out_specs=(
            P("lev", "lat", "lon", None),
            P("lev", "lat", "lon", None),
            P("lev", None),
            P("lev", None),
            P("lev"),
        ),
        check_vma=False,
    )
```

```python
import jax
import jax.numpy as jnp
from jax import lax
from jax.experimental import pallas as pl
from jax.experimental.pallas import tpu as pltpu
from jax.sharding import PartitionSpec as P

HEADS = 8
WIN = 8
AREA = WIN * WIN
D = 512
HEAD_DIM = D // HEADS
GROUP = 256
GROUP_HEADS = GROUP // HEAD_DIM
GROUPS = D // GROUP
KEYS = 8 * AREA
LAND = 1000.0
NEVER = -1e9
FAR = 1e30
F32 = jnp.float32
BF16 = jnp.bfloat16
EXACT = lax.Precision.HIGHEST


def dot(a, b, ca, cb, precision=None):
    return lax.dot_general(
        a, b, (((ca,), (cb,)), ((), ())), preferred_element_type=F32, precision=precision
    )


def iota(shape, dim):
    return lax.broadcasted_iota(jnp.int32, shape, dim)


def window_of(grid, w):
    r, c = divmod(w, 2)
    part = grid[r * WIN : (r + 1) * WIN, c * WIN : (c + 1) * WIN, :]
    return part.reshape(AREA, grid.shape[-1])


def grid_of(windows):
    rows = []
    for r in range(2):
        parts = [windows[2 * r + c].reshape(WIN, WIN, -1) for c in range(2)]
        rows.append(jnp.concatenate(parts, axis=1))
    return jnp.concatenate(rows, axis=0)


def token_mask(mask):
    t = iota((4 * AREA, 2 * WIN), 0)
    lane = iota((4 * AREA, 2 * WIN), 1)
    w, i, j = t // AREA, (t % AREA) // WIN, t % WIN
    pick_row = (lane == WIN * (w // 2) + i).astype(F32)
    pick_col = (lane == WIN * (w % 2) + j).astype(F32)
    rows = dot(pick_row, mask, 1, 0)
    return jnp.sum(rows * pick_col, axis=1, keepdims=True)


def norm_rows(x):
    center = x - jnp.mean(x, axis=-1, keepdims=True)
    spread = jnp.mean(center * center, axis=-1, keepdims=True)
    scaling = lax.rsqrt(spread + 1e-05)
    return center * scaling, scaling


def head_blocks():
    row = iota((GROUP, GROUP), 0) // HEAD_DIM
    col = iota((GROUP, GROUP), 1) // HEAD_DIM
    return (row == col).astype(F32)


def stack_heads(part, blocks):
    return jnp.concatenate([part] * GROUP_HEADS, axis=0) * blocks.astype(part.dtype)


def unstack_heads(full, blocks):
    kept = full * blocks
    return sum(kept[h * AREA : (h + 1) * AREA] for h in range(GROUP_HEADS))


def lanes(g):
    return slice(g * GROUP, (g + 1) * GROUP)


def lat_side(row):
    return (row + lax.axis_index("lat") + 1) % 2


def load(pairs, sems):
    copies = [pltpu.make_async_copy(a, b, sems.at[k]) for k, (a, b) in enumerate(pairs)]
    for copy in copies:
        copy.start()
    return copies


def wait(copies):
    for copy in copies:
        copy.wait()


def prep_kernel(
    x_hbm, mask_hbm, all_ref, first_ref, second_ref, x_ref, mask_ref, sems
):
    copies = load(((mask_hbm, mask_ref), (x_hbm, x_ref)), sems)
    copies[0].wait()
    ocean = token_mask(mask_ref[0].astype(F32))
    copies[1].wait()
    x = x_ref[0].astype(F32)
    parts = []
    for w in range(4):
        part = jnp.where(ocean[w * AREA : (w + 1) * AREA] > 0.5, window_of(x, w), LAND)
        parts.append(part.astype(BF16))
        all_ref[w] = parts[w]
    odd = lax.axis_index("lat") % 2 == 1
    for c in range(2):
        first_ref[c] = jnp.where(odd, parts[c], parts[2 + c])
        second_ref[c] = jnp.where(odd, parts[2 + c], parts[c])


def land_bias(tokens):
    first = (iota((8, D), 1) == 0).astype(BF16)
    picked = dot(first, tokens, 1, 1)[:1]
    return jnp.where(picked > 0.5 * LAND, NEVER, 0.0)


def hidden_of(tokens, gain_ref):
    normed, _ = norm_rows(tokens.astype(F32))
    return (normed * gain_ref[...]).astype(BF16)


def write_block(tokens, wqkv_ref, gain_ref, q_ref, kv_ref, hid_ref, bias_ref, info_ref):
    hidden = hidden_of(tokens, gain_ref)
    hid_ref[: 4 * AREA] = hidden
    projected = dot(hidden, wqkv_ref[...], 1, 0).astype(BF16)
    q_ref[...] = (projected[:, :D] * BF16(HEAD_DIM ** -0.5)).reshape(4, AREA, D)
    kv_ref[:4] = projected[:, D:].reshape(4, AREA, 2 * D)
    row = land_bias(tokens)
    alive = []
    for w in range(4):
        part = row[:, w * AREA : (w + 1) * AREA]
        bias_ref[w] = jnp.broadcast_to(part, (8, AREA))
        alive.append((jnp.max(part) > 0.5 * NEVER).astype(jnp.int32))
        info_ref[1 + w] = alive[w]
    info_ref[0] = jnp.where(
        alive[3] == 0, 3, jnp.where(alive[2] == 0, 2, jnp.where(alive[1] == 0, 1, 0))
    )


def own_kernel(
    tok_ref, wqkv_ref, gain_ref, cot_hbm, mask_hbm,
    q_ref, kv_ref, hid_ref, gb_ref, bias_ref, info_ref, cot_ref, mask_ref, sems,
):
    copies = load(((mask_hbm, mask_ref), (cot_hbm, cot_ref)), sems)
    tokens = tok_ref[...].reshape(4 * AREA, D)
    write_block(tokens, wqkv_ref, gain_ref, q_ref, kv_ref, hid_ref, bias_ref, info_ref)
    wait(copies)
    ocean = token_mask(mask_ref[0].astype(F32))
    cot = cot_ref[0].astype(F32)
    for w in range(4):
        gb_ref[w] = (window_of(cot, w) * ocean[w * AREA : (w + 1) * AREA]).astype(BF16)


def lat_block(first_ref, second_ref, wkv_ref, gain_ref, kv_ref, hid_ref, bias_ref, at):
    lat, lat_count = lax.axis_index("lat"), lax.axis_size("lat")
    odd = lat % 2 == 1
    first_ok = jnp.logical_or(odd, lat < lat_count - 1)
    second_ok = jnp.where(odd, lat_count - 1 - lat, lat) > 0
    parts = [first_ref[0], first_ref[1], second_ref[0], second_ref[1]]
    tokens = jnp.concatenate(parts, axis=0)
    hidden = hidden_of(tokens, gain_ref)
    hid_ref[at * AREA : (at + 4) * AREA] = hidden
    kv_ref[at : at + 4] = dot(hidden, wkv_ref[...], 1, 0).astype(BF16).reshape(4, AREA, 2 * D)
    row = land_bias(tokens)
    for k in range(4):
        part = row[:, k * AREA : (k + 1) * AREA]
        part = jnp.where(first_ok if k < 2 else second_ok, part, NEVER)
        bias_ref[at + k] = jnp.broadcast_to(part, (8, AREA))


def near_kernel(
    lon_ref, first_ref, second_ref, wqkv_ref, gain_ref, q_ref, kv_ref, hid_ref, bias_ref, info_ref
):
    tokens = lon_ref[...].reshape(4 * AREA, D)
    write_block(tokens, wqkv_ref, gain_ref, q_ref, kv_ref, hid_ref, bias_ref, info_ref)
    lat_block(first_ref, second_ref, wqkv_ref.at[:, D:], gain_ref, kv_ref, hid_ref, bias_ref, 4)


def main_kernel(block, last, *refs):
    refs = list(refs)
    take = lambda n: [refs.pop(0) for _ in range(n)]
    info_ref, infon_ref = take(2)
    wqkv_ref, wout_ref, gain_ref, q, gb = take(5)
    if block == 0:
        first_ref, second_ref, kv_own, kv_near, hid_own, hid_near, bias_own, bias_near = take(8)
    else:
        kv, bias, _ = take(3)
    acc, mixed, gq = take(3)
    if block == 0:
        hid, kv, bias = take(3)
    if last:
        dkv, back1_ref, back2_ref = take(3)
        side_ref = None if block else take(1)[0]
    gm, kcat, *sems = refs
    wkv_ref = wqkv_ref.at[:, D:]
    if block == 0:
        pairs = (
            (kv_own, kv.at[:4]), (kv_near, kv.at[4:12]),
            (hid_own, hid.at[: 4 * AREA]), (hid_near, hid.at[4 * AREA : 12 * AREA]),
            (bias_own, bias.at[:4]), (bias_near, bias.at[4:12]),
        )
        copies = load(pairs, sems[0])
        acc[...] = jnp.zeros_like(acc)
        lat_block(first_ref, second_ref, wkv_ref, gain_ref, kv, hid, bias, 12)
        wait(copies)
    mixed[...] = jnp.zeros_like(mixed)
    gq[...] = jnp.zeros_like(gq)
    blocks = head_blocks()
    gm[...] = dot(gb[...].reshape(4 * AREA, D), wout_ref[...], 1, 1).astype(BF16).reshape(gm.shape)
    info = infon_ref if block else info_ref

    def window_at(slot):
        return slot + (slot >= info[0]).astype(jnp.int32)

    def attend(slot, all_keys, all_values, with_out, with_query):
        at = window_at(slot)

        @pl.when(info[1 + at] > 0)
        def _():
            r, c = at // 2, at % 2
            mine, other, side = 4 * block, 4 * (1 - block), 2 * lat_side(r)
            near = [mine + window_at(k) for k in range(3)] + [8 + mine + side, 9 + mine + side]
            away = [other + 1 - c, other + 3 - c, 8 + other + side + 1 - c]
            places = away + near if block else near + away
            few = 3 if block else 5
            key_count, value_count = 8 if all_keys else few, 8 if all_values else few
            for k in range(8):
                kcat[k * AREA : (k + 1) * AREA] = kv[places[k]]
            bias_row = jnp.concatenate([bias[place][:1] for place in places], axis=1)
            spans = [slice(D + g * GROUP, D + (g + 1) * GROUP) for g in range(GROUPS)]
            both = range(GROUPS)
            q_stack = [stack_heads(q[at, :, lanes(g)], blocks) for g in both]
            gm_stack = [stack_heads(gm[at, :, lanes(g)], blocks) for g in both]
            scores = [dot(q_stack[g], kcat[:, lanes(g)], 1, 1) + bias_row for g in both]
            grad_probs = [dot(gm_stack[g], kcat[:, spans[g]], 1, 1) for g in both]
            weights = [jnp.exp(x - jnp.max(x, axis=1, keepdims=True)) for x in scores]
            inverse = [1.0 / jnp.sum(x, axis=1, keepdims=True) for x in weights]
            low = [(x * y).astype(BF16) for x, y in zip(weights, inverse)]
            delta = [jnp.sum(weights[g] * grad_probs[g], axis=1, keepdims=True) * inverse[g] for g in both]
            grad_scores = [
                (weights[g] * ((grad_probs[g] - delta[g]) * inverse[g])).astype(BF16) for g in both
            ]
            if with_out:
                out = [unstack_heads(dot(low[g], kcat[:, spans[g]], 1, 0), blocks) for g in both]
            if with_query:
                grad = [unstack_heads(dot(grad_scores[g], kcat[:, lanes(g)], 1, 0), blocks) for g in both]
            grad_keys = [dot(grad_scores[g][:, : key_count * AREA], q_stack[g], 0, 0) for g in both]
            grad_values = [dot(low[g][:, : value_count * AREA], gm_stack[g], 0, 0) for g in both]
            for g in both:
                if with_out:
                    mixed[at, :, lanes(g)] = out[g].astype(BF16)
                if with_query:
                    gq[at, :, lanes(g)] = (grad[g] * HEAD_DIM ** -0.5).astype(BF16)
                for k in range(8):
                    rows = slice(k * AREA, (k + 1) * AREA)
                    if k < key_count:
                        acc[places[k], :, lanes(g)] += grad_keys[g][rows]
                    if k < value_count:
                        acc[places[k], :, spans[g]] += grad_values[g][rows]

    def sweep(*wanted):
        def step(slot, carry):
            attend(slot, *wanted)
            return carry

        lax.fori_loop(0, 3, step, 0)

    if block == 0 and last:
        sweep(True, True, True, True)
    else:
        lon = lax.axis_index("lon")
        pl.when(lon == 0)(lambda: sweep(True, False, block == 0, True))
        pl.when(lon == 1)(lambda: sweep(False, True, True, block == 0))
    if not last:
        return
    dkv[...] = acc[...].astype(BF16)
    near = dkv[8:12] if block else dkv[4:]
    shares = dot(near.reshape(-1, 2 * D), wkv_ref[...], 1, 1).astype(BF16).reshape(-1, AREA, D)
    if block:
        back1_ref[...] = shares[:2]
        back2_ref[...] = shares[2:4]
    else:
        side_ref[...] = shares[:4]
        for ref, at in ((back1_ref, 4), (back2_ref, 6)):
            ref[:2] = shares[at : at + 2]
            ref[2:] = shares[at + 4 : at + 6]


def sums_kernel(pair, other, hid, dkv, *refs):
    held = [refs[k : k + 3] for k in range(0, len(refs) - 1, 3)]
    to = refs[-1]
    flat = lambda ref: ref[...].reshape(4 * AREA, D)
    lev = lax.axis_index("lev")

    def columns(rel):
        return pl.ds(pl.multiple_of((lev ^ rel) * 128, 128), 128)

    def grad_part(at, width):
        return dkv[:, :, at : at + width].reshape(16 * AREA, width)

    def query_sum(rel):
        parts = [
            dot(hid[4 * b * AREA : 4 * (b + 1) * AREA, columns(rel)], flat(gq), 0, 0)
            for b, (gq, _, _) in enumerate(held)
        ]
        return sum(parts[1:], parts[0])

    def out_sum(rel):
        parts = [
            dot(mixed[:, :, columns(rel)].reshape(4 * AREA, 128), flat(gb), 0, 0) for _, mixed, gb in held
        ]
        return sum(parts[1:], parts[0])

    if pair:
        odd, lon = lax.axis_index("lat") % 2, lax.axis_index("lon")

        def put(rel, at, value):
            value = value.astype(BF16)
            for k in range(2):
                to[rel // 2, k ^ odd, :, at : at + D] = value[k * 64 : (k + 1) * 64]

        @pl.when(lon == 0)
        def _():
            for rel in (other, 2 + other):
                put(rel, 0, query_sum(rel))
                put(rel, D, dot(hid[:, columns(rel)], grad_part(0, D), 0, 0))

        @pl.when(lon == 1)
        def _():
            for rel in (other, 2 + other):
                put(rel, 0, out_sum(rel))
                put(rel, D, dot(hid[:, columns(rel)], grad_part(D, D), 0, 0))

    else:
        for rel in (other, 2 + other):
            to[rel // 2, :, :D] = query_sum(rel).astype(BF16)
            to[rel // 2, :, D : 2 * D] = out_sum(rel).astype(BF16)
            to[rel // 2, :, 2 * D :] = dot(hid[:, columns(rel)], grad_part(0, 2 * D), 0, 0).astype(BF16)


def split_kernel(keep_ref, come_ref, far_ref, lat_ref, lev_ref, own_ref):
    for k, ref in enumerate((own_ref, lat_ref, lev_ref, far_ref)):
        total = keep_ref[k // 2, k % 2].astype(F32) + come_ref[k // 2, k % 2].astype(F32)
        ref[...] = total.astype(ref.dtype)


def input_kernel(pair, dkv, back1_ref, back2_ref, gq, tok_ref, mixed, *rest):
    refs = rest if pair else rest[1:]
    wqkv_ref, wout_ref, gain_ref, cot_hbm, x_hbm, mask_hbm, out_ref, ing_ref = refs[:8]
    cot_ref, x_ref, mask_ref, sems = refs[8:]
    copies = load(((x_hbm, x_ref), (mask_hbm, mask_ref), (cot_hbm, cot_ref)), sems)
    odd = lax.axis_index("lat") % 2 == 1
    shares = []
    for w in range(4):
        one, two = back1_ref[w % 2].astype(F32), back2_ref[w % 2].astype(F32)
        share = jnp.where(odd, one, two) if w < 2 else jnp.where(odd, two, one)
        shares.append(share if pair else share + rest[0][w].astype(F32))
    normed, scaling = norm_rows(tok_ref[...].reshape(4 * AREA, D).astype(F32))
    wait(copies)
    ocean = token_mask(mask_ref[0].astype(F32))
    added = (dot(mixed[:4].reshape(4 * AREA, D), wout_ref[...], 1, 0) * ocean).reshape(4, AREA, D)
    out_ref[0] = (x_ref[0].astype(F32) + grid_of([added[w] for w in range(4)])).astype(BF16)
    grad_hidden = jnp.concatenate(shares, axis=0)
    grad_hidden = grad_hidden + dot(gq[:4].reshape(4 * AREA, D), wqkv_ref[:, :D], 1, 1)
    grad_hidden = grad_hidden + dot(dkv[:4].reshape(4 * AREA, 2 * D), wqkv_ref[:, D:], 1, 1)
    scaled = grad_hidden * gain_ref[...]
    correction = (
        scaled
        - jnp.mean(scaled, axis=-1, keepdims=True)
        - normed * jnp.mean(scaled * normed, axis=-1, keepdims=True)
    )
    added = (scaling * correction).reshape(4, AREA, D)
    ing_ref[0] = (cot_ref[0].astype(F32) + grid_of([added[w] for w in range(4)])).astype(BF16)


def gain_row(wqkv_ref, gain_ref, qkv_ref):
    at = pl.ds(pl.multiple_of(lax.axis_index("lev") * 128, 128), 128)
    product = wqkv_ref[at, :].astype(F32) * qkv_ref[...]
    return dot(jnp.ones((8, 3 * D), F32), product, 1, 1, EXACT)[:1] / gain_ref[:, at]


def finish_rows_kernel(
    own_ref, far_ref, wqkv_ref, gain_ref, qkv_ref, out_ref, gg_ref
):
    half = own_ref.shape[0]
    first = lax.axis_index("lon") % 2 == 0
    own, far = own_ref[...], far_ref[...]
    for k in range(2):
        value = (jnp.where(first, own, far) if k == 0 else jnp.where(first, far, own)).astype(F32)
        rows = slice(k * half, (k + 1) * half)
        qkv_ref[rows, :D] = value[:, :D]
        qkv_ref[rows, D:] = value[:, 2 * D :]
        out_ref[rows] = value[:, D : 2 * D]
    gg_ref[...] = gain_row(wqkv_ref, gain_ref, qkv_ref)


def finish_pair_kernel(
    own_ref, lat_ref, lon_ref, far_ref, wqkv_ref, gain_ref, qkv_ref, out_ref, gg_ref
):
    odd = lax.axis_index("lat") % 2 == 1
    first = lax.axis_index("lon") == 0
    for k in range(2):
        rows = slice(64 * k, 64 * k + 64)
        mine = odd if k == 1 else jnp.logical_not(odd)
        near = jnp.where(mine, own_ref[...], lat_ref[...]).astype(F32)
        away = jnp.where(mine, lon_ref[...], far_ref[...]).astype(F32)
        low, high = jnp.where(first, near, away), jnp.where(first, away, near)
        qkv_ref[rows, : 2 * D] = low
        out_ref[rows] = high[:, :D]
        qkv_ref[rows, 2 * D :] = high[:, D:]
    gg_ref[...] = gain_row(wqkv_ref, gain_ref, qkv_ref)


SMEM = pl.BlockSpec(memory_space=pltpu.SMEM)
VMEM = pl.BlockSpec(memory_space=pltpu.VMEM)
ANY = pl.BlockSpec(memory_space=pl.ANY)
HBM = pl.BlockSpec(memory_space=pltpu.HBM)
DMAS = pltpu.SemaphoreType.DMA


def call(
    name, kernel, outs, scalars, arrays, loose, far, scratch, mebibytes, flops=0, out_specs=None, aliases=None
):
    moved = sum(a.size * a.dtype.itemsize for a in (*arrays, *loose, *far, *outs))
    specs = [SMEM] * len(scalars) + [VMEM] * len(arrays) + [ANY] * len(loose) + [HBM] * len(far)
    return pl.pallas_call(
        kernel,
        out_shape=outs,
        in_specs=specs,
        out_specs=out_specs or [VMEM] * len(outs),
        scratch_shapes=list(scratch),
        input_output_aliases=aliases or {},
        compiler_params=pltpu.CompilerParams(vmem_limit_bytes=mebibytes * 1024 * 1024),
        cost_estimate=pl.CostEstimate(flops=flops, bytes_accessed=moved, transcendentals=0),
        name=name,
    )(*scalars, *arrays, *loose, *far)


def shape(dims, dtype=BF16):
    return jax.ShapeDtypeStruct(dims, dtype)


def ring(count, step, periodic):
    return [
        (i, (i + step) % count) for i in range(count) if periodic or 0 <= i + step < count
    ]


def lon_halo(own):
    count = lax.axis_size("lon")
    if count == 2:
        return lax.ppermute(own, "lon", [(0, 1), (1, 0)])
    left = lax.ppermute(own[1::2], "lon", ring(count, 1, True))
    right = lax.ppermute(own[0::2], "lon", ring(count, -1, True))
    return jnp.stack([right, left], axis=1).reshape(own.shape)


def lon_return(side):
    count = lax.axis_size("lon")
    if count == 2:
        return lax.ppermute(side, "lon", [(0, 1), (1, 0)])
    from_left = lax.ppermute(side[0::2], "lon", ring(count, 1, True))
    from_right = lax.ppermute(side[1::2], "lon", ring(count, -1, True))
    return jnp.stack([from_left, from_right], axis=1).reshape(side.shape)


def lat_swap(value, start):
    pairs = [(i, i + 1) for i in range(start, lax.axis_size("lat") - 1, 2)]
    return lax.ppermute(value, "lat", pairs + [(b, a) for a, b in pairs])


def lat_swaps(first, second):
    return lat_swap(first, 0), lat_swap(second, 1)


def corner_swap(value, start):
    count = lax.axis_size("lat")
    pairs = [(i, i + 1) for i in range(start, count - 1, 2)]
    pairs = [(a + k * count, b + (1 - k) * count) for a, b in pairs for k in range(2)]
    return lax.ppermute(value, ("lon", "lat"), pairs + [(b, a) for a, b in pairs])


def swap(value, axis, bit):
    return lax.ppermute(value, axis, [(i, i ^ bit) for i in range(lax.axis_size(axis))])


def halve(parts, axis, bit):
    at = (lax.axis_index(axis) // bit) % 2
    sent = lax.dynamic_index_in_dim(parts, 1 - at, 0, False).astype(BF16)
    kept = lax.dynamic_index_in_dim(parts, at, 0, False)
    return kept + swap(sent, axis, bit).astype(F32)


def rejoin(half, axis, bit):
    first = (lax.axis_index(axis) // bit) % 2 == 0
    far = swap(half, axis, bit)
    return jnp.concatenate([jnp.where(first, half, far), jnp.where(first, far, half)], axis=0)


def bits(axis):
    count = lax.axis_size(axis)
    return [1 << k for k in range(count.bit_length() - 1)]


def gradient_sum(keep, send):
    width = keep.shape[2] // 2
    total = keep.astype(F32) + swap(send, "lev", 1).astype(F32)
    part_a = total[0, :, :width] + swap(total[1, :, :width].astype(BF16), "lev", 2).astype(F32)
    part_b = total[:, :, width:]
    for bit in bits("lon"):
        rows = part_a.shape[0] // 2
        part_a = halve(part_a.reshape(2, rows, width), "lon", bit)
        part_b = halve(jnp.swapaxes(part_b.reshape(2, 2, rows, width), 0, 1), "lon", bit)
    part_b = part_b[0] + swap(part_b[1].astype(BF16), "lev", 2).astype(F32)
    return jnp.concatenate([part_a, part_b], axis=1)


def plane_sum(part):
    for bit in bits("lat"):
        part = halve(part.reshape(2, part.shape[0] // 2, -1), "lat", bit)
    part = part.astype(BF16)
    for bit in reversed(bits("lat")):
        part = rejoin(part, "lat", bit)
    for bit in reversed(bits("lon")[1:]):
        part = rejoin(part, "lon", bit)
    return part, swap(part, "lon", 1)


def pair_sum(keep, send):
    count = lax.axis_size("lat")
    width = keep.shape[-1]
    come = swap(send, "lev", 1)
    piece = shape(keep.shape[2:])
    to_far, to_lat, to_lev, own = call(
        "split", split_kernel, [piece, piece, piece, shape(piece.shape, F32)], [], [keep, come], [], [], [], 8
    )
    from_far = lax.ppermute(to_far, ("lat", "lev"), [(i, i ^ 6) for i in range(4 * count)])
    from_lat = swap(to_lat, "lat", 1)
    from_lev = swap(to_lev, "lev", 2)
    own = own + from_lev.astype(F32) + from_lat.astype(F32) + from_far.astype(F32)
    return own.astype(BF16)


def lat_sum(own):
    for bit in bits("lat")[1:]:
        own = (own.astype(F32) + swap(own, "lat", bit).astype(F32)).astype(BF16)
    return own


def pair_spread(own):
    count = lax.axis_size("lat")
    by_far = lax.ppermute(own, ("lon", "lat"), [(i, i ^ (count + 1)) for i in range(2 * count)])
    return own, swap(own, "lat", 1), swap(own, "lon", 1), by_far


def on_device(tokens_in, cotangent, qkv_weight, out_weight, norm_gain, ocean_mask):
    pair = lax.axis_size("lon") == 2
    gain = norm_gain.reshape(1, D)
    half = shape((2, AREA, D))
    four = shape((4, AREA, D))
    wide = shape((4, AREA, 2 * D))
    info_shape = shape((8,), jnp.int32)
    vmem = lambda *dims: pltpu.VMEM(dims, BF16)
    grid = vmem(*tokens_in.shape)
    mask = pltpu.VMEM(ocean_mask.shape, jnp.int32)
    tok, tok_first, tok_second = call(
        "prep", prep_kernel, [four, half, half], [], [], [], [tokens_in, ocean_mask],
        [grid, mask, DMAS((2,))], 8, flops=10 ** 10,
    )
    tok_lon = lon_halo(tok)
    odd = lax.axis_index("lat") % 2
    sides = tok_first, tok_second
    tok_first, tok_second = lat_swaps(tok_first, tok_second)
    q, kv, hid, gb, bias, info = call(
        "own", own_kernel,
        [four, wide, shape((4 * AREA, D)), four, shape((4, 8, AREA), F32), info_shape],
        [], [tok, qkv_weight, gain], [], [cotangent, ocean_mask], [grid, mask, DMAS((2,))], 16,
        flops=2 * 256 * 512 * 1536, out_specs=[VMEM] * 5 + [SMEM],
    )
    wqkv, wout = qkv_weight, out_weight
    if pair:
        sides, gb = lax.optimization_barrier((sides, gb))
        corner_first, corner_second = corner_swap(sides[0], 0), corner_swap(sides[1], 1)
        gb_near = lon_halo(gb)
    else:
        rows = tok_lon.reshape(2, 2, AREA, D)
        corner_first, corner_second = lat_swaps(
            lax.dynamic_index_in_dim(rows, 1 - odd, 0, False),
            lax.dynamic_index_in_dim(rows, odd, 0, False),
        )
    q_near, kv_near, hid_near, bias_near, info_near = call(
        "near", near_kernel,
        [four, shape((8, AREA, 2 * D)), shape((8 * AREA, D)), shape((8, 8, AREA), F32), info_shape],
        [], [tok_lon, tok_first, tok_second, wqkv, gain], [], [], [], 20,
        flops=2 * 512 * 512 * 1280, out_specs=[VMEM] * 4 + [SMEM],
    )
    all_shape, all32 = shape((16, AREA, 2 * D)), shape((16, AREA, 2 * D), F32)
    back = shape((2 if pair else 4, AREA, D))
    ends = [all_shape, back, back] + ([] if pair else [four])
    weights = [wqkv, wout, gain]
    scratch = [vmem(4, AREA, D), vmem(KEYS, 2 * D)]
    flops = 3 * 12 * 2 * 512 * 256 * 256
    acc, mixed, gq, hid_all, kv_all, bias_all, *rest = call(
        "main", lambda *refs: main_kernel(0, not pair, *refs),
        [all32, four, four, shape((16 * AREA, D)), all_shape, shape((16, 8, AREA), F32)]
        + ([] if pair else ends),
        [info, info_near], weights + [q, gb, corner_first, corner_second],
        [kv, kv_near, hid, hid_near, bias, bias_near], [], scratch + [DMAS((6,))], 28, flops=flops,
    )
    parts = [gq, mixed, gb]
    if pair:
        _, mixed_near, gq_near, *rest = call(
            "other", lambda *refs: main_kernel(1, True, *refs), [all32, four, four] + ends,
            [info, info_near], weights + [q_near, gb_near, kv_all, bias_all, acc], [], [],
            scratch, 28, flops=flops, aliases={9: 0},
        )
        parts += [gq_near, mixed_near, gb_near]
    dkv, back_first, back_second, *side = rest
    share = shape((2, 2, 64, 2 * D) if pair else (2, 128, 4 * D))
    send, keep = [
        call(
            name, lambda *refs, other=other: sums_kernel(pair, other, *refs), [share], [],
            [hid_all, dkv] + parts, [], [], [], 24, flops=1024 * 512 * 1024,
        )[0]
        for name, other in (("sent", 1), ("kept", 0))
    ]
    if pair:
        total = pair_sum(keep, send)
        back_second = lat_swap(back_second, 1)
        total, back_first, back_second = lax.optimization_barrier((total, back_first, back_second))
        back_first = lat_swap(back_first, 0)
        total = lat_sum(total)
        total, back_first = lax.optimization_barrier((total, back_first))
        sums = pair_spread(total)
        lon_share = []
        finish = finish_pair_kernel
    else:
        part = gradient_sum(keep, send)
        back_first, back_second = lat_swaps(back_first, back_second)
        one, two = back_first[2:].astype(F32), back_second[2:].astype(F32)
        rows = jnp.stack([jnp.where(odd == 1, one, two), jnp.where(odd == 1, two, one)])
        side = (side[0].reshape(rows.shape).astype(F32) + rows).astype(BF16)
        lon_share = [lon_return(side.reshape(four.shape))]
        sums = plane_sum(part)
        finish = finish_rows_kernel
    layer_out, input_grad = call(
        "input", lambda *refs: input_kernel(pair, *refs),
        [shape(tokens_in.shape), shape(tokens_in.shape)], [],
        [dkv, back_first, back_second, gq, tok, mixed] + lon_share + weights, [],
        [cotangent, tokens_in, ocean_mask], [grid, grid, mask, DMAS((3,))], 24, flops=2 * 256 * 512 * 1536,
    )
    qkv_grad, out_grad, gain_grad = call(
        "finish", finish,
        [shape((128, 3 * D), F32), shape((128, D), F32), shape((1, 128), F32)], [],
        [*sums, wqkv, gain], [], [], [], 16,
    )
    return layer_out, input_grad, qkv_grad, out_grad, gain_grad.reshape(128)


def solution(mesh):
    placed = (
        P("lev", "lat", "lon", None),
        P("lev", "lat", "lon", None),
        P(),
        P(),
        P(),
        P("lev", "lat", "lon"),
    )
    return jax.shard_map(
        on_device,
        mesh=mesh,
        in_specs=placed,
        out_specs=(
            P("lev", "lat", "lon", None),
            P("lev", "lat", "lon", None),
            P("lev", None),
            P("lev", None),
            P("lev"),
        ),
        check_vma=False,
    )
```

```python
import jax
import jax.numpy as jnp
from jax import lax
from jax.experimental import pallas as pl
from jax.experimental.pallas import tpu as pltpu
from jax.sharding import PartitionSpec as P

HEADS = 8
WIN = 8
AREA = WIN * WIN
D = 512
HEAD_DIM = D // HEADS
GROUP = 256
GROUP_HEADS = GROUP // HEAD_DIM
GROUPS = D // GROUP
KEYS = 8 * AREA
LAND = 1000.0
NEVER = -1e9
FAR = 1e30
F32 = jnp.float32
BF16 = jnp.bfloat16
EXACT = lax.Precision.HIGHEST


def dot(a, b, ca, cb, precision=None):
    return lax.dot_general(
        a, b, (((ca,), (cb,)), ((), ())), preferred_element_type=F32, precision=precision
    )


def iota(shape, dim):
    return lax.broadcasted_iota(jnp.int32, shape, dim)


def window_of(grid, w):
    r, c = divmod(w, 2)
    part = grid[r * WIN : (r + 1) * WIN, c * WIN : (c + 1) * WIN, :]
    return part.reshape(AREA, grid.shape[-1])


def grid_of(windows):
    rows = []
    for r in range(2):
        parts = [windows[2 * r + c].reshape(WIN, WIN, -1) for c in range(2)]
        rows.append(jnp.concatenate(parts, axis=1))
    return jnp.concatenate(rows, axis=0)


def token_mask(mask):
    t = iota((4 * AREA, 2 * WIN), 0)
    lane = iota((4 * AREA, 2 * WIN), 1)
    w, i, j = t // AREA, (t % AREA) // WIN, t % WIN
    pick_row = (lane == WIN * (w // 2) + i).astype(F32)
    pick_col = (lane == WIN * (w % 2) + j).astype(F32)
    rows = dot(pick_row, mask, 1, 0)
    return jnp.sum(rows * pick_col, axis=1, keepdims=True)


def norm_rows(x):
    center = x - jnp.mean(x, axis=-1, keepdims=True)
    spread = jnp.mean(center * center, axis=-1, keepdims=True)
    scaling = lax.rsqrt(spread + 1e-05)
    return center * scaling, scaling


def head_blocks():
    row = iota((GROUP, GROUP), 0) // HEAD_DIM
    col = iota((GROUP, GROUP), 1) // HEAD_DIM
    return (row == col).astype(F32)


def stack_heads(part, blocks):
    return jnp.concatenate([part] * GROUP_HEADS, axis=0) * blocks.astype(part.dtype)


def unstack_heads(full, blocks):
    kept = full * blocks
    return sum(kept[h * AREA : (h + 1) * AREA] for h in range(GROUP_HEADS))


def lanes(g):
    return slice(g * GROUP, (g + 1) * GROUP)


def lat_side(row):
    return (row + lax.axis_index("lat") + 1) % 2


def load(pairs, sems):
    copies = [pltpu.make_async_copy(a, b, sems.at[k]) for k, (a, b) in enumerate(pairs)]
    for copy in copies:
        copy.start()
    return copies


def wait(copies):
    for copy in copies:
        copy.wait()


def prep_kernel(
    x_hbm, mask_hbm, all_ref, first_ref, second_ref, x_ref, mask_ref, sems
):
    copies = load(((mask_hbm, mask_ref), (x_hbm, x_ref)), sems)
    copies[0].wait()
    ocean = token_mask(mask_ref[0].astype(F32))
    copies[1].wait()
    x = x_ref[0].astype(F32)
    parts = []
    for w in range(4):
        part = jnp.where(ocean[w * AREA : (w + 1) * AREA] > 0.5, window_of(x, w), LAND)
        parts.append(part.astype(BF16))
        all_ref[w] = parts[w]
    odd = lax.axis_index("lat") % 2 == 1
    for c in range(2):
        first_ref[c] = jnp.where(odd, parts[c], parts[2 + c])
        second_ref[c] = jnp.where(odd, parts[2 + c], parts[c])


def land_bias(tokens):
    first = (iota((8, D), 1) == 0).astype(BF16)
    picked = dot(first, tokens, 1, 1)[:1]
    return jnp.where(picked > 0.5 * LAND, NEVER, 0.0)


def hidden_of(tokens, gain_ref):
    normed, _ = norm_rows(tokens.astype(F32))
    return (normed * gain_ref[...]).astype(BF16)


def write_block(tokens, wqkv_ref, gain_ref, q_ref, kv_ref, hid_ref, bias_ref, info_ref):
    hidden = hidden_of(tokens, gain_ref)
    hid_ref[: 4 * AREA] = hidden
    projected = dot(hidden, wqkv_ref[...], 1, 0).astype(BF16)
    q_ref[...] = (projected[:, :D] * BF16(HEAD_DIM ** -0.5)).reshape(4, AREA, D)
    kv_ref[:4] = projected[:, D:].reshape(4, AREA, 2 * D)
    row = land_bias(tokens)
    alive = []
    for w in range(4):
        part = row[:, w * AREA : (w + 1) * AREA]
        bias_ref[w] = jnp.broadcast_to(part, (8, AREA))
        alive.append((jnp.max(part) > 0.5 * NEVER).astype(jnp.int32))
        info_ref[1 + w] = alive[w]
    info_ref[0] = jnp.where(
        alive[3] == 0, 3, jnp.where(alive[2] == 0, 2, jnp.where(alive[1] == 0, 1, 0))
    )


def own_kernel(
    tok_ref, wqkv_ref, gain_ref, cot_hbm, mask_hbm,
    q_ref, kv_ref, hid_ref, gb_ref, bias_ref, info_ref, cot_ref, mask_ref, sems,
):
    copies = load(((mask_hbm, mask_ref), (cot_hbm, cot_ref)), sems)
    tokens = tok_ref[...].reshape(4 * AREA, D)
    write_block(tokens, wqkv_ref, gain_ref, q_ref, kv_ref, hid_ref, bias_ref, info_ref)
    wait(copies)
    ocean = token_mask(mask_ref[0].astype(F32))
    cot = cot_ref[0].astype(F32)
    for w in range(4):
        gb_ref[w] = (window_of(cot, w) * ocean[w * AREA : (w + 1) * AREA]).astype(BF16)


def lat_block(first_ref, second_ref, wkv_ref, gain_ref, kv_ref, hid_ref, bias_ref, at):
    lat, lat_count = lax.axis_index("lat"), lax.axis_size("lat")
    odd = lat % 2 == 1
    first_ok = jnp.logical_or(odd, lat < lat_count - 1)
    second_ok = jnp.where(odd, lat_count - 1 - lat, lat) > 0
    parts = [first_ref[0], first_ref[1], second_ref[0], second_ref[1]]
    tokens = jnp.concatenate(parts, axis=0)
    hidden = hidden_of(tokens, gain_ref)
    hid_ref[at * AREA : (at + 4) * AREA] = hidden
    kv_ref[at : at + 4] = dot(hidden, wkv_ref[...], 1, 0).astype(BF16).reshape(4, AREA, 2 * D)
    row = land_bias(tokens)
    for k in range(4):
        part = row[:, k * AREA : (k + 1) * AREA]
        part = jnp.where(first_ok if k < 2 else second_ok, part, NEVER)
        bias_ref[at + k] = jnp.broadcast_to(part, (8, AREA))


def near_kernel(
    lon_ref, first_ref, second_ref, wqkv_ref, gain_ref, q_ref, kv_ref, hid_ref, bias_ref, info_ref
):
    tokens = lon_ref[...].reshape(4 * AREA, D)
    write_block(tokens, wqkv_ref, gain_ref, q_ref, kv_ref, hid_ref, bias_ref, info_ref)
    lat_block(first_ref, second_ref, wqkv_ref.at[:, D:], gain_ref, kv_ref, hid_ref, bias_ref, 4)


def main_kernel(block, last, *refs):
    refs = list(refs)
    take = lambda n: [refs.pop(0) for _ in range(n)]
    info_ref, infon_ref = take(2)
    wqkv_ref, wout_ref, gain_ref, q, gb = take(5)
    if block == 0:
        first_ref, second_ref, kv_own, kv_near, hid_own, hid_near, bias_own, bias_near = take(8)
    else:
        kv, bias, _ = take(3)
    acc, mixed, gq = take(3)
    if block == 0:
        hid, kv, bias = take(3)
    if last:
        dkv, back1_ref, back2_ref = take(3)
        side_ref = None if block else take(1)[0]
    gm, kcat, *sems = refs
    wkv_ref = wqkv_ref.at[:, D:]
    if block == 0:
        pairs = (
            (kv_own, kv.at[:4]), (kv_near, kv.at[4:12]),
            (hid_own, hid.at[: 4 * AREA]), (hid_near, hid.at[4 * AREA : 12 * AREA]),
            (bias_own, bias.at[:4]), (bias_near, bias.at[4:12]),
        )
        copies = load(pairs, sems[0])
        acc[...] = jnp.zeros_like(acc)
        lat_block(first_ref, second_ref, wkv_ref, gain_ref, kv, hid, bias, 12)
        wait(copies)
    mixed[...] = jnp.zeros_like(mixed)
    gq[...] = jnp.zeros_like(gq)
    blocks = head_blocks()
    gm[...] = dot(gb[...].reshape(4 * AREA, D), wout_ref[...], 1, 1).astype(BF16).reshape(gm.shape)
    info = infon_ref if block else info_ref

    def window_at(slot):
        return slot + (slot >= info[0]).astype(jnp.int32)

    def attend(slot, all_keys, all_values, with_out, with_query):
        at = window_at(slot)

        @pl.when(info[1 + at] > 0)
        def _():
            r, c = at // 2, at % 2
            mine, other, side = 4 * block, 4 * (1 - block), 2 * lat_side(r)
            near = [mine + window_at(k) for k in range(3)] + [8 + mine + side, 9 + mine + side]
            away = [other + 1 - c, other + 3 - c, 8 + other + side + 1 - c]
            places = away + near if block else near + away
            few = 3 if block else 5
            key_count, value_count = 8 if all_keys else few, 8 if all_values else few
            for k in range(8):
                kcat[k * AREA : (k + 1) * AREA] = kv[places[k]]
            bias_row = jnp.concatenate([bias[place][:1] for place in places], axis=1)
            spans = [slice(D + g * GROUP, D + (g + 1) * GROUP) for g in range(GROUPS)]
            both = range(GROUPS)
            q_stack = [stack_heads(q[at, :, lanes(g)], blocks) for g in both]
            gm_stack = [stack_heads(gm[at, :, lanes(g)], blocks) for g in both]
            scores = [dot(q_stack[g], kcat[:, lanes(g)], 1, 1) + bias_row for g in both]
            grad_probs = [dot(gm_stack[g], kcat[:, spans[g]], 1, 1) for g in both]
            weights = [jnp.exp(x - jnp.max(x, axis=1, keepdims=True)) for x in scores]
            inverse = [1.0 / jnp.sum(x, axis=1, keepdims=True) for x in weights]
            low = [(x * y).astype(BF16) for x, y in zip(weights, inverse)]
            delta = [jnp.sum(weights[g] * grad_probs[g], axis=1, keepdims=True) * inverse[g] for g in both]
            grad_scores = [
                (weights[g] * ((grad_probs[g] - delta[g]) * inverse[g])).astype(BF16) for g in both
            ]
            if with_out:
                out = [unstack_heads(dot(low[g], kcat[:, spans[g]], 1, 0), blocks) for g in both]
            if with_query:
                grad = [unstack_heads(dot(grad_scores[g], kcat[:, lanes(g)], 1, 0), blocks) for g in both]
            grad_keys = [dot(grad_scores[g][:, : key_count * AREA], q_stack[g], 0, 0) for g in both]
            grad_values = [dot(low[g][:, : value_count * AREA], gm_stack[g], 0, 0) for g in both]
            for g in both:
                if with_out:
                    mixed[at, :, lanes(g)] = out[g].astype(BF16)
                if with_query:
                    gq[at, :, lanes(g)] = (grad[g] * HEAD_DIM ** -0.5).astype(BF16)
                for k in range(8):
                    rows = slice(k * AREA, (k + 1) * AREA)
                    if k < key_count:
                        acc[places[k], :, lanes(g)] += grad_keys[g][rows]
                    if k < value_count:
                        acc[places[k], :, spans[g]] += grad_values[g][rows]

    def sweep(*wanted):
        def step(slot, carry):
            attend(slot, *wanted)
            return carry

        lax.fori_loop(0, 3, step, 0)

    if block == 0 and last:
        sweep(True, True, True, True)
    else:
        lon = lax.axis_index("lon")
        pl.when(lon == 0)(lambda: sweep(True, False, block == 0, True))
        pl.when(lon == 1)(lambda: sweep(False, True, True, block == 0))
    if not last:
        return
    dkv[...] = acc[...].astype(BF16)
    near = dkv[8:12] if block else dkv[4:]
    shares = dot(near.reshape(-1, 2 * D), wkv_ref[...], 1, 1).astype(BF16).reshape(-1, AREA, D)
    if block:
        back1_ref[...] = shares[:2]
        back2_ref[...] = shares[2:4]
    else:
        side_ref[...] = shares[:4]
        for ref, at in ((back1_ref, 4), (back2_ref, 6)):
            ref[:2] = shares[at : at + 2]
            ref[2:] = shares[at + 4 : at + 6]


def sums_kernel(pair, other, hid, dkv, *refs):
    held = [refs[k : k + 3] for k in range(0, len(refs) - 1, 3)]
    to = refs[-1]
    flat = lambda ref: ref[...].reshape(4 * AREA, D)
    lev = lax.axis_index("lev")

    def columns(rel):
        return pl.ds(pl.multiple_of((lev ^ rel) * 128, 128), 128)

    def grad_part(at, width):
        return dkv[:, :, at : at + width].reshape(16 * AREA, width)

    def query_sum(rel):
        parts = [
            dot(hid[4 * b * AREA : 4 * (b + 1) * AREA, columns(rel)], flat(gq), 0, 0)
            for b, (gq, _, _) in enumerate(held)
        ]
        return sum(parts[1:], parts[0])

    def out_sum(rel):
        parts = [
            dot(mixed[:, :, columns(rel)].reshape(4 * AREA, 128), flat(gb), 0, 0) for _, mixed, gb in held
        ]
        return sum(parts[1:], parts[0])

    if pair:
        odd, lon = lax.axis_index("lat") % 2, lax.axis_index("lon")

        def put(rel, at, value):
            value = value.astype(BF16)
            for k in range(2):
                to[rel // 2, k ^ odd, :, at : at + D] = value[k * 64 : (k + 1) * 64]

        @pl.when(lon == 0)
        def _():
            for rel in (other, 2 + other):
                put(rel, 0, query_sum(rel))
                put(rel, D, dot(hid[:, columns(rel)], grad_part(0, D), 0, 0))

        @pl.when(lon == 1)
        def _():
            for rel in (other, 2 + other):
                put(rel, 0, out_sum(rel))
                put(rel, D, dot(hid[:, columns(rel)], grad_part(D, D), 0, 0))

    else:
        for rel in (other, 2 + other):
            to[rel // 2, :, :D] = query_sum(rel).astype(BF16)
            to[rel // 2, :, D : 2 * D] = out_sum(rel).astype(BF16)
            to[rel // 2, :, 2 * D :] = dot(hid[:, columns(rel)], grad_part(0, 2 * D), 0, 0).astype(BF16)


def split_kernel(keep_ref, come_ref, far_ref, lat_ref, lev_ref, own_ref):
    for k, ref in enumerate((own_ref, lat_ref, lev_ref, far_ref)):
        total = keep_ref[k // 2, k % 2].astype(F32) + come_ref[k // 2, k % 2].astype(F32)
        ref[...] = total.astype(ref.dtype)


def input_kernel(pair, dkv, back1_ref, back2_ref, gq, tok_ref, mixed, *rest):
    refs = rest if pair else rest[1:]
    wqkv_ref, wout_ref, gain_ref, cot_hbm, x_hbm, mask_hbm, out_ref, ing_ref = refs[:8]
    cot_ref, x_ref, mask_ref, sems = refs[8:]
    copies = load(((x_hbm, x_ref), (mask_hbm, mask_ref), (cot_hbm, cot_ref)), sems)
    odd = lax.axis_index("lat") % 2 == 1
    shares = []
    for w in range(4):
        one, two = back1_ref[w % 2].astype(F32), back2_ref[w % 2].astype(F32)
        share = jnp.where(odd, one, two) if w < 2 else jnp.where(odd, two, one)
        shares.append(share if pair else share + rest[0][w].astype(F32))
    normed, scaling = norm_rows(tok_ref[...].reshape(4 * AREA, D).astype(F32))
    wait(copies)
    ocean = token_mask(mask_ref[0].astype(F32))
    added = (dot(mixed[:4].reshape(4 * AREA, D), wout_ref[...], 1, 0) * ocean).reshape(4, AREA, D)
    out_ref[0] = (x_ref[0].astype(F32) + grid_of([added[w] for w in range(4)])).astype(BF16)
    grad_hidden = jnp.concatenate(shares, axis=0)
    grad_hidden = grad_hidden + dot(gq[:4].reshape(4 * AREA, D), wqkv_ref[:, :D], 1, 1)
    grad_hidden = grad_hidden + dot(dkv[:4].reshape(4 * AREA, 2 * D), wqkv_ref[:, D:], 1, 1)
    scaled = grad_hidden * gain_ref[...]
    correction = (
        scaled
        - jnp.mean(scaled, axis=-1, keepdims=True)
        - normed * jnp.mean(scaled * normed, axis=-1, keepdims=True)
    )
    added = (scaling * correction).reshape(4, AREA, D)
    ing_ref[0] = (cot_ref[0].astype(F32) + grid_of([added[w] for w in range(4)])).astype(BF16)


def gain_row(wqkv_ref, gain_ref, qkv_ref):
    at = pl.ds(pl.multiple_of(lax.axis_index("lev") * 128, 128), 128)
    product = wqkv_ref[at, :].astype(F32) * qkv_ref[...]
    product = sum(product[:, k : k + 128] for k in range(0, 3 * D, 128))
    return dot(jnp.ones((8, 128), F32), product, 1, 1, EXACT)[:1] / gain_ref[:, at]


def finish_rows_kernel(
    own_ref, far_ref, wqkv_ref, gain_ref, qkv_ref, out_ref, gg_ref
):
    half = own_ref.shape[0]
    first = lax.axis_index("lon") % 2 == 0
    own, far = own_ref[...], far_ref[...]
    for k in range(2):
        value = (jnp.where(first, own, far) if k == 0 else jnp.where(first, far, own)).astype(F32)
        rows = slice(k * half, (k + 1) * half)
        qkv_ref[rows, :D] = value[:, :D]
        qkv_ref[rows, D:] = value[:, 2 * D :]
        out_ref[rows] = value[:, D : 2 * D]
    gg_ref[...] = gain_row(wqkv_ref, gain_ref, qkv_ref)


def finish_pair_kernel(
    own_ref, lat_ref, lon_ref, far_ref, wqkv_ref, gain_ref, qkv_ref, out_ref, gg_ref
):
    odd = lax.axis_index("lat") % 2 == 1
    first = lax.axis_index("lon") == 0
    for k in range(2):
        rows = slice(64 * k, 64 * k + 64)
        mine = odd if k == 1 else jnp.logical_not(odd)
        near = jnp.where(mine, own_ref[...], lat_ref[...]).astype(F32)
        away = jnp.where(mine, lon_ref[...], far_ref[...]).astype(F32)
        low, high = jnp.where(first, near, away), jnp.where(first, away, near)
        qkv_ref[rows, : 2 * D] = low
        out_ref[rows] = high[:, :D]
        qkv_ref[rows, 2 * D :] = high[:, D:]
    gg_ref[...] = gain_row(wqkv_ref, gain_ref, qkv_ref)


SMEM = pl.BlockSpec(memory_space=pltpu.SMEM)
VMEM = pl.BlockSpec(memory_space=pltpu.VMEM)
ANY = pl.BlockSpec(memory_space=pl.ANY)
HBM = pl.BlockSpec(memory_space=pltpu.HBM)
DMAS = pltpu.SemaphoreType.DMA


def call(
    name, kernel, outs, scalars, arrays, loose, far, scratch, mebibytes, flops=0, out_specs=None, aliases=None
):
    moved = sum(a.size * a.dtype.itemsize for a in (*arrays, *loose, *far, *outs))
    specs = [SMEM] * len(scalars) + [VMEM] * len(arrays) + [ANY] * len(loose) + [HBM] * len(far)
    return pl.pallas_call(
        kernel,
        out_shape=outs,
        in_specs=specs,
        out_specs=out_specs or [VMEM] * len(outs),
        scratch_shapes=list(scratch),
        input_output_aliases=aliases or {},
        compiler_params=pltpu.CompilerParams(vmem_limit_bytes=mebibytes * 1024 * 1024),
        cost_estimate=pl.CostEstimate(flops=flops, bytes_accessed=moved, transcendentals=0),
        name=name,
    )(*scalars, *arrays, *loose, *far)


def shape(dims, dtype=BF16):
    return jax.ShapeDtypeStruct(dims, dtype)


def ring(count, step, periodic):
    return [
        (i, (i + step) % count) for i in range(count) if periodic or 0 <= i + step < count
    ]


def lon_halo(own):
    count = lax.axis_size("lon")
    if count == 2:
        return lax.ppermute(own, "lon", [(0, 1), (1, 0)])
    left = lax.ppermute(own[1::2], "lon", ring(count, 1, True))
    right = lax.ppermute(own[0::2], "lon", ring(count, -1, True))
    return jnp.stack([right, left], axis=1).reshape(own.shape)


def lon_return(side):
    count = lax.axis_size("lon")
    if count == 2:
        return lax.ppermute(side, "lon", [(0, 1), (1, 0)])
    from_left = lax.ppermute(side[0::2], "lon", ring(count, 1, True))
    from_right = lax.ppermute(side[1::2], "lon", ring(count, -1, True))
    return jnp.stack([from_left, from_right], axis=1).reshape(side.shape)


def lat_swap(value, start):
    pairs = [(i, i + 1) for i in range(start, lax.axis_size("lat") - 1, 2)]
    return lax.ppermute(value, "lat", pairs + [(b, a) for a, b in pairs])


def lat_swaps(first, second):
    return lat_swap(first, 0), lat_swap(second, 1)


def corner_swap(value, start):
    count = lax.axis_size("lat")
    pairs = [(i, i + 1) for i in range(start, count - 1, 2)]
    pairs = [(a + k * count, b + (1 - k) * count) for a, b in pairs for k in range(2)]
    return lax.ppermute(value, ("lon", "lat"), pairs + [(b, a) for a, b in pairs])


def swap(value, axis, bit):
    return lax.ppermute(value, axis, [(i, i ^ bit) for i in range(lax.axis_size(axis))])


def halve(parts, axis, bit):
    at = (lax.axis_index(axis) // bit) % 2
    sent = lax.dynamic_index_in_dim(parts, 1 - at, 0, False).astype(BF16)
    kept = lax.dynamic_index_in_dim(parts, at, 0, False)
    return kept + swap(sent, axis, bit).astype(F32)


def rejoin(half, axis, bit):
    first = (lax.axis_index(axis) // bit) % 2 == 0
    far = swap(half, axis, bit)
    return jnp.concatenate([jnp.where(first, half, far), jnp.where(first, far, half)], axis=0)


def bits(axis):
    count = lax.axis_size(axis)
    return [1 << k for k in range(count.bit_length() - 1)]


def gradient_sum(keep, send):
    width = keep.shape[2] // 2
    total = keep.astype(F32) + swap(send, "lev", 1).astype(F32)
    part_a = total[0, :, :width] + swap(total[1, :, :width].astype(BF16), "lev", 2).astype(F32)
    part_b = total[:, :, width:]
    for bit in bits("lon"):
        rows = part_a.shape[0] // 2
        part_a = halve(part_a.reshape(2, rows, width), "lon", bit)
        part_b = halve(jnp.swapaxes(part_b.reshape(2, 2, rows, width), 0, 1), "lon", bit)
    part_b = part_b[0] + swap(part_b[1].astype(BF16), "lev", 2).astype(F32)
    return jnp.concatenate([part_a, part_b], axis=1)


def plane_sum(part):
    for bit in bits("lat"):
        part = halve(part.reshape(2, part.shape[0] // 2, -1), "lat", bit)
    part = part.astype(BF16)
    for bit in reversed(bits("lat")):
        part = rejoin(part, "lat", bit)
    for bit in reversed(bits("lon")[1:]):
        part = rejoin(part, "lon", bit)
    return part, swap(part, "lon", 1)


def pair_sum(keep, send):
    count = lax.axis_size("lat")
    width = keep.shape[-1]
    come = swap(send, "lev", 1)
    piece = shape(keep.shape[2:])
    to_far, to_lat, to_lev, own = call(
        "split", split_kernel, [piece, piece, piece, shape(piece.shape, F32)], [], [keep, come], [], [], [], 8
    )
    from_far = lax.ppermute(to_far, ("lat", "lev"), [(i, i ^ 6) for i in range(4 * count)])
    from_lat = swap(to_lat, "lat", 1)
    from_lev = swap(to_lev, "lev", 2)
    own = own + from_lev.astype(F32) + from_lat.astype(F32) + from_far.astype(F32)
    return own.astype(BF16)


def lat_sum(own):
    for bit in bits("lat")[1:]:
        own = (own.astype(F32) + swap(own, "lat", bit).astype(F32)).astype(BF16)
    return own


def pair_spread(own):
    count = lax.axis_size("lat")
    by_far = lax.ppermute(own, ("lon", "lat"), [(i, i ^ (count + 1)) for i in range(2 * count)])
    return own, swap(own, "lat", 1), swap(own, "lon", 1), by_far


def on_device(tokens_in, cotangent, qkv_weight, out_weight, norm_gain, ocean_mask):
    pair = lax.axis_size("lon") == 2
    gain = norm_gain.reshape(1, D)
    half = shape((2, AREA, D))
    four = shape((4, AREA, D))
    wide = shape((4, AREA, 2 * D))
    info_shape = shape((8,), jnp.int32)
    vmem = lambda *dims: pltpu.VMEM(dims, BF16)
    grid = vmem(*tokens_in.shape)
    mask = pltpu.VMEM(ocean_mask.shape, jnp.int32)
    tok, tok_first, tok_second = call(
        "prep", prep_kernel, [four, half, half], [], [], [], [tokens_in, ocean_mask],
        [grid, mask, DMAS((2,))], 8, flops=10 ** 10,
    )
    tok_lon = lon_halo(tok)
    odd = lax.axis_index("lat") % 2
    sides = tok_first, tok_second
    tok_first, tok_second = lat_swaps(tok_first, tok_second)
    q, kv, hid, gb, bias, info = call(
        "own", own_kernel,
        [four, wide, shape((4 * AREA, D)), four, shape((4, 8, AREA), F32), info_shape],
        [], [tok, qkv_weight, gain], [], [cotangent, ocean_mask], [grid, mask, DMAS((2,))], 16,
        flops=2 * 256 * 512 * 1536, out_specs=[VMEM] * 5 + [SMEM],
    )
    wqkv, wout = qkv_weight, out_weight
    if pair:
        sides, gb = lax.optimization_barrier((sides, gb))
        corner_first, corner_second = corner_swap(sides[0], 0), corner_swap(sides[1], 1)
        gb_near = lon_halo(gb)
    else:
        rows = tok_lon.reshape(2, 2, AREA, D)
        corner_first, corner_second = lat_swaps(
            lax.dynamic_index_in_dim(rows, 1 - odd, 0, False),
            lax.dynamic_index_in_dim(rows, odd, 0, False),
        )
    q_near, kv_near, hid_near, bias_near, info_near = call(
        "near", near_kernel,
        [four, shape((8, AREA, 2 * D)), shape((8 * AREA, D)), shape((8, 8, AREA), F32), info_shape],
        [], [tok_lon, tok_first, tok_second, wqkv, gain], [], [], [], 20,
        flops=2 * 512 * 512 * 1280, out_specs=[VMEM] * 4 + [SMEM],
    )
    all_shape, all32 = shape((16, AREA, 2 * D)), shape((16, AREA, 2 * D), F32)
    back = shape((2 if pair else 4, AREA, D))
    ends = [all_shape, back, back] + ([] if pair else [four])
    weights = [wqkv, wout, gain]
    scratch = [vmem(4, AREA, D), vmem(KEYS, 2 * D)]
    flops = 3 * 12 * 2 * 512 * 256 * 256
    acc, mixed, gq, hid_all, kv_all, bias_all, *rest = call(
        "main", lambda *refs: main_kernel(0, not pair, *refs),
        [all32, four, four, shape((16 * AREA, D)), all_shape, shape((16, 8, AREA), F32)]
        + ([] if pair else ends),
        [info, info_near], weights + [q, gb, corner_first, corner_second],
        [kv, kv_near, hid, hid_near, bias, bias_near], [], scratch + [DMAS((6,))], 28, flops=flops,
    )
    parts = [gq, mixed, gb]
    if pair:
        _, mixed_near, gq_near, *rest = call(
            "other", lambda *refs: main_kernel(1, True, *refs), [all32, four, four] + ends,
            [info, info_near], weights + [q_near, gb_near, kv_all, bias_all, acc], [], [],
            scratch, 28, flops=flops, aliases={9: 0},
        )
        parts += [gq_near, mixed_near, gb_near]
    dkv, back_first, back_second, *side = rest
    share = shape((2, 2, 64, 2 * D) if pair else (2, 128, 4 * D))
    send, keep = [
        call(
            name, lambda *refs, other=other: sums_kernel(pair, other, *refs), [share], [],
            [hid_all, dkv] + parts, [], [], [], 24, flops=1024 * 512 * 1024,
        )[0]
        for name, other in (("sent", 1), ("kept", 0))
    ]
    if pair:
        total = pair_sum(keep, send)
        back_second = lat_swap(back_second, 1)
        total, back_first, back_second = lax.optimization_barrier((total, back_first, back_second))
        back_first = lat_swap(back_first, 0)
        total = lat_sum(total)
        total, back_first = lax.optimization_barrier((total, back_first))
        sums = pair_spread(total)
        lon_share = []
        finish = finish_pair_kernel
    else:
        part = gradient_sum(keep, send)
        back_first, back_second = lat_swaps(back_first, back_second)
        one, two = back_first[2:].astype(F32), back_second[2:].astype(F32)
        rows = jnp.stack([jnp.where(odd == 1, one, two), jnp.where(odd == 1, two, one)])
        side = (side[0].reshape(rows.shape).astype(F32) + rows).astype(BF16)
        lon_share = [lon_return(side.reshape(four.shape))]
        sums = plane_sum(part)
        finish = finish_rows_kernel
    layer_out, input_grad = call(
        "input", lambda *refs: input_kernel(pair, *refs),
        [shape(tokens_in.shape), shape(tokens_in.shape)], [],
        [dkv, back_first, back_second, gq, tok, mixed] + lon_share + weights, [],
        [cotangent, tokens_in, ocean_mask], [grid, grid, mask, DMAS((3,))], 24, flops=2 * 256 * 512 * 1536,
    )
    qkv_grad, out_grad, gain_grad = call(
        "finish", finish,
        [shape((128, 3 * D), F32), shape((128, D), F32), shape((1, 128), F32)], [],
        [*sums, wqkv, gain], [], [], [], 16,
    )
    return layer_out, input_grad, qkv_grad, out_grad, gain_grad.reshape(128)


def solution(mesh):
    placed = (
        P("lev", "lat", "lon", None),
        P("lev", "lat", "lon", None),
        P(),
        P(),
        P(),
        P("lev", "lat", "lon"),
    )
    return jax.shard_map(
        on_device,
        mesh=mesh,
        in_specs=placed,
        out_specs=(
            P("lev", "lat", "lon", None),
            P("lev", "lat", "lon", None),
            P("lev", None),
            P("lev", None),
            P("lev"),
        ),
        check_vma=False,
    )
```

```python
import jax
import jax.numpy as jnp
from jax import lax
from jax.experimental import pallas as pl
from jax.experimental.pallas import tpu as pltpu
from jax.sharding import PartitionSpec as P

HEADS = 8
WIN = 8
AREA = WIN * WIN
D = 512
HEAD_DIM = D // HEADS
GROUP = 256
GROUP_HEADS = GROUP // HEAD_DIM
GROUPS = D // GROUP
KEYS = 8 * AREA
LAND = 1000.0
NEVER = -1e9
FAR = 1e30
F32 = jnp.float32
BF16 = jnp.bfloat16
EXACT = lax.Precision.HIGHEST


def dot(a, b, ca, cb, precision=None):
    return lax.dot_general(
        a, b, (((ca,), (cb,)), ((), ())), preferred_element_type=F32, precision=precision
    )


def iota(shape, dim):
    return lax.broadcasted_iota(jnp.int32, shape, dim)


def window_of(grid, w):
    r, c = divmod(w, 2)
    part = grid[r * WIN : (r + 1) * WIN, c * WIN : (c + 1) * WIN, :]
    return part.reshape(AREA, grid.shape[-1])


def grid_of(windows):
    rows = []
    for r in range(2):
        parts = [windows[2 * r + c].reshape(WIN, WIN, -1) for c in range(2)]
        rows.append(jnp.concatenate(parts, axis=1))
    return jnp.concatenate(rows, axis=0)


def token_mask(mask):
    t = iota((4 * AREA, 2 * WIN), 0)
    lane = iota((4 * AREA, 2 * WIN), 1)
    w, i, j = t // AREA, (t % AREA) // WIN, t % WIN
    pick_row = (lane == WIN * (w // 2) + i).astype(F32)
    pick_col = (lane == WIN * (w % 2) + j).astype(F32)
    rows = dot(pick_row, mask, 1, 0)
    return jnp.sum(rows * pick_col, axis=1, keepdims=True)


def norm_rows(x):
    center = x - jnp.mean(x, axis=-1, keepdims=True)
    spread = jnp.mean(center * center, axis=-1, keepdims=True)
    scaling = lax.rsqrt(spread + 1e-05)
    return center * scaling, scaling


def head_blocks():
    row = iota((GROUP, GROUP), 0) // HEAD_DIM
    col = iota((GROUP, GROUP), 1) // HEAD_DIM
    return (row == col).astype(F32)


def stack_heads(part, blocks):
    return jnp.concatenate([part] * GROUP_HEADS, axis=0) * blocks.astype(part.dtype)


def unstack_heads(full, blocks):
    kept = full * blocks
    return sum(kept[h * AREA : (h + 1) * AREA] for h in range(GROUP_HEADS))


def lanes(g):
    return slice(g * GROUP, (g + 1) * GROUP)


def lat_side(row):
    return (row + lax.axis_index("lat") + 1) % 2


def load(pairs, sems):
    copies = [pltpu.make_async_copy(a, b, sems.at[k]) for k, (a, b) in enumerate(pairs)]
    for copy in copies:
        copy.start()
    return copies


def wait(copies):
    for copy in copies:
        copy.wait()


def prep_kernel(
    x_hbm, mask_hbm, all_ref, first_ref, second_ref, x_ref, mask_ref, sems
):
    copies = load(((mask_hbm, mask_ref), (x_hbm, x_ref)), sems)
    copies[0].wait()
    ocean = token_mask(mask_ref[0].astype(F32))
    copies[1].wait()
    x = x_ref[0].astype(F32)
    parts = []
    for w in range(4):
        part = jnp.where(ocean[w * AREA : (w + 1) * AREA] > 0.5, window_of(x, w), LAND)
        parts.append(part.astype(BF16))
        all_ref[w] = parts[w]
    odd = lax.axis_index("lat") % 2 == 1
    for c in range(2):
        first_ref[c] = jnp.where(odd, parts[c], parts[2 + c])
        second_ref[c] = jnp.where(odd, parts[2 + c], parts[c])


def land_bias(tokens):
    first = (iota((8, D), 1) == 0).astype(BF16)
    picked = dot(first, tokens, 1, 1)[:1]
    return jnp.where(picked > 0.5 * LAND, NEVER, 0.0)


def hidden_of(tokens, gain_ref):
    normed, _ = norm_rows(tokens.astype(F32))
    return (normed * gain_ref[...]).astype(BF16)


def write_block(tokens, wqkv_ref, gain_ref, q_ref, kv_ref, hid_ref, bias_ref, info_ref):
    hidden = hidden_of(tokens, gain_ref)
    hid_ref[: 4 * AREA] = hidden
    projected = dot(hidden, wqkv_ref[...], 1, 0).astype(BF16)
    q_ref[...] = (projected[:, :D] * BF16(HEAD_DIM ** -0.5)).reshape(4, AREA, D)
    kv_ref[:4] = projected[:, D:].reshape(4, AREA, 2 * D)
    row = land_bias(tokens)
    alive = []
    for w in range(4):
        part = row[:, w * AREA : (w + 1) * AREA]
        bias_ref[w] = jnp.broadcast_to(part, (8, AREA))
        alive.append((jnp.max(part) > 0.5 * NEVER).astype(jnp.int32))
        info_ref[1 + w] = alive[w]
    info_ref[0] = jnp.where(
        alive[3] == 0, 3, jnp.where(alive[2] == 0, 2, jnp.where(alive[1] == 0, 1, 0))
    )


def own_kernel(
    tok_ref, wqkv_ref, gain_ref, cot_hbm, mask_hbm,
    q_ref, kv_ref, hid_ref, gb_ref, bias_ref, info_ref, cot_ref, mask_ref, sems,
):
    copies = load(((mask_hbm, mask_ref), (cot_hbm, cot_ref)), sems)
    tokens = tok_ref[...].reshape(4 * AREA, D)
    write_block(tokens, wqkv_ref, gain_ref, q_ref, kv_ref, hid_ref, bias_ref, info_ref)
    wait(copies)
    ocean = token_mask(mask_ref[0].astype(F32))
    cot = cot_ref[0].astype(F32)
    for w in range(4):
        gb_ref[w] = (window_of(cot, w) * ocean[w * AREA : (w + 1) * AREA]).astype(BF16)


def lat_block(first_ref, second_ref, wkv_ref, gain_ref, kv_ref, hid_ref, bias_ref, at):
    lat, lat_count = lax.axis_index("lat"), lax.axis_size("lat")
    odd = lat % 2 == 1
    first_ok = jnp.logical_or(odd, lat < lat_count - 1)
    second_ok = jnp.where(odd, lat_count - 1 - lat, lat) > 0
    parts = [first_ref[0], first_ref[1], second_ref[0], second_ref[1]]
    tokens = jnp.concatenate(parts, axis=0)
    hidden = hidden_of(tokens, gain_ref)
    hid_ref[at * AREA : (at + 4) * AREA] = hidden
    kv_ref[at : at + 4] = dot(hidden, wkv_ref[...], 1, 0).astype(BF16).reshape(4, AREA, 2 * D)
    row = land_bias(tokens)
    for k in range(4):
        part = row[:, k * AREA : (k + 1) * AREA]
        part = jnp.where(first_ok if k < 2 else second_ok, part, NEVER)
        bias_ref[at + k] = jnp.broadcast_to(part, (8, AREA))


def near_kernel(
    lon_ref, first_ref, second_ref, wqkv_ref, gain_ref, q_ref, kv_ref, hid_ref, bias_ref, info_ref
):
    tokens = lon_ref[...].reshape(4 * AREA, D)
    write_block(tokens, wqkv_ref, gain_ref, q_ref, kv_ref, hid_ref, bias_ref, info_ref)
    lat_block(first_ref, second_ref, wqkv_ref.at[:, D:], gain_ref, kv_ref, hid_ref, bias_ref, 4)


def main_kernel(block, last, *refs):
    refs = list(refs)
    take = lambda n: [refs.pop(0) for _ in range(n)]
    info_ref, infon_ref = take(2)
    wqkv_ref, wout_ref, gain_ref, q, gb = take(5)
    if block == 0:
        first_ref, second_ref, kv_own, kv_near, hid_own, hid_near, bias_own, bias_near = take(8)
    else:
        kv, bias, _ = take(3)
    acc, mixed, gq = take(3)
    if block == 0:
        hid, kv, bias = take(3)
    if last:
        dkv, back1_ref, back2_ref = take(3)
        side_ref = None if block else take(1)[0]
    gm, kcat, *sems = refs
    wkv_ref = wqkv_ref.at[:, D:]
    if block == 0:
        pairs = (
            (kv_own, kv.at[:4]), (kv_near, kv.at[4:12]),
            (hid_own, hid.at[: 4 * AREA]), (hid_near, hid.at[4 * AREA : 12 * AREA]),
            (bias_own, bias.at[:4]), (bias_near, bias.at[4:12]),
        )
        copies = load(pairs, sems[0])
        acc[...] = jnp.zeros_like(acc)
        lat_block(first_ref, second_ref, wkv_ref, gain_ref, kv, hid, bias, 12)
        wait(copies)
    mixed[...] = jnp.zeros_like(mixed)
    gq[...] = jnp.zeros_like(gq)
    blocks = head_blocks()
    gm[...] = dot(gb[...].reshape(4 * AREA, D), wout_ref[...], 1, 1).astype(BF16).reshape(gm.shape)
    info = infon_ref if block else info_ref

    def window_at(slot):
        return slot + (slot >= info[0]).astype(jnp.int32)

    def attend(slot, all_keys, all_values, with_out, with_query):
        at = window_at(slot)

        @pl.when(info[1 + at] > 0)
        def _():
            r, c = at // 2, at % 2
            mine, other, side = 4 * block, 4 * (1 - block), 2 * lat_side(r)
            near = [mine + window_at(k) for k in range(3)] + [8 + mine + side, 9 + mine + side]
            away = [other + 1 - c, other + 3 - c, 8 + other + side + 1 - c]
            places = away + near if block else near + away
            few = 3 if block else 5
            key_count, value_count = 8 if all_keys else few, 8 if all_values else few
            for k in range(8):
                kcat[k * AREA : (k + 1) * AREA] = kv[places[k]]
            bias_row = jnp.concatenate([bias[place][:1] for place in places], axis=1)
            spans = [slice(D + g * GROUP, D + (g + 1) * GROUP) for g in range(GROUPS)]
            both = range(GROUPS)
            q_stack = [stack_heads(q[at, :, lanes(g)], blocks) for g in both]
            gm_stack = [stack_heads(gm[at, :, lanes(g)], blocks) for g in both]
            scores = [dot(q_stack[g], kcat[:, lanes(g)], 1, 1) + bias_row for g in both]
            grad_probs = [dot(gm_stack[g], kcat[:, spans[g]], 1, 1) for g in both]
            weights = [jnp.exp(x - jnp.max(x, axis=1, keepdims=True)) for x in scores]
            inverse = [1.0 / jnp.sum(x, axis=1, keepdims=True) for x in weights]
            low = [(x * y).astype(BF16) for x, y in zip(weights, inverse)]
            delta = [jnp.sum(weights[g] * grad_probs[g], axis=1, keepdims=True) * inverse[g] for g in both]
            grad_scores = [
                (weights[g] * ((grad_probs[g] - delta[g]) * inverse[g])).astype(BF16) for g in both
            ]
            if with_out:
                out = [unstack_heads(dot(low[g], kcat[:, spans[g]], 1, 0), blocks) for g in both]
            if with_query:
                grad = [unstack_heads(dot(grad_scores[g], kcat[:, lanes(g)], 1, 0), blocks) for g in both]
            grad_keys = [dot(grad_scores[g][:, : key_count * AREA], q_stack[g], 0, 0) for g in both]
            grad_values = [dot(low[g][:, : value_count * AREA], gm_stack[g], 0, 0) for g in both]
            for g in both:
                if with_out:
                    mixed[at, :, lanes(g)] = out[g].astype(BF16)
                if with_query:
                    gq[at, :, lanes(g)] = (grad[g] * HEAD_DIM ** -0.5).astype(BF16)
                for k in range(8):
                    rows = slice(k * AREA, (k + 1) * AREA)
                    if k < key_count:
                        acc[places[k], :, lanes(g)] += grad_keys[g][rows]
                    if k < value_count:
                        acc[places[k], :, spans[g]] += grad_values[g][rows]

    def sweep(*wanted):
        def step(slot, carry):
            attend(slot, *wanted)
            return carry

        lax.fori_loop(0, 3, step, 0)

    if block == 0 and last:
        sweep(True, True, True, True)
    else:
        lon = lax.axis_index("lon")
        pl.when(lon == 0)(lambda: sweep(True, False, block == 0, True))
        pl.when(lon == 1)(lambda: sweep(False, True, True, block == 0))
    if not last:
        return
    dkv[...] = acc[...].astype(BF16)
    near = dkv[8:12] if block else dkv[4:]
    shares = dot(near.reshape(-1, 2 * D), wkv_ref[...], 1, 1).astype(BF16).reshape(-1, AREA, D)
    if block:
        back1_ref[...] = shares[:2]
        back2_ref[...] = shares[2:4]
    else:
        side_ref[...] = shares[:4]
        for ref, at in ((back1_ref, 4), (back2_ref, 6)):
            ref[:2] = shares[at : at + 2]
            ref[2:] = shares[at + 4 : at + 6]


def sums_kernel(pair, other, hid, dkv, *refs):
    held = [refs[k : k + 3] for k in range(0, len(refs) - 1, 3)]
    to = refs[-1]
    flat = lambda ref: ref[...].reshape(4 * AREA, D)
    lev = lax.axis_index("lev")

    def columns(rel):
        return pl.ds(pl.multiple_of((lev ^ rel) * 128, 128), 128)

    def grad_part(at, width):
        return dkv[:, :, at : at + width].reshape(16 * AREA, width)

    def query_sum(rel):
        parts = [
            dot(hid[4 * b * AREA : 4 * (b + 1) * AREA, columns(rel)], flat(gq), 0, 0)
            for b, (gq, _, _) in enumerate(held)
        ]
        return sum(parts[1:], parts[0])

    def out_sum(rel):
        parts = [
            dot(mixed[:, :, columns(rel)].reshape(4 * AREA, 128), flat(gb), 0, 0) for _, mixed, gb in held
        ]
        return sum(parts[1:], parts[0])

    if pair:
        odd, lon = lax.axis_index("lat") % 2, lax.axis_index("lon")

        def put(rel, at, value):
            value = value.astype(BF16)
            for k in range(2):
                to[rel // 2, k ^ odd, :, at : at + D] = value[k * 64 : (k + 1) * 64]

        @pl.when(lon == 0)
        def _():
            for rel in (other, 2 + other):
                put(rel, 0, query_sum(rel))
                put(rel, D, dot(hid[:, columns(rel)], grad_part(0, D), 0, 0))

        @pl.when(lon == 1)
        def _():
            for rel in (other, 2 + other):
                put(rel, 0, out_sum(rel))
                put(rel, D, dot(hid[:, columns(rel)], grad_part(D, D), 0, 0))

    else:
        for rel in (other, 2 + other):
            to[rel // 2, :, :D] = query_sum(rel).astype(BF16)
            to[rel // 2, :, D : 2 * D] = out_sum(rel).astype(BF16)
            to[rel // 2, :, 2 * D :] = dot(hid[:, columns(rel)], grad_part(0, 2 * D), 0, 0).astype(BF16)


def split_kernel(keep_ref, come_ref, far_ref, lat_ref, lev_ref, own_ref):
    for k, ref in enumerate((own_ref, lat_ref, lev_ref, far_ref)):
        total = keep_ref[k // 2, k % 2].astype(F32) + come_ref[k // 2, k % 2].astype(F32)
        ref[...] = total.astype(ref.dtype)


def input_kernel(pair, dkv, back1_ref, back2_ref, gq, tok_ref, mixed, *rest):
    refs = rest if pair else rest[1:]
    wqkv_ref, wout_ref, gain_ref, cot_hbm, x_hbm, mask_hbm, out_ref, ing_ref = refs[:8]
    cot_ref, x_ref, mask_ref, sems = refs[8:]
    copies = load(((x_hbm, x_ref), (mask_hbm, mask_ref), (cot_hbm, cot_ref)), sems)
    odd = lax.axis_index("lat") % 2 == 1
    shares = []
    for w in range(4):
        one, two = back1_ref[w % 2].astype(F32), back2_ref[w % 2].astype(F32)
        share = jnp.where(odd, one, two) if w < 2 else jnp.where(odd, two, one)
        shares.append(share if pair else share + rest[0][w].astype(F32))
    normed, scaling = norm_rows(tok_ref[...].reshape(4 * AREA, D).astype(F32))
    wait(copies)
    ocean = token_mask(mask_ref[0].astype(F32))
    added = (dot(mixed[:4].reshape(4 * AREA, D), wout_ref[...], 1, 0) * ocean).reshape(4, AREA, D)
    out_ref[0] = (x_ref[0].astype(F32) + grid_of([added[w] for w in range(4)])).astype(BF16)
    grad_hidden = jnp.concatenate(shares, axis=0)
    grad_hidden = grad_hidden + dot(gq[:4].reshape(4 * AREA, D), wqkv_ref[:, :D], 1, 1)
    grad_hidden = grad_hidden + dot(dkv[:4].reshape(4 * AREA, 2 * D), wqkv_ref[:, D:], 1, 1)
    scaled = grad_hidden * gain_ref[...]
    correction = (
        scaled
        - jnp.mean(scaled, axis=-1, keepdims=True)
        - normed * jnp.mean(scaled * normed, axis=-1, keepdims=True)
    )
    added = (scaling * correction).reshape(4, AREA, D)
    ing_ref[0] = (cot_ref[0].astype(F32) + grid_of([added[w] for w in range(4)])).astype(BF16)


def gain_row(wqkv_ref, gain_ref, qkv_ref):
    at = pl.ds(pl.multiple_of(lax.axis_index("lev") * 128, 128), 128)
    product = wqkv_ref[at, :].astype(F32) * qkv_ref[...]
    return dot(jnp.ones((8, 3 * D), F32), product, 1, 1, EXACT)[:1] / gain_ref[:, at]


def finish_rows_kernel(
    own_ref, far_ref, wqkv_ref, gain_ref, qkv_ref, out_ref, gg_ref
):
    half = own_ref.shape[0]
    first = lax.axis_index("lon") % 2 == 0
    own, far = own_ref[...], far_ref[...]
    for k in range(2):
        value = (jnp.where(first, own, far) if k == 0 else jnp.where(first, far, own)).astype(F32)
        rows = slice(k * half, (k + 1) * half)
        qkv_ref[rows, :D] = value[:, :D]
        qkv_ref[rows, D:] = value[:, 2 * D :]
        out_ref[rows] = value[:, D : 2 * D]
    gg_ref[...] = gain_row(wqkv_ref, gain_ref, qkv_ref)


def finish_pair_kernel(
    own_ref, lat_ref, lon_ref, far_ref, wqkv_ref, gain_ref, qkv_ref, out_ref, gg_ref
):
    odd = lax.axis_index("lat") % 2 == 1
    first = lax.axis_index("lon") == 0
    for k in range(2):
        rows = slice(64 * k, 64 * k + 64)
        mine = odd if k == 1 else jnp.logical_not(odd)
        near = jnp.where(mine, own_ref[...], lat_ref[...]).astype(F32)
        away = jnp.where(mine, lon_ref[...], far_ref[...]).astype(F32)
        low, high = jnp.where(first, near, away), jnp.where(first, away, near)
        qkv_ref[rows, : 2 * D] = low
        out_ref[rows] = high[:, :D]
        qkv_ref[rows, 2 * D :] = high[:, D:]
    gg_ref[...] = gain_row(wqkv_ref, gain_ref, qkv_ref)


SMEM = pl.BlockSpec(memory_space=pltpu.SMEM)
VMEM = pl.BlockSpec(memory_space=pltpu.VMEM)
ANY = pl.BlockSpec(memory_space=pl.ANY)
HBM = pl.BlockSpec(memory_space=pltpu.HBM)
DMAS = pltpu.SemaphoreType.DMA


def call(
    name, kernel, outs, scalars, arrays, loose, far, scratch, mebibytes, flops=0, out_specs=None, aliases=None
):
    moved = sum(a.size * a.dtype.itemsize for a in (*arrays, *loose, *far, *outs))
    specs = [SMEM] * len(scalars) + [VMEM] * len(arrays) + [ANY] * len(loose) + [HBM] * len(far)
    return pl.pallas_call(
        kernel,
        out_shape=outs,
        in_specs=specs,
        out_specs=out_specs or [VMEM] * len(outs),
        scratch_shapes=list(scratch),
        input_output_aliases=aliases or {},
        compiler_params=pltpu.CompilerParams(vmem_limit_bytes=mebibytes * 1024 * 1024),
        cost_estimate=pl.CostEstimate(flops=flops, bytes_accessed=moved, transcendentals=0),
        name=name,
    )(*scalars, *arrays, *loose, *far)


def shape(dims, dtype=BF16):
    return jax.ShapeDtypeStruct(dims, dtype)


def ring(count, step, periodic):
    return [
        (i, (i + step) % count) for i in range(count) if periodic or 0 <= i + step < count
    ]


def lon_halo(own):
    count = lax.axis_size("lon")
    if count == 2:
        return lax.ppermute(own, "lon", [(0, 1), (1, 0)])
    left = lax.ppermute(own[1::2], "lon", ring(count, 1, True))
    right = lax.ppermute(own[0::2], "lon", ring(count, -1, True))
    return jnp.stack([right, left], axis=1).reshape(own.shape)


def lon_return(side):
    count = lax.axis_size("lon")
    if count == 2:
        return lax.ppermute(side, "lon", [(0, 1), (1, 0)])
    from_left = lax.ppermute(side[0::2], "lon", ring(count, 1, True))
    from_right = lax.ppermute(side[1::2], "lon", ring(count, -1, True))
    return jnp.stack([from_left, from_right], axis=1).reshape(side.shape)


def lat_swap(value, start):
    pairs = [(i, i + 1) for i in range(start, lax.axis_size("lat") - 1, 2)]
    return lax.ppermute(value, "lat", pairs + [(b, a) for a, b in pairs])


def lat_swaps(first, second):
    return lat_swap(first, 0), lat_swap(second, 1)


def corner_swap(value, start):
    count = lax.axis_size("lat")
    pairs = [(i, i + 1) for i in range(start, count - 1, 2)]
    pairs = [(a + k * count, b + (1 - k) * count) for a, b in pairs for k in range(2)]
    return lax.ppermute(value, ("lon", "lat"), pairs + [(b, a) for a, b in pairs])


def swap(value, axis, bit):
    return lax.ppermute(value, axis, [(i, i ^ bit) for i in range(lax.axis_size(axis))])


def halve(parts, axis, bit):
    at = (lax.axis_index(axis) // bit) % 2
    sent = lax.dynamic_index_in_dim(parts, 1 - at, 0, False).astype(BF16)
    kept = lax.dynamic_index_in_dim(parts, at, 0, False)
    return kept + swap(sent, axis, bit).astype(F32)


def rejoin(half, axis, bit):
    first = (lax.axis_index(axis) // bit) % 2 == 0
    far = swap(half, axis, bit)
    return jnp.concatenate([jnp.where(first, half, far), jnp.where(first, far, half)], axis=0)


def bits(axis):
    count = lax.axis_size(axis)
    return [1 << k for k in range(count.bit_length() - 1)]


def gradient_sum(keep, send):
    width = keep.shape[2] // 2
    total = keep.astype(F32) + swap(send, "lev", 1).astype(F32)
    part_a = total[0, :, :width] + swap(total[1, :, :width].astype(BF16), "lev", 2).astype(F32)
    part_b = total[:, :, width:]
    for bit in bits("lon"):
        rows = part_a.shape[0] // 2
        part_a = halve(part_a.reshape(2, rows, width), "lon", bit)
        part_b = halve(jnp.swapaxes(part_b.reshape(2, 2, rows, width), 0, 1), "lon", bit)
    part_b = part_b[0] + swap(part_b[1].astype(BF16), "lev", 2).astype(F32)
    return jnp.concatenate([part_a, part_b], axis=1)


def plane_sum(part):
    for bit in bits("lat"):
        part = halve(part.reshape(2, part.shape[0] // 2, -1), "lat", bit)
    part = part.astype(BF16)
    for bit in reversed(bits("lat")):
        part = rejoin(part, "lat", bit)
    for bit in reversed(bits("lon")[1:]):
        part = rejoin(part, "lon", bit)
    return part, swap(part, "lon", 1)


def pair_sum(keep, send):
    count = lax.axis_size("lat")
    width = keep.shape[-1]
    come = swap(send, "lev", 1)
    piece = shape(keep.shape[2:])
    to_far, to_lat, to_lev, own = call(
        "split", split_kernel, [piece, piece, piece, shape(piece.shape, F32)], [], [keep, come], [], [], [], 8
    )
    from_far = lax.ppermute(to_far, ("lat", "lev"), [(i, i ^ 6) for i in range(4 * count)])
    from_lat = swap(to_lat, "lat", 1)
    from_lev = swap(to_lev, "lev", 2)
    own = own + from_lev.astype(F32) + from_lat.astype(F32) + from_far.astype(F32)
    return own.astype(BF16)


def lat_sum(own):
    for bit in bits("lat")[1:]:
        own = (own.astype(F32) + swap(own, "lat", bit).astype(F32)).astype(BF16)
    return own


def pair_spread(own):
    count = lax.axis_size("lat")
    by_far = lax.ppermute(own, ("lon", "lat"), [(i, i ^ (count + 1)) for i in range(2 * count)])
    return own, swap(own, "lat", 1), swap(own, "lon", 1), by_far


def on_device(tokens_in, cotangent, qkv_weight, out_weight, norm_gain, ocean_mask):
    pair = lax.axis_size("lon") == 2
    gain = norm_gain.reshape(1, D)
    half = shape((2, AREA, D))
    four = shape((4, AREA, D))
    wide = shape((4, AREA, 2 * D))
    info_shape = shape((8,), jnp.int32)
    vmem = lambda *dims: pltpu.VMEM(dims, BF16)
    grid = vmem(*tokens_in.shape)
    mask = pltpu.VMEM(ocean_mask.shape, jnp.int32)
    tok, tok_first, tok_second = call(
        "prep", prep_kernel, [four, half, half], [], [], [], [tokens_in, ocean_mask],
        [grid, mask, DMAS((2,))], 8, flops=10 ** 10,
    )
    tok_lon = lon_halo(tok)
    odd = lax.axis_index("lat") % 2
    sides = tok_first, tok_second
    tok_first, tok_second = lat_swaps(tok_first, tok_second)
    q, kv, hid, gb, bias, info = call(
        "own", own_kernel,
        [four, wide, shape((4 * AREA, D)), four, shape((4, 8, AREA), F32), info_shape],
        [], [tok, qkv_weight, gain], [], [cotangent, ocean_mask], [grid, mask, DMAS((2,))], 16,
        flops=2 * 256 * 512 * 1536, out_specs=[VMEM] * 5 + [SMEM],
    )
    wqkv, wout = qkv_weight, out_weight
    if pair:
        sides, gb = lax.optimization_barrier((sides, gb))
        corner_first, corner_second = corner_swap(sides[0], 0), corner_swap(sides[1], 1)
    else:
        rows = tok_lon.reshape(2, 2, AREA, D)
        corner_first, corner_second = lat_swaps(
            lax.dynamic_index_in_dim(rows, 1 - odd, 0, False),
            lax.dynamic_index_in_dim(rows, odd, 0, False),
        )
    q_near, kv_near, hid_near, bias_near, info_near = call(
        "near", near_kernel,
        [four, shape((8, AREA, 2 * D)), shape((8 * AREA, D)), shape((8, 8, AREA), F32), info_shape],
        [], [tok_lon, tok_first, tok_second, wqkv, gain], [], [], [], 20,
        flops=2 * 512 * 512 * 1280, out_specs=[VMEM] * 4 + [SMEM],
    )
    if pair:
        kv_near, gb = lax.optimization_barrier((kv_near, gb))
        gb_near = lon_halo(gb)
    all_shape, all32 = shape((16, AREA, 2 * D)), shape((16, AREA, 2 * D), F32)
    back = shape((2 if pair else 4, AREA, D))
    ends = [all_shape, back, back] + ([] if pair else [four])
    weights = [wqkv, wout, gain]
    scratch = [vmem(4, AREA, D), vmem(KEYS, 2 * D)]
    flops = 3 * 12 * 2 * 512 * 256 * 256
    acc, mixed, gq, hid_all, kv_all, bias_all, *rest = call(
        "main", lambda *refs: main_kernel(0, not pair, *refs),
        [all32, four, four, shape((16 * AREA, D)), all_shape, shape((16, 8, AREA), F32)]
        + ([] if pair else ends),
        [info, info_near], weights + [q, gb, corner_first, corner_second],
        [kv, kv_near, hid, hid_near, bias, bias_near], [], scratch + [DMAS((6,))], 28, flops=flops,
    )
    parts = [gq, mixed, gb]
    if pair:
        _, mixed_near, gq_near, *rest = call(
            "other", lambda *refs: main_kernel(1, True, *refs), [all32, four, four] + ends,
            [info, info_near], weights + [q_near, gb_near, kv_all, bias_all, acc], [], [],
            scratch, 28, flops=flops, aliases={9: 0},
        )
        parts += [gq_near, mixed_near, gb_near]
    dkv, back_first, back_second, *side = rest
    share = shape((2, 2, 64, 2 * D) if pair else (2, 128, 4 * D))
    send, keep = [
        call(
            name, lambda *refs, other=other: sums_kernel(pair, other, *refs), [share], [],
            [hid_all, dkv] + parts, [], [], [], 24, flops=1024 * 512 * 1024,
        )[0]
        for name, other in (("sent", 1), ("kept", 0))
    ]
    if pair:
        total = pair_sum(keep, send)
        back_second = lat_swap(back_second, 1)
        total, back_first, back_second = lax.optimization_barrier((total, back_first, back_second))
        back_first = lat_swap(back_first, 0)
        total = lat_sum(total)
        total, back_first = lax.optimization_barrier((total, back_first))
        sums = pair_spread(total)
        lon_share = []
        finish = finish_pair_kernel
    else:
        part = gradient_sum(keep, send)
        back_first, back_second = lat_swaps(back_first, back_second)
        one, two = back_first[2:].astype(F32), back_second[2:].astype(F32)
        rows = jnp.stack([jnp.where(odd == 1, one, two), jnp.where(odd == 1, two, one)])
        side = (side[0].reshape(rows.shape).astype(F32) + rows).astype(BF16)
        lon_share = [lon_return(side.reshape(four.shape))]
        sums = plane_sum(part)
        finish = finish_rows_kernel
    layer_out, input_grad = call(
        "input", lambda *refs: input_kernel(pair, *refs),
        [shape(tokens_in.shape), shape(tokens_in.shape)], [],
        [dkv, back_first, back_second, gq, tok, mixed] + lon_share + weights, [],
        [cotangent, tokens_in, ocean_mask], [grid, grid, mask, DMAS((3,))], 24, flops=2 * 256 * 512 * 1536,
    )
    qkv_grad, out_grad, gain_grad = call(
        "finish", finish,
        [shape((128, 3 * D), F32), shape((128, D), F32), shape((1, 128), F32)], [],
        [*sums, wqkv, gain], [], [], [], 16,
    )
    return layer_out, input_grad, qkv_grad, out_grad, gain_grad.reshape(128)


def solution(mesh):
    placed = (
        P("lev", "lat", "lon", None),
        P("lev", "lat", "lon", None),
        P(),
        P(),
        P(),
        P("lev", "lat", "lon"),
    )
    return jax.shard_map(
        on_device,
        mesh=mesh,
        in_specs=placed,
        out_specs=(
            P("lev", "lat", "lon", None),
            P("lev", "lat", "lon", None),
            P("lev", None),
            P("lev", None),
            P("lev"),
        ),
        check_vma=False,
    )
```
